32 devices in a mesh: groups: 2 (over y), points: 4 (over z), mp: 2 (over x), sub: 2 (over core).
Axes of the slice: x: 2, y: 2, z: 4, core: 2. Of those that a mesh axis runs over, the one named last changes fastest.
Arguments:
- points_in: bfloat16 [32768, 512], P(('groups', 'points', 'mp', 'sub')), parts along dimension 0, may hold values from -80 to 80
- cotangent: bfloat16 [32768, 512], P(('groups', 'points', 'mp', 'sub')), parts along dimension 0, may hold values from -9 to 9
- w_query: bfloat16 [512, 512], replicated, may hold values from -0.25 to 0.25
- w_key: bfloat16 [512, 512], replicated, may hold values from -1 to 1
- w_value: bfloat16 [512, 512], replicated, may hold values from -1 to 1
Outputs:
- grad_points: bfloat16 [32768, 512], P(('groups', 'points', 'mp', 'sub')), parts along dimension 0
- grad_query: float32 [1024, 512], P(('groups', 'points', 'sub'), 'mp'), parts along dimension 0
- grad_key: float32 [1024, 512], P(('groups', 'points', 'sub'), 'mp'), parts along dimension 0
- grad_value: float32 [1024, 512], P(('groups', 'points', 'sub'), 'mp'), parts along dimension 0
The draws below stay inside these ranges and needn't reach their ends.
There are 2 independent parts, one for each index of `groups`. The reference program is written for one: setup_inputs(seed, part) draws one part's arguments, and reference() takes and returns one part's arrays. A program takes and returns all parts, laid end to end along the dimension named above; an argument that names none is the same for every part. Nothing has to cross between parts.
All inputs are finite; a program needn't handle non-finite values.
Results may differ from the reference program's by a relative error of at most 0.006.
Values sent between devices are 32-bit elements; how exact they have to be, the bound alone decides.
No kernel may reach another device: no remote copies, remote signals or barrier semaphores. Data moves between devices by JAX's collectives and lax.ppermute only.
A program may use at most 64 MiB of HBM per device.

```python
import jax
import jax.numpy as jnp
from jax import lax

D = 512
HEADS = 16
HS = 32
TOK_DEV = 1024
NPTS = 16384


def point_base(key):
    inner = jax.random.fold_in(key, 501)
    return jnp.clip(jax.random.normal(inner, (NPTS, D), jnp.float32), -6.0, 6.0)


def weight_base(key):
    inner = jax.random.fold_in(key, 601)
    return jnp.clip(jax.random.normal(inner, (D, D), jnp.float32), -6.0, 6.0) / jnp.sqrt(jnp.float32(D))


def draw_points_in(key, part):
    shared = point_base(key)
    blocks = NPTS // TOK_DEV
    period = min(D, blocks)
    row_block = jnp.arange(NPTS, dtype=jnp.int32)[:, None] // TOK_DEV
    column = jnp.arange(D, dtype=jnp.int32)[None, :]
    boost = jnp.where(column % period == row_block % period, 6.0, 1.0).astype(jnp.float32)
    values = shared
    return (values * boost).astype(jnp.bfloat16)


def draw_cotangent(key, part):
    shared = point_base(key)
    key = jax.random.fold_in(key, 13)
    noise = jnp.clip(jax.random.normal(key, (NPTS, D), jnp.float32), -6.0, 6.0)
    return (0.6 * shared + 0.8 * noise).astype(jnp.bfloat16)


def draw_w_key(key, part):
    shared = weight_base(key)
    return shared.astype(jnp.bfloat16)


def draw_w_value(key, part):
    shared = weight_base(key)
    key = jax.random.fold_in(key, 19)
    noise = jnp.clip(jax.random.normal(key, (D, D), jnp.float32), -6.0, 6.0) / jnp.sqrt(jnp.float32(D))
    return (0.6 * shared + 0.8 * noise).astype(jnp.bfloat16)


def bell_draw(own_key, extent, deviation, reach, kind=jnp.bfloat16):
    return jnp.clip(deviation * jax.random.normal(own_key, extent, jnp.float32), -reach, reach).astype(kind)


def setup_inputs(seed: int = 0, part: int = 0) -> dict:
    key_of = jax.random.split(jax.random.key(seed), 6)
    part_splits = jax.random.split(jax.random.fold_in(key_of[5], part), 6)
    points_in = draw_points_in(jax.random.fold_in(jax.random.fold_in(key_of[5], part), 71), part)
    cotangent = draw_cotangent(jax.random.fold_in(jax.random.fold_in(key_of[5], part), 71), part)
    w_query = bell_draw(key_of[2], (D, D), D ** -0.5, 0.25)
    w_key = draw_w_key(jax.random.fold_in(key_of[5], 71), part)
    w_value = draw_w_value(jax.random.fold_in(key_of[5], 71), part)
    return {"points_in": points_in, "cotangent": cotangent, "w_query": w_query, "w_key": w_key, "w_value": w_value}


def layer_norm(raw):
    mean_val = lax.optimization_barrier(jnp.mean(raw, axis=-1, keepdims=True))
    centred = raw - mean_val
    spread = lax.optimization_barrier(jnp.mean(centred * centred, axis=-1, keepdims=True))
    inverse = lax.rsqrt(spread + 1e-05)
    return (centred * inverse, inverse)

def norm_back(grad_norm, normed, inverse):
    first = lax.optimization_barrier(jnp.mean(grad_norm, axis=-1, keepdims=True))
    second = lax.optimization_barrier(jnp.mean(grad_norm * normed, axis=-1, keepdims=True))
    return (grad_norm - first - normed * second) * inverse

def project(rows_in, w_query, w_key, w_value):
    count = rows_in.shape[0]
    f32 = jnp.float32
    query = jnp.dot(rows_in, w_query, preferred_element_type=f32).astype(jnp.bfloat16).reshape(count, HEADS, HS)
    key_norm, key_inv = layer_norm(jnp.dot(rows_in, w_key, preferred_element_type=f32).reshape(count, HEADS, HS))
    value_norm, value_inv = layer_norm(jnp.dot(rows_in, w_value, preferred_element_type=f32).reshape(count, HEADS, HS))
    return (query, key_norm, key_inv, value_norm, value_inv)

def reference(points_in, cotangent, w_query, w_key, w_value):
    total = points_in.shape[0]
    f32 = jnp.float32
    block = min(total, 8192)
    nblocks = total // block
    point_blocks = points_in.reshape(nblocks, block, D)
    cot_blocks = cotangent.reshape(nblocks, block, D)

    def first_pass(carry, pair):
        rows_in, cot_rows = pair
        query, key_norm, key_inv, value_norm, value_inv = project(rows_in, w_query, w_key, w_value)
        key_low = key_norm.astype(jnp.bfloat16).astype(f32)
        value_low = value_norm.astype(jnp.bfloat16).astype(f32)
        grad_out = cot_rows.reshape(block, HEADS, HS).astype(f32)
        state_acc = carry[0] + jnp.einsum('nhi,nhj->hij', key_low, value_low)
        grad_acc = carry[1] + jnp.einsum('nhi,nhj->hij', query.astype(f32), grad_out)
        return ((state_acc, grad_acc), None)
    zeros_state = jnp.zeros((HEADS, HS, HS), f32)
    (state_sum, grad_sum), _ = lax.scan(first_pass, (zeros_state, zeros_state), (point_blocks, cot_blocks))
    state_low = (state_sum / total).astype(jnp.bfloat16).astype(f32)
    grad_low = (grad_sum / total).astype(jnp.bfloat16).astype(f32)
    w_all = jnp.concatenate([w_query, w_key, w_value], axis=1)

    def second_pass(carry, pair):
        rows_in, cot_rows = pair
        query, key_norm, key_inv, value_norm, value_inv = project(rows_in, w_query, w_key, w_value)
        key_low = key_norm.astype(jnp.bfloat16).astype(f32)
        value_low = value_norm.astype(jnp.bfloat16).astype(f32)
        grad_out = cot_rows.reshape(block, HEADS, HS).astype(f32)
        grad_q = jnp.einsum('nhj,hij->nhi', grad_out, state_low)
        grad_kn = jnp.einsum('nhj,hij->nhi', value_low, grad_low)
        grad_vn = jnp.einsum('nhi,hij->nhj', key_low, grad_low)
        grad_k = norm_back(grad_kn, key_norm, key_inv)
        grad_v = norm_back(grad_vn, value_norm, value_inv)
        grad_cat = jnp.concatenate([grad_q.reshape(block, D), grad_k.reshape(block, D), grad_v.reshape(block, D)], axis=1).astype(jnp.bfloat16)
        grad_rows = lax.dot_general(grad_cat, w_all, (((1,), (1,)), ((), ())), preferred_element_type=f32).astype(jnp.bfloat16)
        weight_acc = carry + lax.dot_general(rows_in, grad_cat, (((0,), (0,)), ((), ())), preferred_element_type=f32)
        return (weight_acc, grad_rows)
    weight_sum, grad_blocks = lax.scan(second_pass, jnp.zeros((D, 3 * D), f32), (point_blocks, cot_blocks))
    grad_points = grad_blocks.reshape(total, D)
    weight_mean = weight_sum / total
    grad_query = weight_mean[:, :D]
    grad_key = weight_mean[:, D:2 * D]
    grad_value = weight_mean[:, 2 * D:]
    return (grad_points, grad_query, grad_key, grad_value)
```

```python
import functools

import jax
import jax.numpy as jnp
from jax import lax
from jax.experimental import pallas as pl
from jax.experimental.pallas import tpu as pltpu
from jax.sharding import PartitionSpec as P

HS = 32
F32 = jnp.float32
BF16 = jnp.bfloat16
NT = (((1,), (1,)), ((), ()))
TN = (((0,), (0,)), ((), ()))
NN = (((1,), (0,)), ((), ()))
VMEM = pl.BlockSpec(memory_space=pltpu.VMEM)
PARAMS = pltpu.CompilerParams(vmem_limit_bytes=32 * 1024 * 1024)


def dot(a, b, dims):
    return lax.dot_general(a, b, dims, preferred_element_type=F32)


def split(x):
    high = x.astype(BF16)
    return high, (x - high.astype(F32)).astype(BF16)


def head_mask(size):
    rows = lax.broadcasted_iota(jnp.int32, (size, size), 0) // HS
    cols = lax.broadcasted_iota(jnp.int32, (size, size), 1) // HS
    return rows == cols


def averager(size):
    return jnp.where(head_mask(size), F32(1.0 / HS), F32(0.0)).astype(BF16)


def pack(full):
    size = full.shape[0]
    kept = jnp.where(head_mask(size), full, F32(0.0))
    total = kept[:HS]
    for i in range(1, size // HS):
        total = total + kept[i * HS : (i + 1) * HS]
    return total


def unpack(packed):
    size = packed.shape[1]
    tiled = jnp.concatenate([packed] * (size // HS), axis=0)
    return jnp.where(head_mask(size), tiled, F32(0.0))


def place(refs, value, x_first):
    z, x, s = lax.axis_index("points"), lax.axis_index("mp"), lax.axis_index("sub")
    nz, nx, ns = lax.axis_size("points"), lax.axis_size("mp"), lax.axis_size("sub")
    rb, cb = value.shape[0] // (nz * ns), value.shape[1] // nx
    for zb in range(nz):
        for sb in range(ns):
            row = (zb * ns + sb) * rb
            for xb in range(nx):
                block = value[row : row + rb, xb * cb : (xb + 1) * cb]
                first, second = (x ^ xb, z ^ zb) if x_first else (z ^ zb, x ^ xb)
                refs[s ^ sb, first, second] = block


def cross_kernel(p_ref, c_ref, wq_ref, m_ref, g_ref):
    width = p_ref.shape[1]
    ns = lax.axis_size("sub")
    s = lax.axis_index("sub")
    half = width // ns
    parts = []
    for g in range(ns):
        cols = slice(g * half, (g + 1) * half)
        cross = dot(p_ref[...], c_ref[:, cols], TN)
        high, low = split(cross)
        wq = wq_ref[:, cols]
        g_ref[s ^ g] = pack(dot(wq, high, TN) + dot(wq, low, TN))
        parts.append(cross)
    place(m_ref, jnp.concatenate(parts, axis=1), True)


def norm_kernel(p_ref, wk_ref, wv_ref, kn_ref, kr_ref, vn_ref, vr_ref, s_ref, wc_ref):
    rows, width = p_ref.shape
    ns = lax.axis_size("sub")
    s = lax.axis_index("sub")
    half = width // ns
    mean = averager(half)
    for w, w_ref in enumerate((wk_ref, wv_ref)):
        for g in range(ns):
            cols = slice(g * half, (g + 1) * half)
            raw = w_ref[:, cols]
            high, low = split(raw.astype(F32) - dot(raw, mean, NN))
            wc_ref[w, 0, :, cols] = high
            wc_ref[w, 1, :, cols] = low
    for g in range(ns):
        cols = slice(g * half, (g + 1) * half)
        for w, (n_ref, r_ref) in enumerate(((kn_ref, kr_ref), (vn_ref, vr_ref))):
            chunk = 256
            for r in range(rows // chunk):
                span = slice(r * chunk, (r + 1) * chunk)
                p = p_ref[span, :]
                centred = dot(p, wc_ref[w, 0, :, cols], NN) + dot(p, wc_ref[w, 1, :, cols], NN)
                high, low = split(centred * centred)
                inverse = lax.rsqrt(dot(high, mean, NN) + dot(low, mean, NN) + 1e-05)
                n_ref[span, cols] = centred * inverse
                r_ref[span, cols] = inverse
        s_ref[s ^ g] = pack(dot(kn_ref[:, cols].astype(BF16), vn_ref[:, cols].astype(BF16), TN))


def back_kernel(total, key, p_ref, n_ref, r_ref, o_ref, own_ref, got_ref, w_ref, gl_ref):
    rows, width = p_ref.shape
    ns = lax.axis_size("sub")
    s = lax.axis_index("sub")
    half = width // ns
    mean = averager(half)
    parts = []
    for g in range(ns):
        cols = slice(g * half, (g + 1) * half)
        packed = jnp.where(s == g, own_ref[...], got_ref[...])
        low = (packed / total).astype(BF16).astype(F32)
        full = unpack(low)
        if key:
            grouped = dot(mean, full.astype(BF16), NN)
            dims = NT
        else:
            grouped = dot(full.astype(BF16), mean, NN)
            dims = NN
        high, small = split(full - grouped)
        chunk = 256
        for r in range(rows // chunk):
            span = slice(r * chunk, (r + 1) * chunk)
            other = o_ref[span, cols].astype(BF16)
            grad = dot(other, high, dims) + dot(other, small, dims)
            normed = n_ref[span, cols]
            ph, pl_ = split(grad * normed)
            second = dot(ph, mean, NN) + dot(pl_, mean, NN)
            gl_ref[span, cols] = ((grad - normed * second) * r_ref[span, cols]).astype(BF16)
        parts.append(dot(p_ref[...], gl_ref[:, cols], TN))
    place(w_ref, jnp.concatenate(parts, axis=1), key)


def points_kernel(total, c_ref, gk_ref, gv_ref, wq_ref, wk_ref, wv_ref, own_ref, got_ref, m_ref, gp_ref, gq_ref, q_ref):
    rows, width = c_ref.shape
    ns, nx = lax.axis_size("sub"), lax.axis_size("mp")
    s, x = lax.axis_index("sub"), lax.axis_index("mp")
    half = width // ns
    lows = []
    for g in range(ns):
        cols = slice(g * half, (g + 1) * half)
        packed = jnp.where(s == g, own_ref[...], got_ref[...])
        low = (packed / total).astype(BF16).astype(F32)
        lows.append(low)
        q_ref[:, cols] = dot(c_ref[:, cols], unpack(low).astype(BF16), NT).astype(BF16)
    whole = jnp.concatenate(lows, axis=1)
    cb = width // nx
    high, rest = split(m_ref[...])
    third = (m_ref[...] - high.astype(F32) - rest.astype(F32)).astype(BF16)
    for xb in range(nx):

        @pl.when(x == xb)
        def _():
            state = unpack(whole[:, xb * cb : (xb + 1) * cb]).astype(BF16)
            gq_ref[...] = (dot(high, state, NT) + dot(rest, state, NT) + dot(third, state, NT)) / total

    chunk = 256
    for r in range(rows // chunk):
        span = slice(r * chunk, (r + 1) * chunk)
        acc = dot(gk_ref[span, :], wk_ref[...], NT) + dot(gv_ref[span, :], wv_ref[...], NT)
        gp_ref[span, :] = (acc + dot(q_ref[span, :], wq_ref[...], NT)).astype(BF16)


def pairs(size, bit):
    return [(i, i ^ bit) for i in range(size)]


def swap(value, axis, bit):
    return lax.ppermute(value, axis, pairs(lax.axis_size(axis), bit))


def bits(axis):
    bit = 1
    while bit < lax.axis_size(axis):
        yield bit
        bit *= 2


def sum_all(value):
    own = value[0] + swap(value[1], "sub", 1)
    for axis in ("mp", "points"):
        for bit in bits(axis):
            own = own + swap(own, axis, bit)
    return own, swap(own, "sub", 1)


def scatter(value, axes):
    got = swap(value[1], "sub", 1)
    kept = value[0]
    for place_, axis in enumerate(axes):
        for bit in bits(axis):
            shape = kept.shape
            if place_ == 0:
                view = lambda a, i: a.reshape((shape[0] // 2, 2) + shape[1:])[:, i]
            else:
                view = lambda a, i: a.reshape((shape[0] // 2, 2) + shape[1:])[:, i]
            send = view(kept, 1) + view(got, 1)
            kept = view(kept, 0) + view(got, 0)
            got = swap(send, axis, bit)
        kept, got = kept[0], got[0]
    return kept + got


def local(points_in, cotangent, w_query, w_key, w_value):
    rows, width = points_in.shape
    nz, nx, ns = lax.axis_size("points"), lax.axis_size("mp"), lax.axis_size("sub")
    total = rows * nz * nx * ns
    half = width // ns
    rb, cb = width // (nz * ns), width // nx
    by_x = jax.ShapeDtypeStruct((ns, nx, nz, rb, cb), F32)
    by_z = jax.ShapeDtypeStruct((ns, nz, nx, rb, cb), F32)
    state = jax.ShapeDtypeStruct((ns, HS, half), F32)
    wide = jax.ShapeDtypeStruct((rows, width), F32)
    low = jax.ShapeDtypeStruct((rows, width), BF16)

    cross, grad_part = pl.pallas_call(
        cross_kernel, out_shape=(by_x, state), in_specs=[VMEM] * 3, out_specs=(VMEM,) * 2, compiler_params=PARAMS, name="cross"
    )(points_in, cotangent, w_query)
    key_norm, key_inv, value_norm, value_inv, state_part = pl.pallas_call(
        norm_kernel,
        out_shape=(wide, wide, wide, wide, state),
        in_specs=[VMEM] * 3,
        out_specs=(VMEM,) * 5,
        scratch_shapes=[pltpu.VMEM((2, 2, width, width), BF16)],
        compiler_params=PARAMS,
        name="norm",
    )(points_in, w_key, w_value)
    g_own, g_got = sum_all(grad_part)
    s_own, s_got = sum_all(state_part)
    m_total = scatter(cross, ("mp", "points"))

    def back(key, normed, inverse, other):
        return pl.pallas_call(
            functools.partial(back_kernel, total, key),
            out_shape=(by_x if key else by_z, low),
            in_specs=[VMEM] * 6,
            out_specs=(VMEM,) * 2,
            compiler_params=PARAMS,
            name="back_key" if key else "back_value",
        )(points_in, normed, inverse, other, g_own, g_got)

    key_blocks, key_low = back(True, key_norm, key_inv, value_norm)
    value_blocks, value_low = back(False, value_norm, value_inv, key_norm)
    grad_key = scatter(key_blocks, ("mp", "points")) / total
    grad_value = scatter(value_blocks, ("points", "mp")) / total
    grad_points, grad_query = pl.pallas_call(
        functools.partial(points_kernel, total),
        out_shape=(low, jax.ShapeDtypeStruct((rb, cb), F32)),
        in_specs=[VMEM] * 9,
        out_specs=(VMEM,) * 2,
        scratch_shapes=[pltpu.VMEM((rows, width), BF16)],
        compiler_params=PARAMS,
        name="grad_points",
    )(cotangent, key_low, value_low, w_query, w_key, w_value, s_own, s_got, m_total)
    return grad_points, grad_query, grad_key, grad_value


def solution(mesh):
    whole = P(("groups", "points", "mp", "sub"), None)
    block = P(("groups", "points", "sub"), "mp")
    return jax.shard_map(
        local,
        mesh=mesh,
        in_specs=(whole, whole, P(), P(), P()),
        out_specs=(whole, block, block, block),
        check_vma=False,
    )
```

```python
import functools

import jax
import jax.numpy as jnp
from jax import lax
from jax.experimental import pallas as pl
from jax.experimental.pallas import tpu as pltpu
from jax.sharding import PartitionSpec as P

HS = 32
F32 = jnp.float32
BF16 = jnp.bfloat16
NT = (((1,), (1,)), ((), ()))
TN = (((0,), (0,)), ((), ()))
NN = (((1,), (0,)), ((), ()))
VMEM = pl.BlockSpec(memory_space=pltpu.VMEM)
HBM = pl.BlockSpec(memory_space=pltpu.HBM)
ANY = pl.BlockSpec(memory_space=pl.ANY)
CHUNKS = 4
QUERY_LAST = False
ORDER = "MKVPTKVKV"
US = {"add_key": 5.0, "back_key": 5.0, "back_value": 5.0}

PARAMS = pltpu.CompilerParams(vmem_limit_bytes=16 * 1024 * 1024)


def dot(a, b, dims):
    return lax.dot_general(a, b, dims, preferred_element_type=F32)


def split(x):
    high = x.astype(BF16)
    return high, (x - high.astype(F32)).astype(BF16)


def head_mask(size):
    rows = lax.broadcasted_iota(jnp.int32, (size, size), 0) // HS
    cols = lax.broadcasted_iota(jnp.int32, (size, size), 1) // HS
    return rows == cols


def averager(size):
    return jnp.where(head_mask(size), F32(1.0 / HS), F32(0.0)).astype(BF16)


def pack(full):
    size = full.shape[0]
    kept = jnp.where(head_mask(size), full, F32(0.0))
    total = kept[:HS]
    for i in range(1, size // HS):
        total = total + kept[i * HS : (i + 1) * HS]
    return total


def unpack(packed):
    size = packed.shape[1]
    tiled = jnp.concatenate([packed] * (size // HS), axis=0)
    return jnp.where(head_mask(size), tiled, F32(0.0))


def place(refs, value, x_first):
    z, x, s = lax.axis_index("points"), lax.axis_index("mp"), lax.axis_index("sub")
    nz, nx, ns = lax.axis_size("points"), lax.axis_size("mp"), lax.axis_size("sub")
    rb, cb = value.shape[0] // (nz * ns), value.shape[1] // nx
    for zb in range(nz):
        for sb in range(ns):
            row = (zb * ns + sb) * rb
            for xb in range(nx):
                block = value[row : row + rb, xb * cb : (xb + 1) * cb]
                first, second = (x ^ xb, z ^ zb) if x_first else (z ^ zb, x ^ xb)
                refs[s ^ sb, first, second] = block


def cross_kernel(p_hbm, c_hbm, wq_hbm, m_ref, g_ref, p_ref, pt_ref, c_ref, wq_ref, sums, sems):
    rows, width = p_hbm.shape
    ns = lax.axis_size("sub")
    s = lax.axis_index("sub")
    half = width // ns
    chunk = rows // CHUNKS
    spans = [slice(r * chunk, (r + 1) * chunk) for r in range(CHUNKS)]
    loads = []
    for r, span in enumerate(spans):
        for k, (src, dst) in enumerate(((p_hbm, p_ref), (c_hbm, c_ref))):
            loads.append(pltpu.make_async_copy(src.at[span, :], dst.at[span, :], sems.at[2 * r + k]))
    loads.append(pltpu.make_async_copy(wq_hbm, wq_ref, sems.at[2 * CHUNKS]))
    for load in loads:
        load.start()
    for r, span in enumerate(spans):
        loads[2 * r].wait()
        flipped = p_ref[span, :].T
        pt_ref[:, span] = flipped
        loads[2 * r + 1].wait()
        for g in range(ns):
            cols = slice(g * half, (g + 1) * half)
            part = dot(flipped, c_ref[span, cols], NN)
            sums[:, cols] = part if r == 0 else sums[:, cols] + part
    loads[-1].wait()
    for g in range(ns):
        cols = slice(g * half, (g + 1) * half)
        high, low = split(sums[:, cols])
        wq = wq_ref[:, cols]
        g_ref[s ^ g] = pack(dot(wq, high, TN) + dot(wq, low, TN))
    place(m_ref, sums[...], True)


def norm_kernel(g, p_ref, wk_ref, wv_ref, *rest):
    ns = lax.axis_size("sub")
    s = lax.axis_index("sub")
    kn_ref, kr_ref, vn_ref, vr_ref, s_ref, c_ref, sq_ref = rest[-7:]
    rows, width = p_ref.shape
    half = width // ns
    cols = slice(g * half, (g + 1) * half)
    mean = averager(half)
    chunk = rows // CHUNKS
    spans = [slice(r * chunk, (r + 1) * chunk) for r in range(CHUNKS)]
    for w, w_ref in enumerate((wk_ref, wv_ref)):
        raw = w_ref[:, cols]
        high, low = split(raw.astype(F32) - dot(raw, mean, NN))
        for span in spans:
            p = p_ref[span, :]
            centred = dot(p, high, NN) + dot(p, low, NN)
            c_ref[w, span, :] = centred
            sq_ref[w, span, :] = (centred * centred).astype(BF16)
    for w, (n_ref, r_ref) in enumerate(((kn_ref, kr_ref), (vn_ref, vr_ref))):
        for span in spans:
            inverse = lax.rsqrt(dot(sq_ref[w, span, :], mean, NN) + 1e-05)
            n_ref[span, :] = c_ref[w, span, :] * inverse
            r_ref[span, :] = inverse
    packed = pack(dot(kn_ref[...].astype(BF16), vn_ref[...].astype(BF16), TN))
    if g < ns - 1:
        s_ref[...] = packed
    else:
        s_ref[s ^ g] = packed
        for earlier in range(g):
            s_ref[s ^ earlier] = rest[earlier][...]


def back_kernel(total, key, pt_ref, own_ref, got_ref, *rest):
    w_ref, gl_ref, grad_ref, prod_ref = rest[-4:]
    rows, width = gl_ref.shape
    ns = lax.axis_size("sub")
    n_refs, r_refs, o_refs = rest[:ns], rest[ns : 2 * ns], rest[2 * ns : 3 * ns]
    s = lax.axis_index("sub")
    half = width // ns
    mean = averager(half)
    dims = NT if key else NN
    chunk = rows // CHUNKS
    spans = [slice(r * chunk, (r + 1) * chunk) for r in range(CHUNKS)]
    for g in range(ns):
        cols = slice(g * half, (g + 1) * half)
        packed = jnp.where(s == g, own_ref[...], got_ref[...])
        full = unpack((packed / total).astype(BF16).astype(F32))
        if key:
            grouped = dot(mean, full.astype(BF16), NN)
        else:
            grouped = dot(full.astype(BF16), mean, NN)
        high, small = split(full - grouped)
        for span in spans:
            other = o_refs[g][span, :].astype(BF16)
            grad = dot(other, high, dims) + dot(other, small, dims)
            grad_ref[span, cols] = grad
            prod_ref[span, cols] = (grad * n_refs[g][span, :]).astype(BF16)
    for g in range(ns):
        cols = slice(g * half, (g + 1) * half)
        for span in spans:
            second = dot(prod_ref[span, cols], mean, NN)
            gl_ref[span, cols] = ((grad_ref[span, cols] - n_refs[g][span, :] * second) * r_refs[g][span, :]).astype(BF16)
    parts = [dot(pt_ref[...], gl_ref[:, g * half : (g + 1) * half], NN) for g in range(ns)]
    place(w_ref, jnp.concatenate(parts, axis=1), not key)


def points_kernel(gk_ref, gv_ref, wk_ref, wv_ref, *rest):
    acc_ref = rest[-1]
    rows = acc_ref.shape[0]
    chunk = rows // CHUNKS
    for r in range(CHUNKS):
        span = slice(r * chunk, (r + 1) * chunk)
        acc_ref[span, :] = dot(gk_ref[span, :], wk_ref[...], NT) + dot(gv_ref[span, :], wv_ref[...], NT)


def query_kernel(total, acc_ref, c_ref, wq_ref, own_ref, got_ref, m_ref, *rest):
    gp_ref, gq_ref, q_ref = rest[-3:]
    rows, width = c_ref.shape
    ns, nx = lax.axis_size("sub"), lax.axis_size("mp")
    s, x = lax.axis_index("sub"), lax.axis_index("mp")
    half = width // ns
    lows = []
    for g in range(ns):
        cols = slice(g * half, (g + 1) * half)
        packed = jnp.where(s == g, own_ref[...], got_ref[...])
        low = (packed / total).astype(BF16).astype(F32)
        lows.append(low)
        q_ref[:, cols] = dot(c_ref[:, cols], unpack(low).astype(BF16), NT).astype(BF16)
    whole = jnp.concatenate(lows, axis=1)
    cb = width // nx
    high, rest_ = split(m_ref[...])
    third = (m_ref[...] - high.astype(F32) - rest_.astype(F32)).astype(BF16)
    for xb in range(nx):

        @pl.when(x == xb)
        def _():
            state = unpack(whole[:, xb * cb : (xb + 1) * cb]).astype(BF16)
            gq_ref[...] = (dot(high, state, NT) + dot(rest_, state, NT) + dot(third, state, NT)) / total

    chunk = rows // CHUNKS
    for r in range(CHUNKS):
        span = slice(r * chunk, (r + 1) * chunk)
        gp_ref[span, :] = (acc_ref[span, :] + dot(q_ref[span, :], wq_ref[...], NT)).astype(BF16)


def step_kernel(tailed, *refs):
    kept_ref, got_ref = refs[:2]
    send_ref, keep_ref = refs[-3 if tailed else -2 :][:2]
    count, size = keep_ref.shape[0], keep_ref.shape[1]
    for i in range(count):
        even, odd = 2 * i, 2 * i + 1
        keep_ref[i] = kept_ref[even] + got_ref[even * size : (even + 1) * size, :]
        send_ref[i * size : (i + 1) * size, :] = kept_ref[odd] + got_ref[odd * size : (odd + 1) * size, :]
    if tailed:
        refs[-1][...] = refs[2][...]
        joined = 2 * count * size
        if got_ref.shape[0] > joined:
            refs[-1][...] += got_ref[joined:, :]
        send_ref[count * size :, :] = refs[-1][...]


def pairs(size, bit):
    return [(i, i ^ bit) for i in range(size)]


def swap(value, axis, bit):
    return lax.ppermute(value, axis, pairs(lax.axis_size(axis), bit))


def bits(axis):
    bit = 1
    while bit < lax.axis_size(axis):
        yield bit
        bit *= 2


def call(kernel, name, out_shape, inputs, specs, after=(), scratch=(), us=1.0):
    us = US.get(name, us)
    inputs, specs = list(inputs) + list(after), list(specs) + [ANY] * len(after)
    return pl.pallas_call(
        kernel,
        out_shape=out_shape,
        in_specs=specs,
        out_specs=(VMEM,) * len(out_shape),
        scratch_shapes=scratch,
        compiler_params=PARAMS,
        cost_estimate=pl.CostEstimate(flops=int(us * 1.1e9), bytes_accessed=int(us * 1e5), transcendentals=0),
        name=name,
    )(*inputs)


def sum_kernel(a_ref, b_ref, *rest):
    rest[-1][...] = a_ref[...] + b_ref[...]


class Total:
    def __init__(self, parts, axes):
        self.value, self.got = parts[0], swap(parts[1], "sub", 1)
        self.todo = [(axis, bit) for axis in axes for bit in bits(axis)]

    def add(self, after=()):
        (self.value,) = call(
            sum_kernel,
            "sum",
            (jax.ShapeDtypeStruct(self.value.shape, F32),),
            (self.value, self.got),
            [VMEM] * 2,
            after=after,
            us=0.1,
        )
        self.sent = self.value
        if self.todo:
            self.got = swap(self.value, *self.todo.pop(0))
            return True
        self.got = swap(self.value, "sub", 1)
        return False


class Scatter:
    def __init__(self, blocks, axes, name):
        self.name = name
        self.sizes = blocks.shape
        self.kept = blocks[0]
        self.tail = None
        self.got = swap(blocks[1], "sub", 1)
        self.todo = [(axis, bit) for axis in axes for bit in bits(axis)]
        self.axes = axes

    def step(self, after=(), tail=None):
        axis, bit = self.todo.pop(0)
        rb, cb = self.sizes[-2:]
        inner = self.sizes[2] if axis == self.axes[0] else 1
        size = inner * rb
        kept = self.kept.reshape(-1, size, cb)
        got = self.got.reshape(-1, cb)
        count = kept.shape[0] // 2
        if tail is not None:
            self.tail = tail.reshape(-1, cb)
        tailed = self.tail is not None
        extra = self.tail.shape[0] if tailed else 0
        shape = jax.ShapeDtypeStruct
        outs = (shape((count * size + extra, cb), F32), shape((count, size, cb), F32))
        if tailed:
            outs += (shape((extra, cb), F32),)
        res = call(
            functools.partial(step_kernel, tailed),
            "add_" + self.name,
            outs,
            (kept, got) + ((self.tail,) if tailed else ()),
            [VMEM] * (3 if tailed else 2),
            after=after,
            us=0.2,
        )
        self.kept = res[1]
        if tailed:
            self.tail = res[2]
        self.sent = res[0]
        self.got = swap(res[0], axis, bit)

    def end(self, after=()):
        rb, cb = self.sizes[-2:]
        (total,) = call(
            sum_kernel,
            "end_" + self.name,
            (jax.ShapeDtypeStruct((rb, cb), F32),),
            (self.kept.reshape(rb, cb), self.got.reshape(rb, cb)),
            [VMEM] * 2,
            after=after,
            us=0.1,
        )
        return total

    def result(self):
        rb, cb = self.sizes[-2:]
        total = self.kept.reshape(rb, cb) + self.got.reshape(-1, cb)[:rb]
        if self.tail is None:
            return total
        return total, self.tail + self.got.reshape(-1, cb)[rb:]


def local(points_in, cotangent, w_query, w_key, w_value):
    rows, width = points_in.shape
    nz, nx, ns = lax.axis_size("points"), lax.axis_size("mp"), lax.axis_size("sub")
    total = rows * nz * nx * ns
    half = width // ns
    rb, cb = width // (nz * ns), width // nx
    shape = jax.ShapeDtypeStruct
    by_x = shape((ns, nx, nz, rb, cb), F32)
    by_z = shape((ns, nz, nx, rb, cb), F32)
    state = shape((ns, HS, half), F32)
    low = shape((rows, width), BF16)
    tall = shape((rows, half), F32)

    cross, grad_part, p_in, p_flip = call(
        cross_kernel,
        "cross",
        (by_x, state, low, shape((width, rows), BF16)),
        [pltpu.with_memory_space_constraint(a, pltpu.HBM) for a in (points_in, cotangent, w_query)],
        [HBM] * 3,
        scratch=[
            pltpu.VMEM((rows, width), BF16),
            pltpu.VMEM((width, width), BF16),
            pltpu.VMEM((width, width), F32),
            pltpu.SemaphoreType.DMA((2 * CHUNKS + 1,)),
        ],
        us=3.0,
    )
    cross_sum = Scatter(cross, ("mp", "points"), "query")
    g_sum = Total(grad_part, ("mp", "points"))
    norms, states = [], []
    g_sum.add()
    for g in range(ns):
        norms.append(
            call(
                functools.partial(norm_kernel, g),
                "norm",
                (tall, tall, tall, tall, state if g == ns - 1 else shape((HS, half), F32)),
                [p_in, w_key, w_value] + states,
                [VMEM] * (3 + g),
                after=(g_sum.sent,),
                scratch=[pltpu.VMEM((2, rows, half), F32), pltpu.VMEM((2, rows, half), BF16)],
                us=2.3,
            )
        )
        states.append(norms[-1][-1])
        g_sum.add(after=(states[-1],))
        if g == 0:
            cross_sum.step(after=(g_sum.sent,))
            g_sum.add(after=(cross_sum.sent,))
    while g_sum.todo:
        g_sum.add()
    g_own, g_got = g_sum.value, g_sum.got
    key_norm, key_inv, value_norm, value_inv, _ = zip(*norms)
    s_half = states[-1][0] + swap(states[-1][1], "sub", 1)
    cross_sum.step(after=(g_own,))

    def back(key, normed, inverse, other, after):
        return call(
            functools.partial(back_kernel, total, key),
            "back_key" if key else "back_value",
            (by_z if key else by_x, low),
            (p_flip, g_own, g_got) + normed + inverse + other,
            [VMEM] * (3 + 3 * ns),
            after=after,
            scratch=[pltpu.VMEM((rows, width), F32), pltpu.VMEM((rows, width), BF16)],
            us=2.1,
        )

    key_blocks, key_low = back(True, key_norm, key_inv, value_norm, (cross_sum.sent,))
    key_sum = Scatter(key_blocks, ("points", "mp"), "key")
    value_blocks, value_low = back(False, value_norm, value_inv, key_norm, (key_low,))
    value_sum = Scatter(value_blocks, ("mp", "points"), "value")
    last = value_low
    m_total = None
    for turn in ORDER:
        if turn == "P":
            (partial,) = call(
                points_kernel,
                "grad_points_part",
                (shape((rows, width), F32),),
                (key_low, value_low, w_key, w_value),
                [VMEM] * 4,
                after=(last,),
                us=1.3,
            )
            last = partial
            continue
        if turn == "T":
            if not cross_sum.todo:
                m_total = cross_sum.end(after=(last,))
                last = m_total
            continue
        one = {"M": cross_sum, "K": key_sum, "V": value_sum}[turn]
        one.step(after=(last,), tail=s_half if turn == "K" and one.tail is None else None)
        last = one.sent
    while cross_sum.todo or key_sum.todo or value_sum.todo:
        for turn in (cross_sum, key_sum, value_sum):
            if turn.todo:
                turn.step()
    if m_total is None:
        m_total = cross_sum.end()
    grad_value = value_sum.result()
    grad_key, s_own = key_sum.result()
    s_own = s_own.reshape(HS, half)
    s_got = swap(s_own, "sub", 1)
    grad_points, grad_query = call(
        functools.partial(query_kernel, total),
        "grad_points",
        (low, shape((rb, cb), F32)),
        (partial, cotangent, w_query, s_own, s_got, m_total),
        [VMEM] * 6,
        after=(last,) if QUERY_LAST else (),
        scratch=[pltpu.VMEM((rows, width), BF16)],
        us=1.5,
    )
    return grad_points, grad_query, grad_key / total, grad_value / total


def solution(mesh):
    whole = P(("groups", "points", "mp", "sub"), None)
    block = P(("groups", "points", "sub"), "mp")
    return jax.shard_map(
        local,
        mesh=mesh,
        in_specs=(whole, whole, P(), P(), P()),
        out_specs=(whole, block, block, block),
        check_vma=False,
    )
```

```python
import functools

import jax
import jax.numpy as jnp
from jax import lax
from jax.experimental import pallas as pl
from jax.experimental.pallas import tpu as pltpu
from jax.sharding import PartitionSpec as P

HS = 32
F32 = jnp.float32
BF16 = jnp.bfloat16
NT = (((1,), (1,)), ((), ()))
TN = (((0,), (0,)), ((), ()))
NN = (((1,), (0,)), ((), ()))
VMEM = pl.BlockSpec(memory_space=pltpu.VMEM)
HBM = pl.BlockSpec(memory_space=pltpu.HBM)
ANY = pl.BlockSpec(memory_space=pl.ANY)
CHUNKS = 4
ORDER = "MKVPKVTVK"
US = {"add_key_0": 5.0, "sum_0": 5.0, "back_key": 5.0, "back_value": 5.0}

PARAMS = pltpu.CompilerParams(vmem_limit_bytes=16 * 1024 * 1024)


def dot(a, b, dims):
    return lax.dot_general(a, b, dims, preferred_element_type=F32)


def split(x):
    high = x.astype(BF16)
    return high, (x - high.astype(F32)).astype(BF16)


def head_mask(size):
    rows = lax.broadcasted_iota(jnp.int32, (size, size), 0) // HS
    cols = lax.broadcasted_iota(jnp.int32, (size, size), 1) // HS
    return rows == cols


def averager(size):
    return jnp.where(head_mask(size), F32(1.0 / HS), F32(0.0)).astype(BF16)


def pack(full):
    size = full.shape[0]
    kept = jnp.where(head_mask(size), full, F32(0.0))
    total = kept[:HS]
    for i in range(1, size // HS):
        total = total + kept[i * HS : (i + 1) * HS]
    return total


def unpack(packed):
    size = packed.shape[1]
    tiled = jnp.concatenate([packed] * (size // HS), axis=0)
    return jnp.where(head_mask(size), tiled, F32(0.0))


def place(refs, value, x_first):
    z, x, s = lax.axis_index("points"), lax.axis_index("mp"), lax.axis_index("sub")
    nz, nx, ns = lax.axis_size("points"), lax.axis_size("mp"), lax.axis_size("sub")
    rb, cb = value.shape[0] // (nz * ns), value.shape[1] // nx
    for zb in range(nz):
        for sb in range(ns):
            row = (zb * ns + sb) * rb
            for xb in range(nx):
                block = value[row : row + rb, xb * cb : (xb + 1) * cb]
                first, second = (x ^ xb, z ^ zb) if x_first else (z ^ zb, x ^ xb)
                refs[s ^ sb, first, second] = block


def cross_kernel(p_hbm, c_hbm, wq_hbm, sums, g_ref, p_ref, pt_ref, c_ref, wq_ref, sems):
    rows, width = p_hbm.shape
    ns = lax.axis_size("sub")
    s = lax.axis_index("sub")
    half = width // ns
    chunk = rows // CHUNKS
    spans = [slice(r * chunk, (r + 1) * chunk) for r in range(CHUNKS)]
    loads = []
    for r, span in enumerate(spans):
        for k, (src, dst) in enumerate(((p_hbm, p_ref), (c_hbm, c_ref))):
            loads.append(pltpu.make_async_copy(src.at[span, :], dst.at[span, :], sems.at[2 * r + k]))
    loads.append(pltpu.make_async_copy(wq_hbm, wq_ref, sems.at[2 * CHUNKS]))
    for load in loads:
        load.start()
    for r, span in enumerate(spans):
        loads[2 * r].wait()
        flipped = p_ref[span, :].T
        pt_ref[:, span] = flipped
        loads[2 * r + 1].wait()
        for g in range(ns):
            cols = slice(g * half, (g + 1) * half)
            part = dot(flipped, c_ref[span, cols], NN)
            sums[:, cols] = part if r == 0 else sums[:, cols] + part
    loads[-1].wait()
    for g in range(ns):
        cols = slice(g * half, (g + 1) * half)
        high, low = split(sums[:, cols])
        wq = wq_ref[:, cols]
        g_ref[s ^ g] = pack(dot(wq, high, TN) + dot(wq, low, TN))


def deal_kernel(sums_ref, *rest):
    place(rest[-1], sums_ref[...], True)


def norm_kernel(g, p_ref, wk_ref, wv_ref, *rest):
    ns = lax.axis_size("sub")
    s = lax.axis_index("sub")
    kn_ref, kr_ref, vn_ref, vr_ref, s_ref, c_ref, sq_ref = rest[-7:]
    rows, width = p_ref.shape
    half = width // ns
    cols = slice(g * half, (g + 1) * half)
    mean = averager(half)
    chunk = rows // CHUNKS
    spans = [slice(r * chunk, (r + 1) * chunk) for r in range(CHUNKS)]
    for w, w_ref in enumerate((wk_ref, wv_ref)):
        raw = w_ref[:, cols]
        high, low = split(raw.astype(F32) - dot(raw, mean, NN))
        for span in spans:
            p = p_ref[span, :]
            centred = dot(p, high, NN) + dot(p, low, NN)
            c_ref[w, span, :] = centred
            sq_ref[w, span, :] = (centred * centred).astype(BF16)
    for w, (n_ref, r_ref) in enumerate(((kn_ref, kr_ref), (vn_ref, vr_ref))):
        for span in spans:
            inverse = lax.rsqrt(dot(sq_ref[w, span, :], mean, NN) + 1e-05)
            n_ref[span, :] = c_ref[w, span, :] * inverse
            r_ref[span, :] = inverse
    packed = pack(dot(kn_ref[...].astype(BF16), vn_ref[...].astype(BF16), TN))
    if g < ns - 1:
        s_ref[...] = packed
    else:
        s_ref[s ^ g] = packed
        for earlier in range(g):
            s_ref[s ^ earlier] = rest[earlier][...]


def back_kernel(total, key, pt_ref, own_ref, got_ref, *rest):
    w_ref, gl_ref, grad_ref, prod_ref = rest[-4:]
    rows, width = gl_ref.shape
    ns = lax.axis_size("sub")
    n_refs, r_refs, o_refs = rest[:ns], rest[ns : 2 * ns], rest[2 * ns : 3 * ns]
    s = lax.axis_index("sub")
    half = width // ns
    mean = averager(half)
    dims = NT if key else NN
    chunk = rows // CHUNKS
    spans = [slice(r * chunk, (r + 1) * chunk) for r in range(CHUNKS)]
    for g in range(ns):
        cols = slice(g * half, (g + 1) * half)
        packed = jnp.where(s == g, own_ref[...], got_ref[...])
        full = unpack((packed / total).astype(BF16).astype(F32))
        if key:
            grouped = dot(mean, full.astype(BF16), NN)
        else:
            grouped = dot(full.astype(BF16), mean, NN)
        high, small = split(full - grouped)
        for span in spans:
            other = o_refs[g][span, :].astype(BF16)
            grad = dot(other, high, dims) + dot(other, small, dims)
            grad_ref[span, cols] = grad
            prod_ref[span, cols] = (grad * n_refs[g][span, :]).astype(BF16)
    for g in range(ns):
        cols = slice(g * half, (g + 1) * half)
        for span in spans:
            second = dot(prod_ref[span, cols], mean, NN)
            gl_ref[span, cols] = ((grad_ref[span, cols] - n_refs[g][span, :] * second) * r_refs[g][span, :]).astype(BF16)
    parts = [dot(pt_ref[...], gl_ref[:, g * half : (g + 1) * half], NN) for g in range(ns)]
    place(w_ref, jnp.concatenate(parts, axis=1), not key)


def points_kernel(gk_ref, gv_ref, wk_ref, wv_ref, *rest):
    acc_ref = rest[-1]
    rows = acc_ref.shape[0]
    chunk = rows // CHUNKS
    for r in range(CHUNKS):
        span = slice(r * chunk, (r + 1) * chunk)
        acc_ref[span, :] = dot(gk_ref[span, :], wk_ref[...], NT) + dot(gv_ref[span, :], wv_ref[...], NT)


def query_kernel(total, acc_ref, c_ref, wq_ref, own_ref, got_ref, m_ref, *rest):
    gp_ref, gq_ref, q_ref = rest[-3:]
    rows, width = c_ref.shape
    ns, nx = lax.axis_size("sub"), lax.axis_size("mp")
    s, x = lax.axis_index("sub"), lax.axis_index("mp")
    half = width // ns
    lows = []
    for g in range(ns):
        cols = slice(g * half, (g + 1) * half)
        packed = jnp.where(s == g, own_ref[...], got_ref[...])
        low = (packed / total).astype(BF16).astype(F32)
        lows.append(low)
        q_ref[:, cols] = dot(c_ref[:, cols], unpack(low).astype(BF16), NT).astype(BF16)
    whole = jnp.concatenate(lows, axis=1)
    cb = width // nx
    high, rest_ = split(m_ref[...])
    third = (m_ref[...] - high.astype(F32) - rest_.astype(F32)).astype(BF16)
    for xb in range(nx):

        @pl.when(x == xb)
        def _():
            state = unpack(whole[:, xb * cb : (xb + 1) * cb]).astype(BF16)
            gq_ref[...] = (dot(high, state, NT) + dot(rest_, state, NT) + dot(third, state, NT)) / total

    chunk = rows // CHUNKS
    for r in range(CHUNKS):
        span = slice(r * chunk, (r + 1) * chunk)
        gp_ref[span, :] = (acc_ref[span, :] + dot(q_ref[span, :], wq_ref[...], NT)).astype(BF16)


def step_kernel(tailed, *refs):
    kept_ref, got_ref = refs[:2]
    send_ref, keep_ref = refs[-3 if tailed else -2 :][:2]
    count, size = keep_ref.shape[0], keep_ref.shape[1]
    for i in range(count):
        even, odd = 2 * i, 2 * i + 1
        keep_ref[i] = kept_ref[even] + got_ref[even * size : (even + 1) * size, :]
        send_ref[i * size : (i + 1) * size, :] = kept_ref[odd] + got_ref[odd * size : (odd + 1) * size, :]
    if tailed:
        refs[-1][...] = refs[2][...]
        joined = 2 * count * size
        if got_ref.shape[0] > joined:
            refs[-1][...] += got_ref[joined:, :]
        send_ref[count * size :, :] = refs[-1][...]


def pairs(size, bit):
    return [(i, i ^ bit) for i in range(size)]


def swap(value, axis, bit):
    return lax.ppermute(value, axis, pairs(lax.axis_size(axis), bit))


def bits(axis):
    bit = 1
    while bit < lax.axis_size(axis):
        yield bit
        bit *= 2


def call(kernel, name, out_shape, inputs, specs, after=(), scratch=(), us=1.0):
    us = US.get(name, us)
    inputs, specs = list(inputs) + list(after), list(specs) + [ANY] * len(after)
    return pl.pallas_call(
        kernel,
        out_shape=out_shape,
        in_specs=specs,
        out_specs=(VMEM,) * len(out_shape),
        scratch_shapes=scratch,
        compiler_params=PARAMS,
        cost_estimate=pl.CostEstimate(flops=int(us * 1.1e9), bytes_accessed=int(us * 1e5), transcendentals=0),
        name=name,
    )(*inputs)


def sum_kernel(a_ref, b_ref, *rest):
    rest[-1][...] = a_ref[...] + b_ref[...]


def end_kernel(kept_ref, got_ref, *rest):
    rb = kept_ref.shape[0]
    if got_ref.shape[0] == rb:
        rest[-1][...] = kept_ref[...] + got_ref[...]
    else:
        rest[-2][...] = kept_ref[...] + got_ref[:rb, :]
        rest[-1][...] = rest[0][...] + got_ref[rb:, :]


def scale_kernel(total, *refs):
    for i in range(2):
        refs[-2 + i][...] = (refs[2 * i][...] + refs[2 * i + 1][...]) / total


class Total:
    def __init__(self, parts, axes):
        self.value, self.got, self.done = parts[0], swap(parts[1], "sub", 1), 0
        self.todo = [(axis, bit) for axis in axes for bit in bits(axis)]

    def add(self, after=()):
        (self.value,) = call(
            sum_kernel,
            "sum_%d" % self.done,
            (jax.ShapeDtypeStruct(self.value.shape, F32),),
            (self.value, self.got),
            [VMEM] * 2,
            after=after,
            us=0.1,
        )
        self.sent = self.value
        self.done += 1
        if self.todo:
            self.got = swap(self.value, *self.todo.pop(0))
            return True
        self.got = swap(self.value, "sub", 1)
        return False


class Scatter:
    def __init__(self, blocks, axes, name):
        self.name, self.done = name, 0
        self.sizes = blocks.shape
        self.kept = blocks[0]
        self.tail = None
        self.got = swap(blocks[1], "sub", 1)
        self.todo = [(axis, bit) for axis in axes for bit in bits(axis)]
        self.axes = axes

    def step(self, after=(), tail=None):
        axis, bit = self.todo.pop(0)
        rb, cb = self.sizes[-2:]
        inner = self.sizes[2] if axis == self.axes[0] else 1
        size = inner * rb
        kept = self.kept.reshape(-1, size, cb)
        got = self.got.reshape(-1, cb)
        count = kept.shape[0] // 2
        if tail is not None:
            self.tail = tail.reshape(-1, cb)
        tailed = self.tail is not None
        extra = self.tail.shape[0] if tailed else 0
        shape = jax.ShapeDtypeStruct
        outs = (shape((count * size + extra, cb), F32), shape((count, size, cb), F32))
        if tailed:
            outs += (shape((extra, cb), F32),)
        res = call(
            functools.partial(step_kernel, tailed),
            "add_%s_%d" % (self.name, self.done),
            outs,
            (kept, got) + ((self.tail,) if tailed else ()),
            [VMEM] * (3 if tailed else 2),
            after=after,
            us=0.2,
        )
        self.kept = res[1]
        if tailed:
            self.tail = res[2]
        self.sent = res[0]
        self.got = swap(res[0], axis, bit)
        self.done += 1

    def end(self, after=()):
        rb, cb = self.sizes[-2:]
        kept = self.kept.reshape(rb, cb)
        shapes = [jax.ShapeDtypeStruct((rb, cb), F32)]
        inputs = [kept, self.got]
        if self.tail is not None:
            shapes.append(jax.ShapeDtypeStruct(self.tail.shape, F32))
            inputs.append(self.tail)
        return call(end_kernel, "end_" + self.name, shapes, inputs, [VMEM] * len(inputs), after=after, us=0.1)


def local(points_in, cotangent, w_query, w_key, w_value):
    rows, width = points_in.shape
    nz, nx, ns = lax.axis_size("points"), lax.axis_size("mp"), lax.axis_size("sub")
    total = rows * nz * nx * ns
    half = width // ns
    rb, cb = width // (nz * ns), width // nx
    shape = jax.ShapeDtypeStruct
    by_x = shape((ns, nx, nz, rb, cb), F32)
    by_z = shape((ns, nz, nx, rb, cb), F32)
    state = shape((ns, HS, half), F32)
    low = shape((rows, width), BF16)
    tall = shape((rows, half), F32)

    sums, grad_part, p_in, p_flip = call(
        cross_kernel,
        "cross",
        (shape((width, width), F32), state, low, shape((width, rows), BF16)),
        [pltpu.with_memory_space_constraint(a, pltpu.HBM) for a in (points_in, cotangent, w_query)],
        [HBM] * 3,
        scratch=[
            pltpu.VMEM((rows, width), BF16),
            pltpu.VMEM((width, width), BF16),
            pltpu.SemaphoreType.DMA((2 * CHUNKS + 1,)),
        ],
        us=3.0,
    )
    g_sum = Total(grad_part, ("mp", "points"))
    (cross,) = call(deal_kernel, "deal", (by_x,), (sums,), [VMEM], us=0.3)
    cross_sum = Scatter(cross, ("mp", "points"), "query")
    g_sum.add()
    cross_sum.step(after=(g_sum.sent,))
    g_sum.add(after=(cross_sum.sent,))
    norms, states = [], []
    for g in range(ns):
        norms.append(
            call(
                functools.partial(norm_kernel, g),
                "norm",
                (tall, tall, tall, tall, state if g == ns - 1 else shape((HS, half), F32)),
                [p_in, w_key, w_value] + states,
                [VMEM] * (3 + g),
                after=(g_sum.sent,),
                scratch=[pltpu.VMEM((2, rows, half), F32), pltpu.VMEM((2, rows, half), BF16)],
                us=2.3,
            )
        )
        states.append(norms[-1][-1])
        g_sum.add(after=(states[-1],))
    while g_sum.todo:
        g_sum.add()
    g_own, g_got = g_sum.value, g_sum.got
    key_norm, key_inv, value_norm, value_inv, _ = zip(*norms)
    s_half = states[-1][0] + swap(states[-1][1], "sub", 1)
    while cross_sum.todo[0][0] == "mp":
        cross_sum.step()
    cross_sum.step(after=(g_own,), tail=s_half)

    def back(key, normed, inverse, other, after):
        return call(
            functools.partial(back_kernel, total, key),
            "back_key" if key else "back_value",
            (by_z if key else by_x, low),
            (p_flip, g_own, g_got) + normed + inverse + other,
            [VMEM] * (3 + 3 * ns),
            after=after,
            scratch=[pltpu.VMEM((rows, width), F32), pltpu.VMEM((rows, width), BF16)],
            us=2.1,
        )

    key_blocks, key_low = back(True, key_norm, key_inv, value_norm, (cross_sum.sent,))
    key_sum = Scatter(key_blocks, ("points", "mp"), "key")
    value_blocks, value_low = back(False, value_norm, value_inv, key_norm, (key_low,))
    value_sum = Scatter(value_blocks, ("mp", "points"), "value")
    last = value_low
    m_total = None
    for turn in ORDER:
        if turn == "P":
            (partial,) = call(
                points_kernel,
                "grad_points_part",
                (shape((rows, width), F32),),
                (key_low, value_low, w_key, w_value),
                [VMEM] * 4,
                after=(last,),
                us=1.3,
            )
            last = partial
            continue
        if turn == "T":
            if not cross_sum.todo:
                m_total, s_own = cross_sum.end(after=(last,))
                last = m_total
            continue
        one = {"M": cross_sum, "K": key_sum, "V": value_sum}[turn]
        one.step(after=(last,))
        last = one.sent
    while cross_sum.todo or key_sum.todo or value_sum.todo:
        for turn in (cross_sum, key_sum, value_sum):
            if turn.todo:
                turn.step()
    if m_total is None:
        m_total, s_own = cross_sum.end()
    s_own = s_own.reshape(HS, half)
    for bit in bits("mp"):
        s_own = s_own + swap(s_own, "mp", bit)
    s_got = swap(s_own, "sub", 1)
    grad_points, grad_query = call(
        functools.partial(query_kernel, total),
        "grad_points",
        (low, shape((rb, cb), F32)),
        (partial, cotangent, w_query, s_own, s_got, m_total),
        [VMEM] * 6,
        scratch=[pltpu.VMEM((rows, width), BF16)],
        us=1.5,
    )
    parts = []
    for one in (key_sum, value_sum):
        parts += [one.kept.reshape(rb, cb), one.got]
    grad_key, grad_value = call(
        functools.partial(scale_kernel, total),
        "scale",
        (shape((rb, cb), F32),) * 2,
        parts,
        [VMEM] * 4,
        us=0.7,
    )
    return grad_points, grad_query, grad_key, grad_value


def solution(mesh):
    whole = P(("groups", "points", "mp", "sub"), None)
    block = P(("groups", "points", "sub"), "mp")
    return jax.shard_map(
        local,
        mesh=mesh,
        in_specs=(whole, whole, P(), P(), P()),
        out_specs=(whole, block, block, block),
        check_vma=False,
    )
```

```python
import functools

import jax
import jax.numpy as jnp
from jax import lax
from jax.experimental import pallas as pl
from jax.experimental.pallas import tpu as pltpu
from jax.sharding import PartitionSpec as P

HS = 32
F32 = jnp.float32
BF16 = jnp.bfloat16
NT = (((1,), (1,)), ((), ()))
TN = (((0,), (0,)), ((), ()))
NN = (((1,), (0,)), ((), ()))
VMEM = pl.BlockSpec(memory_space=pltpu.VMEM)
HBM = pl.BlockSpec(memory_space=pltpu.HBM)
ANY = pl.BlockSpec(memory_space=pl.ANY)
CHUNKS = 2
BLOCKS = 4
NORM_BLOCKS = 1
ORDER = "kVMPkVTkVS"
US = {"end_query": 2.0, "grad_points": 0.01, "back_own": 0.01, "add_key_0": 5.0, "sum_0": 5.0, "back_key": 5.0, "back_value": 5.0}

PARAMS = pltpu.CompilerParams(vmem_limit_bytes=16 * 1024 * 1024)


def dot(a, b, dims):
    return lax.dot_general(a, b, dims, preferred_element_type=F32)


def split(x):
    high = x.astype(BF16)
    return high, (x - high.astype(F32)).astype(BF16)


def head_mask(size):
    rows = lax.broadcasted_iota(jnp.int32, (size, size), 0) // HS
    cols = lax.broadcasted_iota(jnp.int32, (size, size), 1) // HS
    return rows == cols


def averager(size):
    return jnp.where(head_mask(size), F32(1.0 / HS), F32(0.0)).astype(BF16)


def pack(full):
    size = full.shape[0]
    kept = jnp.where(head_mask(size), full, F32(0.0))
    total = kept[:HS]
    for i in range(1, size // HS):
        total = total + kept[i * HS : (i + 1) * HS]
    return total


def unpack(packed):
    size = packed.shape[1]
    tiled = jnp.concatenate([packed] * (size // HS), axis=0)
    return jnp.where(head_mask(size), tiled, F32(0.0))


def bits(axis):
    bit = 1
    while bit < lax.axis_size(axis):
        yield axis, bit
        bit *= 2


def routes(name):
    x, z = list(bits("mp")), list(bits("points"))
    if name == "state":
        return x + z, z + x
    return x + z, z[:1] + x + z[1:]


def place(refs, value, g, name):
    z, x, s = lax.axis_index("points"), lax.axis_index("mp"), lax.axis_index("sub")
    nz, nx, ns = lax.axis_size("points"), lax.axis_size("mp"), lax.axis_size("sub")
    rb, cb = refs.shape[-2:]
    count = value.shape[1] // cb
    for zb in range(nz):
        for sb in range(ns):
            row = (zb * ns + sb) * rb
            for j in range(count):
                away = {"points": z ^ zb, "mp": x ^ (g * count + j)}
                spot = 0
                for t, (axis, bit) in enumerate(routes(name)[sb]):
                    spot = spot + jnp.where((away[axis] & bit) != 0, 1 << t, 0)
                refs[s ^ sb, spot] = value[row : row + rb, j * cb : (j + 1) * cb]


def half_columns(g, width):
    half = width // lax.axis_size("sub")
    return pl.ds(pl.multiple_of(g * half, half), half)


def cross_kernel(p_hbm, c_hbm, wq_hbm, sums, g_ref, p_ref, pt_ref, c_ref, wq_ref, sems):
    rows, width = p_hbm.shape
    ns = lax.axis_size("sub")
    s = lax.axis_index("sub")
    half = width // ns
    chunk = rows // CHUNKS
    spans = [slice(r * chunk, (r + 1) * chunk) for r in range(CHUNKS)]
    loads = []
    for r, span in enumerate(spans):
        for k, (src, dst) in enumerate(((p_hbm, p_ref), (c_hbm, c_ref))):
            loads.append(pltpu.make_async_copy(src.at[span, :], dst.at[span, :], sems.at[2 * r + k]))
    loads.append(pltpu.make_async_copy(wq_hbm, wq_ref, sems.at[2 * CHUNKS]))
    for load in loads:
        load.start()
    for r, span in enumerate(spans):
        loads[2 * r].wait()
        flipped = p_ref[span, :].T
        pt_ref[:, span] = flipped
        loads[2 * r + 1].wait()
        for g in range(ns):
            cols = slice(g * half, (g + 1) * half)
            part = dot(flipped, c_ref[span, cols], NN)
            sums[:, cols] = part if r == 0 else sums[:, cols] + part
    loads[-1].wait()
    for g in range(ns):
        cols = slice(g * half, (g + 1) * half)
        high, low = split(sums[:, cols])
        wq = wq_ref[:, cols]
        g_ref[s ^ g] = pack(dot(wq, high, TN) + dot(wq, low, TN))


def deal_kernel(sums_ref, *rest):
    half = sums_ref.shape[1] // lax.axis_size("sub")
    for g in range(lax.axis_size("sub")):
        place(rest[-1], sums_ref[:, g * half : (g + 1) * half], g, "query")


def norm_kernel(other, p_ref, wk_ref, wv_ref, *rest):
    kn_ref, kr_ref, vn_ref, vr_ref, s_ref, c_ref, sq_ref = rest[-7:]
    rows, width = p_ref.shape
    cols = half_columns(lax.axis_index("sub") ^ other, width)
    mean = averager(width // lax.axis_size("sub"))
    chunk = rows // NORM_BLOCKS
    spans = [slice(r * chunk, (r + 1) * chunk) for r in range(NORM_BLOCKS)]
    for w, w_ref in enumerate((wk_ref, wv_ref)):
        raw = w_ref[:, cols]
        high, low = split(raw.astype(F32) - dot(raw, mean, NN))
        for span in spans:
            p = p_ref[span, :]
            centred = dot(p, high, NN) + dot(p, low, NN)
            c_ref[w, span, :] = centred
            sq_ref[w, span, :] = (centred * centred).astype(BF16)
    for w, (n_ref, r_ref) in enumerate(((kn_ref, kr_ref), (vn_ref, vr_ref))):
        for span in spans:
            inverse = lax.rsqrt(dot(sq_ref[w, span, :], mean, NN) + 1e-05)
            n_ref[span, :] = c_ref[w, span, :] * inverse
            r_ref[span, :] = inverse
    s_ref[...] = pack(dot(kn_ref[...].astype(BF16), vn_ref[...].astype(BF16), TN))


def back_centre(total, key, g_ref):
    full = unpack((g_ref[...] / total).astype(BF16).astype(F32))
    mean = averager(full.shape[0])
    grouped = dot(mean, full.astype(BF16), NN) if key else dot(full.astype(BF16), mean, NN)
    return split(full - grouped)


def back_halves(total, keys, g_ref, sets, gl_refs, grad_refs, prod_refs):
    rows, half = gl_refs[0].shape
    mean = averager(half)
    chunk = rows // BLOCKS
    spans = [slice(r * chunk, (r + 1) * chunk) for r in range(BLOCKS)]
    centred = [back_centre(total, key, g_ref) for key in keys]
    for key, (high, small), (n_ref, r_ref, o_ref), grad_ref, prod_ref in zip(keys, centred, sets, grad_refs, prod_refs):
        dims = NT if key else NN
        for span in spans:
            low = o_ref[span, :].astype(BF16)
            grad = dot(low, high, dims) + dot(low, small, dims)
            grad_ref[span, :] = grad
            prod_ref[span, :] = (grad * n_ref[span, :]).astype(BF16)
    for (n_ref, r_ref, o_ref), gl_ref, grad_ref, prod_ref in zip(sets, gl_refs, grad_refs, prod_refs):
        for span in spans:
            second = dot(prod_ref[span, :], mean, NN)
            gl_ref[span, :] = ((grad_ref[span, :] - n_ref[span, :] * second) * r_ref[span, :]).astype(BF16)


def own_kernel(total, pt_ref, g_ref, kn_ref, kr_ref, vn_ref, vr_ref, *rest):
    gk_ref, gv_ref, wk_ref, wv_ref, kgrad_ref, vgrad_ref, kprod_ref, vprod_ref = rest[-8:]
    sets = ((kn_ref, kr_ref, vn_ref), (vn_ref, vr_ref, kn_ref))
    back_halves(total, (True, False), g_ref, sets, (gk_ref, gv_ref), (kgrad_ref, vgrad_ref), (kprod_ref, vprod_ref))
    wk_ref[...] = dot(pt_ref[...], gk_ref[...], NN)
    wv_ref[...] = dot(pt_ref[...], gv_ref[...], NN)


def other_kernel(total, key, pt_ref, own_ref, g_ref, n_ref, r_ref, o_ref, *rest):
    gl_ref, w_ref, grad_ref, prod_ref = rest[-4:]
    s = lax.axis_index("sub")
    back_halves(total, (key,), g_ref, ((n_ref, r_ref, o_ref),), (gl_ref,), (grad_ref,), (prod_ref,))
    place(w_ref, own_ref[...], s, "key")
    place(w_ref, dot(pt_ref[...], gl_ref[...], NN), 1 - s, "key")


def points_kernel(*refs):
    acc_ref = refs[-1]
    rows, width = acc_ref.shape
    s = lax.axis_index("sub")
    chunk = rows // BLOCKS
    for r in range(BLOCKS):
        span = slice(r * chunk, (r + 1) * chunk)
        total = None
        for w_ref, halves in ((refs[4], refs[:2]), (refs[5], refs[2:4])):
            for other, gl_ref in enumerate(halves):
                part = dot(gl_ref[span, :], w_ref[:, half_columns(s ^ other, width)], NT)
                total = part if total is None else total + part
        acc_ref[span, :] = total


def state_low(total, ref):
    return (ref[...] / total).astype(BF16).astype(F32)


def query_own_kernel(total, acc_ref, c_ref, wq_ref, own_ref, *rest):
    out_ref, q_ref = rest[-2:]
    rows, width = c_ref.shape
    cols = half_columns(lax.axis_index("sub"), width)
    q_ref[...] = dot(c_ref[:, cols], unpack(state_low(total, own_ref)).astype(BF16), NT).astype(BF16)
    chunk = rows // BLOCKS
    for r in range(BLOCKS):
        span = slice(r * chunk, (r + 1) * chunk)
        out_ref[span, :] = acc_ref[span, :] + dot(q_ref[span, :], wq_ref[:, cols], NT)


def last_kernel(total, acc_ref, c_ref, wq_ref, own_ref, got_ref, m_ref, *rest):
    parts, outs, (q_ref, gp_ref, g_ref, sems) = rest[:4], rest[-8:-4], rest[-4:]
    rows, width = c_ref.shape
    rb, cb = m_ref.shape
    ns, nx = lax.axis_size("sub"), lax.axis_size("mp")
    s, x = lax.axis_index("sub"), lax.axis_index("mp")
    other = 1 - s
    cols = half_columns(other, width)
    low_own, low_got = state_low(total, own_ref), state_low(total, got_ref)
    q_ref[...] = dot(c_ref[:, cols], unpack(low_got).astype(BF16), NT).astype(BF16)
    copies = []
    for i in range(2):
        kept_ref, got_part = parts[2 * i], parts[2 * i + 1]
        g_ref[1 + i] = (kept_ref[...] + got_part[:rb, :]) / total
        copies.append(pltpu.make_async_copy(g_ref.at[1 + i], outs[2 + i], sems.at[1 + i]))
        copies[-1].start()
    chunk = rows // BLOCKS
    for r in range(BLOCKS):
        span = slice(r * chunk, (r + 1) * chunk)
        gp_ref[span, :] = (acc_ref[span, :] + dot(q_ref[span, :], wq_ref[:, cols], NT)).astype(BF16)
        copies.append(pltpu.make_async_copy(gp_ref.at[span, :], outs[0].at[span, :], sems.at[3 + r]))
        copies[-1].start()
    whole = jnp.concatenate([jnp.where(s == g, low_own, low_got) for g in range(ns)], axis=1)
    high, rest_ = split(m_ref[...])
    third = (m_ref[...] - high.astype(F32) - rest_.astype(F32)).astype(BF16)
    for xb in range(nx):

        @pl.when(x == xb)
        def _():
            state = unpack(whole[:, xb * cb : (xb + 1) * cb]).astype(BF16)
            g_ref[0] = (dot(high, state, NT) + dot(rest_, state, NT) + dot(third, state, NT)) / total

    copies.append(pltpu.make_async_copy(g_ref.at[0], outs[1], sems.at[0]))
    copies[-1].start()
    for copy in copies:
        copy.wait()


def step_kernel(arrived, tailed, *refs):
    kept_ref, send_ref, keep_ref = refs[0], refs[-2], refs[-1]
    count, size = keep_ref.shape[0], keep_ref.shape[1]

    def block(i):
        return kept_ref[i] + refs[1][i * size : (i + 1) * size, :] if arrived else kept_ref[i]

    for i in range(count):
        keep_ref[i] = block(2 * i)
        send_ref[i * size : (i + 1) * size, :] = block(2 * i + 1)
    if tailed:
        send_ref[count * size :, :] = refs[1 + arrived][...]


def call(kernel, name, out_shape, inputs, specs, after=(), scratch=(), us=1.0, outs=None):
    us = US.get(name, us)
    inputs, specs = list(inputs) + list(after), list(specs) + [ANY] * len(after)
    return pl.pallas_call(
        kernel,
        out_shape=out_shape,
        in_specs=specs,
        out_specs=outs or (VMEM,) * len(out_shape),
        scratch_shapes=scratch,
        compiler_params=PARAMS,
        cost_estimate=pl.CostEstimate(flops=int(us * 1.1e9), bytes_accessed=int(us * 1e5), transcendentals=0),
        name=name,
    )(*inputs)


def swap_cores(value):
    return lax.ppermute(value, "sub", [(i, i ^ 1) for i in range(lax.axis_size("sub"))])


def swap(value, exchanges):
    nz, nx, ns = lax.axis_size("points"), lax.axis_size("mp"), lax.axis_size("sub")
    pairs = []
    for z in range(nz):
        for x in range(nx):
            for s, (axis, bit) in enumerate(exchanges):
                to = (z ^ bit, x) if axis == "points" else (z, x ^ bit)
                pairs.append(((z * nx + x) * ns + s, (to[0] * nx + to[1]) * ns + s))
    return lax.ppermute(value, ("points", "mp", "sub"), pairs)


def sum_kernel(a_ref, b_ref, *rest):
    rest[-1][...] = a_ref[...] + b_ref[: a_ref.shape[0], :]


class Total:
    def __init__(self, parts):
        self.value, self.got, self.done = parts[0], swap_cores(parts[1]), 0
        self.todo = list(zip(*routes("state")))

    def add(self, after=()):
        (self.value,) = call(
            sum_kernel,
            "sum_%d" % self.done,
            (jax.ShapeDtypeStruct(self.value.shape, F32),),
            (self.value, self.got),
            [VMEM] * 2,
            after=after,
            us=0.1,
        )
        self.sent = self.value
        self.done += 1
        if self.todo:
            self.got = swap(self.value, self.todo.pop(0))
            return True
        self.got = swap_cores(self.value)
        return False


class Tail:
    def __init__(self, value):
        self.value, self.got = value, None
        self.todo = [list(route) for route in routes("state")]

    def takes(self, exchanges):
        return all(one in todo for one, todo in zip(exchanges, self.todo))

    def add(self, after=()):
        if self.got is not None:
            (self.value,) = call(
                sum_kernel,
                "sum_state",
                (jax.ShapeDtypeStruct(self.value.shape, F32),),
                (self.value, self.got.reshape(self.value.shape)),
                [VMEM] * 2,
                after=after,
                us=0.1,
            )
        return self.value

    def sent(self, exchanges, got):
        self.got = got
        for one, todo in zip(exchanges, self.todo):
            todo.remove(one)

    def step(self, after=()):
        self.add(after)
        exchanges = [todo[0] for todo in self.todo]
        self.sent(exchanges, swap(self.value, exchanges))


class Scatter:
    def __init__(self, blocks, name):
        self.name, self.done = name, 0
        self.kept, self.got = blocks[0], swap_cores(blocks[1])
        self.todo = list(zip(*routes(name)))

    def step(self, after=(), tail=None):
        exchanges = self.todo.pop(0)
        blocks, rb, cb = self.kept.shape
        got = () if self.got is None else (self.got.reshape(-1, cb),)
        count = blocks // 2
        tailed = tail is not None and tail.takes(exchanges)
        extra = (tail.add().reshape(-1, cb),) if tailed else ()
        rows = count * rb
        shape = jax.ShapeDtypeStruct
        self.sent, self.kept = call(
            functools.partial(step_kernel, len(got), tailed),
            "add_%s_%d" % (self.name, self.done),
            (shape((rows + (extra[0].shape[0] if tailed else 0), cb), F32), shape((count, rb, cb), F32)),
            (self.kept,) + got + extra,
            [VMEM] * (1 + len(got) + tailed),
            after=after,
            us=0.2,
        )
        self.got = swap(self.sent, exchanges)
        if tailed:
            tail.sent(exchanges, self.got[rows:])
        self.done += 1

    def settle(self):
        blocks, rb, cb = self.kept.shape
        (summed,) = call(
            sum_kernel,
            "settle_" + self.name,
            (jax.ShapeDtypeStruct((blocks * rb, cb), F32),),
            (self.kept.reshape(blocks * rb, cb), self.got.reshape(-1, cb)),
            [VMEM] * 2,
            us=0.1,
        )
        self.kept, self.got = summed.reshape(blocks, rb, cb), None
        self.sent = summed

    def end(self, after=()):
        _, rb, cb = self.kept.shape
        (total,) = call(
            sum_kernel,
            "end_" + self.name,
            (jax.ShapeDtypeStruct((rb, cb), F32),),
            (self.kept.reshape(rb, cb), self.got),
            [VMEM] * 2,
            after=after,
            us=0.1,
        )
        return total


def local(points_in, cotangent, w_query, w_key, w_value):
    rows, width = points_in.shape
    nz, nx, ns = lax.axis_size("points"), lax.axis_size("mp"), lax.axis_size("sub")
    total = rows * nz * nx * ns
    half = width // ns
    rb, cb = width // (nz * ns), width // nx
    shape = jax.ShapeDtypeStruct
    dealt = shape((ns, nz * nx, rb, cb), F32)
    state = shape((ns, HS, half), F32)
    low = shape((rows, width), BF16)
    tall = shape((rows, half), F32)

    sums, grad_part, p_in, p_flip = call(
        cross_kernel,
        "cross",
        (shape((width, width), F32), state, low, shape((width, rows), BF16)),
        [pltpu.with_memory_space_constraint(a, pltpu.HBM) for a in (points_in, cotangent, w_query)],
        [HBM] * 3,
        scratch=[
            pltpu.VMEM((rows, width), BF16),
            pltpu.VMEM((width, width), BF16),
            pltpu.SemaphoreType.DMA((2 * CHUNKS + 1,)),
        ],
        us=3.0,
    )
    g_sum = Total(grad_part)
    (cross,) = call(deal_kernel, "deal", (dealt,), (sums,), [VMEM], us=0.3)
    cross_sum = Scatter(cross, "query")
    g_sum.add()
    cross_sum.step(after=(g_sum.sent,))
    g_sum.add(after=(cross_sum.sent,))
    norms, states = [], []
    for other in range(ns):
        norms.append(
            call(
                functools.partial(norm_kernel, other),
                "norm",
                (tall, tall, tall, tall, shape((HS, half), F32)),
                [p_in, w_key, w_value],
                [VMEM] * 3,
                after=(g_sum.sent, cross_sum.sent),
                scratch=[pltpu.VMEM((2, rows, half), F32), pltpu.VMEM((2, rows, half), BF16)],
                us=2.3,
            )
        )
        states.append(norms[-1][-1])
        g_sum.add(after=(states[-1],))
        if other == 0:
            cross_sum.step(after=(g_sum.sent,))
    while g_sum.todo:
        g_sum.add()
    g_own, g_got = g_sum.value, g_sum.got
    key_norm, key_inv, value_norm, value_inv, _ = zip(*norms)
    tail = Tail(states[0] + swap_cores(states[1]))
    cross_sum.settle()

    scratch = [pltpu.VMEM((rows, half), F32), pltpu.VMEM((rows, half), BF16)]

    scratch = [pltpu.VMEM((rows, half), F32), pltpu.VMEM((rows, half), BF16)]
    short, column = shape((rows, half), BF16), shape((width, half), F32)
    k_own, v_own, wk_own, wv_own = call(
        functools.partial(own_kernel, total),
        "back_own",
        (short, short, column, column),
        (p_flip, g_own, key_norm[0], key_inv[0], value_norm[0], value_inv[0]),
        [VMEM] * 6,
        scratch=[scratch[0]] * 2 + [scratch[1]] * 2,
        us=1.8,
    )

    def back(key, part, after):
        return call(
            functools.partial(other_kernel, total, key),
            "back_key" if key else "back_value",
            (short, dealt),
            (p_flip, part, g_got) + ((key_norm[1], key_inv[1], value_norm[1]) if key else (value_norm[1], value_inv[1], key_norm[1])),
            [VMEM] * 6,
            after=after,
            scratch=scratch,
            us=1.0,
        )

    k_other, key_blocks = back(True, wk_own, (cross_sum.sent,))
    key_sum = Scatter(key_blocks, "key")
    v_other, value_blocks = back(False, wv_own, (k_other,))
    value_sum = Scatter(value_blocks, "value")
    key_low, value_low = (k_own, k_other), (v_own, v_other)
    last = v_other
    m_total, s_own = None, None
    for turn in ORDER:
        if turn == "P":
            (partial,) = call(
                points_kernel,
                "grad_points_part",
                (shape((rows, width), F32),),
                key_low + value_low + (w_key, w_value),
                [VMEM] * 6,
                after=(last,),
                us=1.3,
            )
            last = partial
        elif turn == "T":
            if not cross_sum.todo:
                m_total = last = cross_sum.end(after=(last,))
        elif turn == "S":
            if tail.todo[0]:
                tail.step(after=(last,))
            else:
                s_own = tail.add(after=(last,))
            last = tail.value
        else:
            one = {"M": cross_sum, "K": key_sum, "V": value_sum}[turn.upper()]
            one.step(after=(last,), tail=tail if turn.islower() else None)
            last = one.sent
    while cross_sum.todo or key_sum.todo or value_sum.todo:
        for turn in (cross_sum, key_sum, value_sum):
            if turn.todo:
                turn.step()
    if m_total is None:
        m_total = cross_sum.end()
    while tail.todo[0]:
        tail.step()
    if s_own is None:
        s_own = tail.add()
    s_got = swap_cores(s_own)
    (partial,) = call(
        functools.partial(query_own_kernel, total),
        "grad_points_own",
        (shape((rows, width), F32),),
        (partial, cotangent, w_query, s_own),
        [VMEM] * 4,
        scratch=[pltpu.VMEM((rows, half), BF16)],
        us=1.0,
    )
    parts = []
    for one in (key_sum, value_sum):
        parts += [one.kept.reshape(rb, cb), one.got]
    block = shape((rb, cb), F32)
    return call(
        functools.partial(last_kernel, total),
        "outputs",
        (low, block, block, block),
        [partial, cotangent, w_query, s_own, s_got, m_total] + parts,
        [VMEM] * 10,
        scratch=[
            pltpu.VMEM((rows, half), BF16),
            pltpu.VMEM((rows, width), BF16),
            pltpu.VMEM((3, rb, cb), F32),
            pltpu.SemaphoreType.DMA((3 + BLOCKS,)),
        ],
        us=0.01,
        outs=(HBM,) * 4,
    )


def solution(mesh):
    whole = P(("groups", "points", "mp", "sub"), None)
    block = P(("groups", "points", "sub"), "mp")
    return jax.shard_map(
        local,
        mesh=mesh,
        in_specs=(whole, whole, P(), P(), P()),
        out_specs=(whole, block, block, block),
        check_vma=False,
    )
```

```python
import functools

import jax
import jax.numpy as jnp
from jax import lax
from jax.experimental import pallas as pl
from jax.experimental.pallas import tpu as pltpu
from jax.sharding import PartitionSpec as P

HS = 32
F32 = jnp.float32
BF16 = jnp.bfloat16
NT = (((1,), (1,)), ((), ()))
TN = (((0,), (0,)), ((), ()))
NN = (((1,), (0,)), ((), ()))
VMEM = pl.BlockSpec(memory_space=pltpu.VMEM)
HBM = pl.BlockSpec(memory_space=pltpu.HBM)
ANY = pl.BlockSpec(memory_space=pl.ANY)
CHUNKS = 2
BLOCKS = 4
NORM_BLOCKS = 1
EARLY_Z = ("state", "value")
ORDER = "kVMPkVTKSVS"
US = {"end_query": 2.0, "grad_points": 0.01, "back_own": 0.01, "add_key_0": 5.0, "sum_0": 5.0, "back_key": 5.0, "back_value": 5.0}

PARAMS = pltpu.CompilerParams(vmem_limit_bytes=16 * 1024 * 1024)


def dot(a, b, dims):
    return lax.dot_general(a, b, dims, preferred_element_type=F32)


def split(x):
    high = x.astype(BF16)
    return high, (x - high.astype(F32)).astype(BF16)


def head_mask(size):
    rows = lax.broadcasted_iota(jnp.int32, (size, size), 0) // HS
    cols = lax.broadcasted_iota(jnp.int32, (size, size), 1) // HS
    return rows == cols


def averager(size):
    return jnp.where(head_mask(size), F32(1.0 / HS), F32(0.0)).astype(BF16)


def pack(full):
    size = full.shape[0]
    kept = jnp.where(head_mask(size), full, F32(0.0))
    total = kept[:HS]
    for i in range(1, size // HS):
        total = total + kept[i * HS : (i + 1) * HS]
    return total


def unpack(packed):
    size = packed.shape[1]
    tiled = jnp.concatenate([packed] * (size // HS), axis=0)
    return jnp.where(head_mask(size), tiled, F32(0.0))


def bits(axis):
    bit = 1
    while bit < lax.axis_size(axis):
        yield axis, bit
        bit *= 2


def routes(name):
    x, z = list(bits("mp")), list(bits("points"))
    if name in EARLY_Z:
        return x + z, z + x
    return x + z, z[:1] + x + z[1:]


def place(refs, value, g, name):
    z, x, s = lax.axis_index("points"), lax.axis_index("mp"), lax.axis_index("sub")
    nz, nx, ns = lax.axis_size("points"), lax.axis_size("mp"), lax.axis_size("sub")
    rb, cb = refs.shape[-2:]
    count = value.shape[1] // cb
    for zb in range(nz):
        for sb in range(ns):
            row = (zb * ns + sb) * rb
            for j in range(count):
                away = {"points": z ^ zb, "mp": x ^ (g * count + j)}
                spot = 0
                for t, (axis, bit) in enumerate(routes(name)[sb]):
                    spot = spot + jnp.where((away[axis] & bit) != 0, 1 << t, 0)
                refs[s ^ sb, spot] = value[row : row + rb, j * cb : (j + 1) * cb]


def half_columns(g, width):
    half = width // lax.axis_size("sub")
    return pl.ds(pl.multiple_of(g * half, half), half)


def cross_kernel(p_hbm, c_hbm, wq_hbm, sums, g_ref, p_ref, pt_ref, c_ref, wq_ref, sems):
    rows, width = p_hbm.shape
    ns = lax.axis_size("sub")
    s = lax.axis_index("sub")
    half = width // ns
    chunk = rows // CHUNKS
    spans = [slice(r * chunk, (r + 1) * chunk) for r in range(CHUNKS)]
    loads = []
    for r, span in enumerate(spans):
        for k, (src, dst) in enumerate(((p_hbm, p_ref), (c_hbm, c_ref))):
            loads.append(pltpu.make_async_copy(src.at[span, :], dst.at[span, :], sems.at[2 * r + k]))
    loads.append(pltpu.make_async_copy(wq_hbm, wq_ref, sems.at[2 * CHUNKS]))
    for load in loads:
        load.start()
    for r, span in enumerate(spans):
        loads[2 * r].wait()
        flipped = p_ref[span, :].T
        pt_ref[:, span] = flipped
        loads[2 * r + 1].wait()
        for g in range(ns):
            cols = slice(g * half, (g + 1) * half)
            part = dot(flipped, c_ref[span, cols], NN)
            sums[:, cols] = part if r == 0 else sums[:, cols] + part
    loads[-1].wait()
    for g in range(ns):
        cols = slice(g * half, (g + 1) * half)
        high, low = split(sums[:, cols])
        wq = wq_ref[:, cols]
        g_ref[s ^ g] = pack(dot(wq, high, TN) + dot(wq, low, TN))


def deal_kernel(sums_ref, *rest):
    half = sums_ref.shape[1] // lax.axis_size("sub")
    for g in range(lax.axis_size("sub")):
        place(rest[-1], sums_ref[:, g * half : (g + 1) * half], g, "query")


def norm_kernel(other, p_ref, wk_ref, wv_ref, *rest):
    kn_ref, kr_ref, vn_ref, vr_ref, s_ref, c_ref, sq_ref = rest[-7:]
    rows, width = p_ref.shape
    cols = half_columns(lax.axis_index("sub") ^ other, width)
    mean = averager(width // lax.axis_size("sub"))
    chunk = rows // NORM_BLOCKS
    spans = [slice(r * chunk, (r + 1) * chunk) for r in range(NORM_BLOCKS)]
    for w, w_ref in enumerate((wk_ref, wv_ref)):
        raw = w_ref[:, cols]
        high, low = split(raw.astype(F32) - dot(raw, mean, NN))
        for span in spans:
            p = p_ref[span, :]
            centred = dot(p, high, NN) + dot(p, low, NN)
            c_ref[w, span, :] = centred
            sq_ref[w, span, :] = (centred * centred).astype(BF16)
    for w, (n_ref, r_ref) in enumerate(((kn_ref, kr_ref), (vn_ref, vr_ref))):
        for span in spans:
            inverse = lax.rsqrt(dot(sq_ref[w, span, :], mean, NN) + 1e-05)
            n_ref[span, :] = c_ref[w, span, :] * inverse
            r_ref[span, :] = inverse
    s_ref[...] = pack(dot(kn_ref[...].astype(BF16), vn_ref[...].astype(BF16), TN))


def back_centre(total, key, g_ref):
    full = unpack((g_ref[...] / total).astype(BF16).astype(F32))
    mean = averager(full.shape[0])
    grouped = dot(mean, full.astype(BF16), NN) if key else dot(full.astype(BF16), mean, NN)
    return split(full - grouped)


def back_halves(total, keys, g_ref, sets, gl_refs, grad_refs, prod_refs):
    rows, half = gl_refs[0].shape
    mean = averager(half)
    chunk = rows // BLOCKS
    spans = [slice(r * chunk, (r + 1) * chunk) for r in range(BLOCKS)]
    centred = [back_centre(total, key, g_ref) for key in keys]
    for key, (high, small), (n_ref, r_ref, o_ref), grad_ref, prod_ref in zip(keys, centred, sets, grad_refs, prod_refs):
        dims = NT if key else NN
        for span in spans:
            low = o_ref[span, :].astype(BF16)
            grad = dot(low, high, dims) + dot(low, small, dims)
            grad_ref[span, :] = grad
            prod_ref[span, :] = (grad * n_ref[span, :]).astype(BF16)
    for (n_ref, r_ref, o_ref), gl_ref, grad_ref, prod_ref in zip(sets, gl_refs, grad_refs, prod_refs):
        for span in spans:
            second = dot(prod_ref[span, :], mean, NN)
            gl_ref[span, :] = ((grad_ref[span, :] - n_ref[span, :] * second) * r_ref[span, :]).astype(BF16)


def own_kernel(total, pt_ref, g_ref, kn_ref, kr_ref, vn_ref, vr_ref, *rest):
    gk_ref, gv_ref, wk_ref, wv_ref, kgrad_ref, vgrad_ref, kprod_ref, vprod_ref = rest[-8:]
    sets = ((kn_ref, kr_ref, vn_ref), (vn_ref, vr_ref, kn_ref))
    back_halves(total, (True, False), g_ref, sets, (gk_ref, gv_ref), (kgrad_ref, vgrad_ref), (kprod_ref, vprod_ref))
    wk_ref[...] = dot(pt_ref[...], gk_ref[...], NN)
    wv_ref[...] = dot(pt_ref[...], gv_ref[...], NN)


def other_kernel(total, key, pt_ref, own_ref, g_ref, n_ref, r_ref, o_ref, *rest):
    gl_ref, w_ref, grad_ref, prod_ref = rest[-4:]
    s = lax.axis_index("sub")
    back_halves(total, (key,), g_ref, ((n_ref, r_ref, o_ref),), (gl_ref,), (grad_ref,), (prod_ref,))
    name = "key" if key else "value"
    place(w_ref, own_ref[...], s, name)
    place(w_ref, dot(pt_ref[...], gl_ref[...], NN), 1 - s, name)


def points_kernel(*refs):
    acc_ref = refs[-1]
    rows, width = acc_ref.shape
    s = lax.axis_index("sub")
    chunk = rows // BLOCKS
    for r in range(BLOCKS):
        span = slice(r * chunk, (r + 1) * chunk)
        total = None
        for w_ref, halves in ((refs[4], refs[:2]), (refs[5], refs[2:4])):
            for other, gl_ref in enumerate(halves):
                part = dot(gl_ref[span, :], w_ref[:, half_columns(s ^ other, width)], NT)
                total = part if total is None else total + part
        acc_ref[span, :] = total


def state_low(total, ref):
    return (ref[...] / total).astype(BF16).astype(F32)


def query_own_kernel(total, acc_ref, c_ref, wq_ref, own_ref, *rest):
    out_ref, q_ref = rest[-2:]
    rows, width = c_ref.shape
    cols = half_columns(lax.axis_index("sub"), width)
    q_ref[...] = dot(c_ref[:, cols], unpack(state_low(total, own_ref)).astype(BF16), NT).astype(BF16)
    chunk = rows // BLOCKS
    for r in range(BLOCKS):
        span = slice(r * chunk, (r + 1) * chunk)
        out_ref[span, :] = acc_ref[span, :] + dot(q_ref[span, :], wq_ref[:, cols], NT)


def last_kernel(total, acc_ref, c_ref, wq_ref, own_ref, got_ref, m_ref, *rest):
    kept_ref, got_part, outs, (q_ref, gp_ref, g_ref, sems) = rest[0], rest[1], rest[-7:-4], rest[-4:]
    rows, width = c_ref.shape
    rb, cb = m_ref.shape
    ns, nx = lax.axis_size("sub"), lax.axis_size("mp")
    s, x = lax.axis_index("sub"), lax.axis_index("mp")
    other = 1 - s
    cols = half_columns(other, width)
    low_own, low_got = state_low(total, own_ref), state_low(total, got_ref)
    q_ref[...] = dot(c_ref[:, cols], unpack(low_got).astype(BF16), NT).astype(BF16)
    g_ref[1] = (kept_ref[...] + got_part[:rb, :]) / total
    copies = [pltpu.make_async_copy(g_ref.at[1], outs[2], sems.at[1])]
    copies[0].start()
    chunk = rows // BLOCKS
    for r in range(BLOCKS):
        span = slice(r * chunk, (r + 1) * chunk)
        gp_ref[span, :] = (acc_ref[span, :] + dot(q_ref[span, :], wq_ref[:, cols], NT)).astype(BF16)
        copies.append(pltpu.make_async_copy(gp_ref.at[span, :], outs[0].at[span, :], sems.at[2 + r]))
        copies[-1].start()
    whole = jnp.concatenate([jnp.where(s == g, low_own, low_got) for g in range(ns)], axis=1)
    high, rest_ = split(m_ref[...])
    third = (m_ref[...] - high.astype(F32) - rest_.astype(F32)).astype(BF16)
    mine = whole[:, :cb]
    for xb in range(1, nx):
        mine = jnp.where(x == xb, whole[:, xb * cb : (xb + 1) * cb], mine)
    state = unpack(mine).astype(BF16)
    g_ref[0] = (dot(high, state, NT) + dot(rest_, state, NT) + dot(third, state, NT)) / total
    copies.append(pltpu.make_async_copy(g_ref.at[0], outs[1], sems.at[0]))
    copies[-1].start()
    for copy in copies:
        copy.wait()


def step_kernel(arrived, tailed, *refs):
    kept_ref, send_ref, keep_ref = refs[0], refs[-2], refs[-1]
    count, size = keep_ref.shape[0], keep_ref.shape[1]

    def block(i):
        return kept_ref[i] + refs[1][i * size : (i + 1) * size, :] if arrived else kept_ref[i]

    for i in range(count):
        keep_ref[i] = block(2 * i)
        send_ref[i * size : (i + 1) * size, :] = block(2 * i + 1)
    if tailed:
        send_ref[count * size :, :] = refs[1 + arrived][...]


def call(kernel, name, out_shape, inputs, specs, after=(), scratch=(), us=1.0, outs=None):
    us = US.get(name, us)
    inputs, specs = list(inputs) + list(after), list(specs) + [ANY] * len(after)
    return pl.pallas_call(
        kernel,
        out_shape=out_shape,
        in_specs=specs,
        out_specs=outs or (VMEM,) * len(out_shape),
        scratch_shapes=scratch,
        compiler_params=PARAMS,
        cost_estimate=pl.CostEstimate(flops=int(us * 1.1e9), bytes_accessed=int(us * 1e5), transcendentals=0),
        name=name,
    )(*inputs)


def swap_cores(value):
    return lax.ppermute(value, "sub", [(i, i ^ 1) for i in range(lax.axis_size("sub"))])


def swap(value, exchanges):
    nz, nx, ns = lax.axis_size("points"), lax.axis_size("mp"), lax.axis_size("sub")
    pairs = []
    for z in range(nz):
        for x in range(nx):
            for s, (axis, bit) in enumerate(exchanges):
                to = (z ^ bit, x) if axis == "points" else (z, x ^ bit)
                pairs.append(((z * nx + x) * ns + s, (to[0] * nx + to[1]) * ns + s))
    return lax.ppermute(value, ("points", "mp", "sub"), pairs)


def sum_kernel(a_ref, b_ref, *rest):
    rest[-1][...] = a_ref[...] + b_ref[: a_ref.shape[0], :]


def value_out_kernel(total, kept_ref, got_ref, *rest):
    rest[-1][...] = (kept_ref[...] + got_ref[...]) / total


class Total:
    def __init__(self, parts):
        self.value, self.got, self.done = parts[0], swap_cores(parts[1]), 0
        self.todo = list(zip(*routes("state")))

    def add(self, after=()):
        (self.value,) = call(
            sum_kernel,
            "sum_%d" % self.done,
            (jax.ShapeDtypeStruct(self.value.shape, F32),),
            (self.value, self.got),
            [VMEM] * 2,
            after=after,
            us=0.1,
        )
        self.sent = self.value
        self.done += 1
        if self.todo:
            self.got = swap(self.value, self.todo.pop(0))
            return True
        self.got = swap_cores(self.value)
        return False


class Tail:
    def __init__(self, value):
        self.value, self.got = value, None
        self.todo = [list(route) for route in routes("state")]

    def takes(self, exchanges):
        return all(one in todo for one, todo in zip(exchanges, self.todo))

    def add(self, after=()):
        if self.got is not None:
            (self.value,) = call(
                sum_kernel,
                "sum_state",
                (jax.ShapeDtypeStruct(self.value.shape, F32),),
                (self.value, self.got.reshape(self.value.shape)),
                [VMEM] * 2,
                after=after,
                us=0.1,
            )
        return self.value

    def sent(self, exchanges, got):
        self.got = got
        for one, todo in zip(exchanges, self.todo):
            todo.remove(one)

    def step(self, after=()):
        self.add(after)
        exchanges = [todo[0] for todo in self.todo]
        self.sent(exchanges, swap(self.value, exchanges))


class Scatter:
    def __init__(self, blocks, name):
        self.name, self.done = name, 0
        self.kept, self.got = blocks[0], swap_cores(blocks[1])
        self.todo = list(zip(*routes(name)))

    def step(self, after=(), tail=None):
        exchanges = self.todo.pop(0)
        blocks, rb, cb = self.kept.shape
        got = () if self.got is None else (self.got.reshape(-1, cb),)
        count = blocks // 2
        tailed = tail is not None and tail.takes(exchanges)
        extra = (tail.add().reshape(-1, cb),) if tailed else ()
        rows = count * rb
        shape = jax.ShapeDtypeStruct
        self.sent, self.kept = call(
            functools.partial(step_kernel, len(got), tailed),
            "add_%s_%d" % (self.name, self.done),
            (shape((rows + (extra[0].shape[0] if tailed else 0), cb), F32), shape((count, rb, cb), F32)),
            (self.kept,) + got + extra,
            [VMEM] * (1 + len(got) + tailed),
            after=after,
            us=0.2,
        )
        self.got = swap(self.sent, exchanges)
        if tailed:
            tail.sent(exchanges, self.got[rows:])
        self.done += 1

    def settle(self):
        blocks, rb, cb = self.kept.shape
        (summed,) = call(
            sum_kernel,
            "settle_" + self.name,
            (jax.ShapeDtypeStruct((blocks * rb, cb), F32),),
            (self.kept.reshape(blocks * rb, cb), self.got.reshape(-1, cb)),
            [VMEM] * 2,
            us=0.1,
        )
        self.kept, self.got = summed.reshape(blocks, rb, cb), None
        self.sent = summed

    def end(self, after=()):
        _, rb, cb = self.kept.shape
        (total,) = call(
            sum_kernel,
            "end_" + self.name,
            (jax.ShapeDtypeStruct((rb, cb), F32),),
            (self.kept.reshape(rb, cb), self.got),
            [VMEM] * 2,
            after=after,
            us=0.1,
        )
        return total


def local(points_in, cotangent, w_query, w_key, w_value):
    rows, width = points_in.shape
    nz, nx, ns = lax.axis_size("points"), lax.axis_size("mp"), lax.axis_size("sub")
    total = rows * nz * nx * ns
    half = width // ns
    rb, cb = width // (nz * ns), width // nx
    shape = jax.ShapeDtypeStruct
    dealt = shape((ns, nz * nx, rb, cb), F32)
    state = shape((ns, HS, half), F32)
    low = shape((rows, width), BF16)
    tall = shape((rows, half), F32)

    sums, grad_part, p_in, p_flip = call(
        cross_kernel,
        "cross",
        (shape((width, width), F32), state, low, shape((width, rows), BF16)),
        [pltpu.with_memory_space_constraint(a, pltpu.HBM) for a in (points_in, cotangent, w_query)],
        [HBM] * 3,
        scratch=[
            pltpu.VMEM((rows, width), BF16),
            pltpu.VMEM((width, width), BF16),
            pltpu.SemaphoreType.DMA((2 * CHUNKS + 1,)),
        ],
        us=3.0,
    )
    g_sum = Total(grad_part)
    (cross,) = call(deal_kernel, "deal", (dealt,), (sums,), [VMEM], us=0.3)
    cross_sum = Scatter(cross, "query")
    g_sum.add()
    cross_sum.step(after=(g_sum.sent,))
    g_sum.add(after=(cross_sum.sent,))
    norms, states = [], []
    for other in range(ns):
        norms.append(
            call(
                functools.partial(norm_kernel, other),
                "norm",
                (tall, tall, tall, tall, shape((HS, half), F32)),
                [p_in, w_key, w_value],
                [VMEM] * 3,
                after=(g_sum.sent, cross_sum.sent),
                scratch=[pltpu.VMEM((2, rows, half), F32), pltpu.VMEM((2, rows, half), BF16)],
                us=2.3,
            )
        )
        states.append(norms[-1][-1])
        g_sum.add(after=(states[-1],))
        if other == 0:
            cross_sum.step(after=(g_sum.sent,))
    while g_sum.todo:
        g_sum.add()
    g_own, g_got = g_sum.value, g_sum.got
    key_norm, key_inv, value_norm, value_inv, _ = zip(*norms)
    tail = Tail(states[0] + swap_cores(states[1]))
    cross_sum.settle()

    scratch = [pltpu.VMEM((rows, half), F32), pltpu.VMEM((rows, half), BF16)]

    scratch = [pltpu.VMEM((rows, half), F32), pltpu.VMEM((rows, half), BF16)]
    short, column = shape((rows, half), BF16), shape((width, half), F32)
    k_own, v_own, wk_own, wv_own = call(
        functools.partial(own_kernel, total),
        "back_own",
        (short, short, column, column),
        (p_flip, g_own, key_norm[0], key_inv[0], value_norm[0], value_inv[0]),
        [VMEM] * 6,
        scratch=[scratch[0]] * 2 + [scratch[1]] * 2,
        us=1.8,
    )

    def back(key, part, after):
        return call(
            functools.partial(other_kernel, total, key),
            "back_key" if key else "back_value",
            (short, dealt),
            (p_flip, part, g_got) + ((key_norm[1], key_inv[1], value_norm[1]) if key else (value_norm[1], value_inv[1], key_norm[1])),
            [VMEM] * 6,
            after=after,
            scratch=scratch,
            us=1.0,
        )

    k_other, key_blocks = back(True, wk_own, (cross_sum.sent,))
    key_sum = Scatter(key_blocks, "key")
    v_other, value_blocks = back(False, wv_own, (k_other,))
    value_sum = Scatter(value_blocks, "value")
    key_low, value_low = (k_own, k_other), (v_own, v_other)
    last = v_other
    m_total, s_own = None, None
    for turn in ORDER:
        if turn == "P":
            (partial,) = call(
                points_kernel,
                "grad_points_part",
                (shape((rows, width), F32),),
                key_low + value_low + (w_key, w_value),
                [VMEM] * 6,
                after=(last,),
                us=1.3,
            )
            last = partial
        elif turn == "T":
            if not cross_sum.todo:
                m_total = last = cross_sum.end(after=(last,))
        elif turn == "S":
            if tail.todo[0]:
                tail.step(after=(last,))
            else:
                s_own = tail.add(after=(last,))
            last = tail.value
        else:
            one = {"M": cross_sum, "K": key_sum, "V": value_sum}[turn.upper()]
            one.step(after=(last,), tail=tail if turn.islower() else None)
            last = one.sent
    while cross_sum.todo or key_sum.todo or value_sum.todo:
        for turn in (cross_sum, key_sum, value_sum):
            if turn.todo:
                turn.step()
    if m_total is None:
        m_total = cross_sum.end()
    while tail.todo[0]:
        tail.step()
    if s_own is None:
        s_own = tail.add()
    s_got = swap_cores(s_own)
    (partial,) = call(
        functools.partial(query_own_kernel, total),
        "grad_points_own",
        (shape((rows, width), F32),),
        (partial, cotangent, w_query, s_own),
        [VMEM] * 4,
        scratch=[pltpu.VMEM((rows, half), BF16)],
        us=1.0,
    )
    block = shape((rb, cb), F32)
    grad_points, grad_query, grad_key = call(
        functools.partial(last_kernel, total),
        "outputs",
        (low, block, block),
        [partial, cotangent, w_query, s_own, s_got, m_total, key_sum.kept.reshape(rb, cb), key_sum.got],
        [VMEM] * 8,
        scratch=[
            pltpu.VMEM((rows, half), BF16),
            pltpu.VMEM((rows, width), BF16),
            pltpu.VMEM((2, rb, cb), F32),
            pltpu.SemaphoreType.DMA((2 + BLOCKS,)),
        ],
        us=0.01,
        outs=(HBM,) * 3,
    )
    (grad_value,) = call(
        functools.partial(value_out_kernel, total),
        "value_out",
        (block,),
        (value_sum.kept.reshape(rb, cb), value_sum.got, pltpu.with_memory_space_constraint(grad_query, pltpu.HBM)),
        [VMEM, VMEM, HBM],
        us=0.01,
    )
    return grad_points, grad_query, grad_key, grad_value


def solution(mesh):
    whole = P(("groups", "points", "mp", "sub"), None)
    block = P(("groups", "points", "sub"), "mp")
    return jax.shard_map(
        local,
        mesh=mesh,
        in_specs=(whole, whole, P(), P(), P()),
        out_specs=(whole, block, block, block),
        check_vma=False,
    )
```

```python
import functools

import jax
import jax.numpy as jnp
from jax import lax
from jax.experimental import pallas as pl
from jax.experimental.pallas import tpu as pltpu
from jax.sharding import PartitionSpec as P

HS = 32
F32 = jnp.float32
BF16 = jnp.bfloat16
NT = (((1,), (1,)), ((), ()))
TN = (((0,), (0,)), ((), ()))
NN = (((1,), (0,)), ((), ()))
VMEM = pl.BlockSpec(memory_space=pltpu.VMEM)
HBM = pl.BlockSpec(memory_space=pltpu.HBM)
ANY = pl.BlockSpec(memory_space=pl.ANY)
CHUNKS = 2
BLOCKS = 4
EARLY_Z = ("state", "value")
ORDER = "kVMPkVTKSVS"
US = {"end_query": 2.0, "grad_points": 0.01, "back_own": 0.01, "add_key_0": 5.0, "sum_0": 5.0, "back_key": 5.0, "back_value": 5.0}

PARAMS = pltpu.CompilerParams(vmem_limit_bytes=16 * 1024 * 1024)


def dot(a, b, dims):
    return lax.dot_general(a, b, dims, preferred_element_type=F32)


def split(x):
    high = x.astype(BF16)
    return high, (x - high.astype(F32)).astype(BF16)


def head_mask(size):
    rows = lax.broadcasted_iota(jnp.int32, (size, size), 0) // HS
    cols = lax.broadcasted_iota(jnp.int32, (size, size), 1) // HS
    return rows == cols


def averager(size):
    return jnp.where(head_mask(size), F32(1.0 / HS), F32(0.0)).astype(BF16)


def pack(full):
    size = full.shape[0]
    kept = jnp.where(head_mask(size), full, F32(0.0))
    total = kept[:HS]
    for i in range(1, size // HS):
        total = total + kept[i * HS : (i + 1) * HS]
    return total


def unpack(packed):
    size = packed.shape[1]
    tiled = jnp.concatenate([packed] * (size // HS), axis=0)
    return jnp.where(head_mask(size), tiled, F32(0.0))


def bits(axis):
    bit = 1
    while bit < lax.axis_size(axis):
        yield axis, bit
        bit *= 2


def routes(name):
    x, z = list(bits("mp")), list(bits("points"))
    if name in EARLY_Z:
        return x + z, z + x
    return x + z, z[:1] + x + z[1:]


def place(refs, value, g, name):
    z, x, s = lax.axis_index("points"), lax.axis_index("mp"), lax.axis_index("sub")
    nz, nx, ns = lax.axis_size("points"), lax.axis_size("mp"), lax.axis_size("sub")
    rb, cb = refs.shape[-2:]
    count = value.shape[1] // cb
    for zb in range(nz):
        for sb in range(ns):
            row = (zb * ns + sb) * rb
            for j in range(count):
                away = {"points": z ^ zb, "mp": x ^ (g * count + j)}
                spot = 0
                for t, (axis, bit) in enumerate(routes(name)[sb]):
                    spot = spot + jnp.where((away[axis] & bit) != 0, 1 << t, 0)
                refs[s ^ sb, spot] = value[row : row + rb, j * cb : (j + 1) * cb]


def half_columns(g, width):
    half = width // lax.axis_size("sub")
    return pl.ds(pl.multiple_of(g * half, half), half)


def cross_kernel(p_hbm, c_hbm, wq_hbm, sums, g_ref, p_ref, pt_ref, c_ref, wq_ref, sems):
    rows, width = p_hbm.shape
    ns = lax.axis_size("sub")
    s = lax.axis_index("sub")
    half = width // ns
    chunk = rows // CHUNKS
    spans = [slice(r * chunk, (r + 1) * chunk) for r in range(CHUNKS)]
    loads = []
    for r, span in enumerate(spans):
        for k, (src, dst) in enumerate(((p_hbm, p_ref), (c_hbm, c_ref))):
            loads.append(pltpu.make_async_copy(src.at[span, :], dst.at[span, :], sems.at[2 * r + k]))
    loads.append(pltpu.make_async_copy(wq_hbm, wq_ref, sems.at[2 * CHUNKS]))
    for load in loads:
        load.start()
    for r, span in enumerate(spans):
        loads[2 * r].wait()
        flipped = p_ref[span, :].T
        pt_ref[:, span] = flipped
        loads[2 * r + 1].wait()
        for g in range(ns):
            cols = slice(g * half, (g + 1) * half)
            part = dot(flipped, c_ref[span, cols], NN)
            sums[:, cols] = part if r == 0 else sums[:, cols] + part
    loads[-1].wait()
    for g in range(ns):
        cols = slice(g * half, (g + 1) * half)
        high, low = split(sums[:, cols])
        wq = wq_ref[:, cols]
        g_ref[s ^ g] = pack(dot(wq, high, TN) + dot(wq, low, TN))


def deal_kernel(sums_ref, *rest):
    half = sums_ref.shape[1] // lax.axis_size("sub")
    for g in range(lax.axis_size("sub")):
        place(rest[-1], sums_ref[:, g * half : (g + 1) * half], g, "query")


def centre_weights(raw):
    return split(raw.astype(F32) - dot(raw, averager(raw.shape[1]), NN))


def norm_kernel(other, p_ref, *rest):
    rows, width = p_ref.shape
    half = width // lax.axis_size("sub")
    mean = averager(half)
    c_ref, sq_ref = rest[-2:]
    if other:
        w_ref = rest[0]
        kn_ref, kr_ref, vn_ref, vr_ref, s_ref = rest[-7:-2]
        weights = [(w_ref[2 * w], w_ref[2 * w + 1]) for w in range(2)]
    else:
        kn_ref, kr_ref, vn_ref, vr_ref, s_ref, w_ref = rest[-8:-2]
        s = lax.axis_index("sub")
        weights = [centre_weights(ref[:, half_columns(s, width)]) for ref in rest[:2]]
    for w, (high, low) in enumerate(weights):
        p = p_ref[...]
        centred = dot(p, high, NN) + dot(p, low, NN)
        c_ref[w] = centred
        sq_ref[w] = (centred * centred).astype(BF16)
    for w, (n_ref, r_ref) in enumerate(((kn_ref, kr_ref), (vn_ref, vr_ref))):
        inverse = lax.rsqrt(dot(sq_ref[w], mean, NN) + 1e-05)
        n_ref[...] = c_ref[w] * inverse
        r_ref[...] = inverse
    s_ref[...] = pack(dot(kn_ref[...].astype(BF16), vn_ref[...].astype(BF16), TN))
    if not other:
        for w, ref in enumerate(rest[:2]):
            w_ref[2 * w], w_ref[2 * w + 1] = centre_weights(ref[:, half_columns(1 - s, width)])


def back_centre(total, key, g_ref):
    full = unpack((g_ref[...] / total).astype(BF16).astype(F32))
    mean = averager(full.shape[0])
    grouped = dot(mean, full.astype(BF16), NN) if key else dot(full.astype(BF16), mean, NN)
    return split(full - grouped)


def back_halves(total, keys, g_ref, sets, gl_refs, grad_refs, prod_refs):
    rows, half = gl_refs[0].shape
    mean = averager(half)
    chunk = rows // BLOCKS
    spans = [slice(r * chunk, (r + 1) * chunk) for r in range(BLOCKS)]
    centred = [back_centre(total, key, g_ref) for key in keys]
    for key, (high, small), (n_ref, r_ref, o_ref), grad_ref, prod_ref in zip(keys, centred, sets, grad_refs, prod_refs):
        dims = NT if key else NN
        for span in spans:
            low = o_ref[span, :].astype(BF16)
            grad = dot(low, high, dims) + dot(low, small, dims)
            grad_ref[span, :] = grad
            prod_ref[span, :] = (grad * n_ref[span, :]).astype(BF16)
    for (n_ref, r_ref, o_ref), gl_ref, grad_ref, prod_ref in zip(sets, gl_refs, grad_refs, prod_refs):
        for span in spans:
            second = dot(prod_ref[span, :], mean, NN)
            gl_ref[span, :] = ((grad_ref[span, :] - n_ref[span, :] * second) * r_ref[span, :]).astype(BF16)


def own_kernel(total, pt_ref, g_ref, kn_ref, kr_ref, vn_ref, vr_ref, *rest):
    gk_ref, gv_ref, wk_ref, wv_ref, kgrad_ref, vgrad_ref, kprod_ref, vprod_ref = rest[-8:]
    sets = ((kn_ref, kr_ref, vn_ref), (vn_ref, vr_ref, kn_ref))
    back_halves(total, (True, False), g_ref, sets, (gk_ref, gv_ref), (kgrad_ref, vgrad_ref), (kprod_ref, vprod_ref))
    wk_ref[...] = dot(pt_ref[...], gk_ref[...], NN)
    wv_ref[...] = dot(pt_ref[...], gv_ref[...], NN)


def other_kernel(total, key, pt_ref, own_ref, g_ref, n_ref, r_ref, o_ref, *rest):
    gl_ref, w_ref, grad_ref, prod_ref = rest[-4:]
    s = lax.axis_index("sub")
    back_halves(total, (key,), g_ref, ((n_ref, r_ref, o_ref),), (gl_ref,), (grad_ref,), (prod_ref,))
    name = "key" if key else "value"
    place(w_ref, own_ref[...], s, name)
    place(w_ref, dot(pt_ref[...], gl_ref[...], NN), 1 - s, name)


def points_kernel(*refs):
    acc_ref = refs[-1]
    rows, width = acc_ref.shape
    s = lax.axis_index("sub")
    chunk = rows // BLOCKS
    for r in range(BLOCKS):
        span = slice(r * chunk, (r + 1) * chunk)
        total = None
        for w_ref, halves in ((refs[4], refs[:2]), (refs[5], refs[2:4])):
            for other, gl_ref in enumerate(halves):
                part = dot(gl_ref[span, :], w_ref[:, half_columns(s ^ other, width)], NT)
                total = part if total is None else total + part
        acc_ref[span, :] = total


def state_low(total, ref):
    return (ref[...] / total).astype(BF16).astype(F32)


def query_own_kernel(total, acc_ref, c_ref, wq_ref, own_ref, *rest):
    out_ref, q_ref = rest[-2:]
    rows, width = c_ref.shape
    cols = half_columns(lax.axis_index("sub"), width)
    q_ref[...] = dot(c_ref[:, cols], unpack(state_low(total, own_ref)).astype(BF16), NT).astype(BF16)
    chunk = rows // BLOCKS
    for r in range(BLOCKS):
        span = slice(r * chunk, (r + 1) * chunk)
        out_ref[span, :] = acc_ref[span, :] + dot(q_ref[span, :], wq_ref[:, cols], NT)


def last_kernel(total, acc_ref, c_ref, wq_ref, own_ref, got_ref, m_ref, *rest):
    kept_ref, got_part, outs, (q_ref, gp_ref, g_ref, sems) = rest[0], rest[1], rest[-7:-4], rest[-4:]
    rows, width = c_ref.shape
    rb, cb = m_ref.shape
    ns, nx = lax.axis_size("sub"), lax.axis_size("mp")
    s, x = lax.axis_index("sub"), lax.axis_index("mp")
    other = 1 - s
    cols = half_columns(other, width)
    low_own, low_got = state_low(total, own_ref), state_low(total, got_ref)
    q_ref[...] = dot(c_ref[:, cols], unpack(low_got).astype(BF16), NT).astype(BF16)
    g_ref[1] = (kept_ref[...] + got_part[:rb, :]) / total
    copies = [pltpu.make_async_copy(g_ref.at[1], outs[2], sems.at[1])]
    copies[0].start()
    chunk = rows // BLOCKS
    for r in range(BLOCKS):
        span = slice(r * chunk, (r + 1) * chunk)
        gp_ref[span, :] = (acc_ref[span, :] + dot(q_ref[span, :], wq_ref[:, cols], NT)).astype(BF16)
        copies.append(pltpu.make_async_copy(gp_ref.at[span, :], outs[0].at[span, :], sems.at[2 + r]))
        copies[-1].start()
    whole = jnp.concatenate([jnp.where(s == g, low_own, low_got) for g in range(ns)], axis=1)
    high, rest_ = split(m_ref[...])
    third = (m_ref[...] - high.astype(F32) - rest_.astype(F32)).astype(BF16)
    mine = whole[:, :cb]
    for xb in range(1, nx):
        mine = jnp.where(x == xb, whole[:, xb * cb : (xb + 1) * cb], mine)
    state = unpack(mine).astype(BF16)
    g_ref[0] = (dot(high, state, NT) + dot(rest_, state, NT) + dot(third, state, NT)) / total
    copies.append(pltpu.make_async_copy(g_ref.at[0], outs[1], sems.at[0]))
    copies[-1].start()
    for copy in copies:
        copy.wait()


def step_kernel(arrived, tailed, *refs):
    kept_ref, send_ref, keep_ref = refs[0], refs[-2], refs[-1]
    count, size = keep_ref.shape[0], keep_ref.shape[1]

    def block(i):
        return kept_ref[i] + refs[1][i * size : (i + 1) * size, :] if arrived else kept_ref[i]

    for i in range(count):
        keep_ref[i] = block(2 * i)
        send_ref[i * size : (i + 1) * size, :] = block(2 * i + 1)
    if tailed:
        send_ref[count * size :, :] = refs[1 + arrived][...]


def call(kernel, name, out_shape, inputs, specs, after=(), scratch=(), us=1.0, outs=None):
    us = US.get(name, us)
    inputs, specs = list(inputs) + list(after), list(specs) + [ANY] * len(after)
    return pl.pallas_call(
        kernel,
        out_shape=out_shape,
        in_specs=specs,
        out_specs=outs or (VMEM,) * len(out_shape),
        scratch_shapes=scratch,
        compiler_params=PARAMS,
        cost_estimate=pl.CostEstimate(flops=int(us * 1.1e9), bytes_accessed=int(us * 1e5), transcendentals=0),
        name=name,
    )(*inputs)


def swap_cores(value):
    return lax.ppermute(value, "sub", [(i, i ^ 1) for i in range(lax.axis_size("sub"))])


def swap(value, exchanges):
    nz, nx, ns = lax.axis_size("points"), lax.axis_size("mp"), lax.axis_size("sub")
    pairs = []
    for z in range(nz):
        for x in range(nx):
            for s, (axis, bit) in enumerate(exchanges):
                to = (z ^ bit, x) if axis == "points" else (z, x ^ bit)
                pairs.append(((z * nx + x) * ns + s, (to[0] * nx + to[1]) * ns + s))
    return lax.ppermute(value, ("points", "mp", "sub"), pairs)


def sum_kernel(a_ref, b_ref, *rest):
    rest[-1][...] = a_ref[...] + b_ref[: a_ref.shape[0], :]


def value_out_kernel(total, kept_ref, got_ref, *rest):
    rest[-1][...] = (kept_ref[...] + got_ref[...]) / total


class Total:
    def __init__(self, parts):
        self.value, self.got, self.done, self.over = parts[0], swap_cores(parts[1]), 0, False
        self.todo = list(zip(*routes("state")))

    def add(self, after=()):
        (self.value,) = call(
            sum_kernel,
            "sum_%d" % self.done,
            (jax.ShapeDtypeStruct(self.value.shape, F32),),
            (self.value, self.got),
            [VMEM] * 2,
            after=after,
            us=0.1,
        )
        self.sent = self.value
        self.done += 1
        if self.todo:
            self.got = swap(self.value, self.todo.pop(0))
        else:
            self.got, self.over = swap_cores(self.value), True


class Tail:
    def __init__(self, value):
        self.value, self.got = value, None
        self.todo = [list(route) for route in routes("state")]

    def takes(self, exchanges):
        return all(one in todo for one, todo in zip(exchanges, self.todo))

    def add(self, after=()):
        if self.got is not None:
            (self.value,) = call(
                sum_kernel,
                "sum_state",
                (jax.ShapeDtypeStruct(self.value.shape, F32),),
                (self.value, self.got.reshape(self.value.shape)),
                [VMEM] * 2,
                after=after,
                us=0.1,
            )
            self.got = None
        return self.value

    def sent(self, exchanges, got):
        self.got = got
        for one, todo in zip(exchanges, self.todo):
            todo.remove(one)

    def step(self, after=()):
        self.add(after)
        exchanges = [todo[0] for todo in self.todo]
        self.sent(exchanges, swap(self.value, exchanges))


class Scatter:
    def __init__(self, blocks, name):
        self.name, self.done = name, 0
        self.kept, self.got = blocks[0], swap_cores(blocks[1])
        self.todo = list(zip(*routes(name)))

    def step(self, after=(), tail=None):
        exchanges = self.todo.pop(0)
        blocks, rb, cb = self.kept.shape
        got = () if self.got is None else (self.got.reshape(-1, cb),)
        count = blocks // 2
        tailed = tail is not None and tail.takes(exchanges)
        extra = (tail.add().reshape(-1, cb),) if tailed else ()
        rows = count * rb
        shape = jax.ShapeDtypeStruct
        self.sent, self.kept = call(
            functools.partial(step_kernel, len(got), tailed),
            "add_%s_%d" % (self.name, self.done),
            (shape((rows + (extra[0].shape[0] if tailed else 0), cb), F32), shape((count, rb, cb), F32)),
            (self.kept,) + got + extra,
            [VMEM] * (1 + len(got) + tailed),
            after=after,
            us=0.2,
        )
        self.got = swap(self.sent, exchanges)
        if tailed:
            tail.sent(exchanges, self.got[rows:])
        self.done += 1

    def settle(self):
        blocks, rb, cb = self.kept.shape
        (summed,) = call(
            sum_kernel,
            "settle_" + self.name,
            (jax.ShapeDtypeStruct((blocks * rb, cb), F32),),
            (self.kept.reshape(blocks * rb, cb), self.got.reshape(-1, cb)),
            [VMEM] * 2,
            us=0.1,
        )
        self.kept, self.got = summed.reshape(blocks, rb, cb), None
        self.sent = summed

    def end(self, after=()):
        _, rb, cb = self.kept.shape
        (total,) = call(
            sum_kernel,
            "end_" + self.name,
            (jax.ShapeDtypeStruct((rb, cb), F32),),
            (self.kept.reshape(rb, cb), self.got),
            [VMEM] * 2,
            after=after,
            us=0.1,
        )
        return total


def local(points_in, cotangent, w_query, w_key, w_value):
    rows, width = points_in.shape
    nz, nx, ns = lax.axis_size("points"), lax.axis_size("mp"), lax.axis_size("sub")
    total = rows * nz * nx * ns
    half = width // ns
    rb, cb = width // (nz * ns), width // nx
    shape = jax.ShapeDtypeStruct
    dealt = shape((ns, nz * nx, rb, cb), F32)
    state = shape((ns, HS, half), F32)
    low = shape((rows, width), BF16)
    tall = shape((rows, half), F32)

    sums, grad_part, p_in, p_flip = call(
        cross_kernel,
        "cross",
        (shape((width, width), F32), state, low, shape((width, rows), BF16)),
        [pltpu.with_memory_space_constraint(a, pltpu.HBM) for a in (points_in, cotangent, w_query)],
        [HBM] * 3,
        scratch=[
            pltpu.VMEM((rows, width), BF16),
            pltpu.VMEM((width, width), BF16),
            pltpu.SemaphoreType.DMA((2 * CHUNKS + 1,)),
        ],
        us=3.0,
    )
    g_sum = Total(grad_part)
    (cross,) = call(deal_kernel, "deal", (dealt,), (sums,), [VMEM], us=0.3)
    cross_sum = Scatter(cross, "query")
    g_sum.add()
    cross_sum.step(after=(g_sum.sent,))
    g_sum.add(after=(cross_sum.sent,))
    norms, states = [], []
    weights = (w_key, w_value)
    for other in range(ns):
        first = other == 0
        res = call(
            functools.partial(norm_kernel, other),
            "norm",
            (tall, tall, tall, tall, shape((HS, half), F32)) + ((shape((4, width, half), BF16),) if first else ()),
            (p_in,) + weights,
            [VMEM] * (1 + len(weights)),
            after=(g_sum.sent, cross_sum.sent),
            scratch=[pltpu.VMEM((2, rows, half), F32), pltpu.VMEM((2, rows, half), BF16)],
            us=2.3,
        )
        norms.append(res[:5])
        states.append(res[4])
        g_sum.add(after=(states[-1],))
        if first:
            weights = (res[5],)
            cross_sum.step(after=(g_sum.sent,))
    while not g_sum.over:
        g_sum.add()
    g_own, g_got = g_sum.value, g_sum.got
    key_norm, key_inv, value_norm, value_inv, _ = zip(*norms)
    tail = Tail(states[0] + swap_cores(states[1]))
    cross_sum.settle()

    scratch = [pltpu.VMEM((rows, half), F32), pltpu.VMEM((rows, half), BF16)]
    short, column = shape((rows, half), BF16), shape((width, half), F32)
    k_own, v_own, wk_own, wv_own = call(
        functools.partial(own_kernel, total),
        "back_own",
        (short, short, column, column),
        (p_flip, g_own, key_norm[0], key_inv[0], value_norm[0], value_inv[0]),
        [VMEM] * 6,
        scratch=[scratch[0]] * 2 + [scratch[1]] * 2,
        us=1.8,
    )

    def back(key, part, after):
        return call(
            functools.partial(other_kernel, total, key),
            "back_key" if key else "back_value",
            (short, dealt),
            (p_flip, part, g_got) + ((key_norm[1], key_inv[1], value_norm[1]) if key else (value_norm[1], value_inv[1], key_norm[1])),
            [VMEM] * 6,
            after=after,
            scratch=scratch,
            us=1.0,
        )

    k_other, key_blocks = back(True, wk_own, (cross_sum.sent,))
    key_sum = Scatter(key_blocks, "key")
    v_other, value_blocks = back(False, wv_own, (k_other,))
    value_sum = Scatter(value_blocks, "value")
    key_low, value_low = (k_own, k_other), (v_own, v_other)
    last = v_other
    m_total, s_own = None, None
    for turn in ORDER:
        if turn == "P":
            (partial,) = call(
                points_kernel,
                "grad_points_part",
                (shape((rows, width), F32),),
                key_low + value_low + (w_key, w_value),
                [VMEM] * 6,
                after=(last,),
                us=1.3,
            )
            last = partial
        elif turn == "T":
            if not cross_sum.todo:
                m_total = last = cross_sum.end(after=(last,))
        elif turn == "S":
            if tail.todo[0]:
                tail.step(after=(last,))
            else:
                s_own = tail.add(after=(last,))
            last = tail.value
        else:
            one = {"M": cross_sum, "K": key_sum, "V": value_sum}[turn.upper()]
            one.step(after=(last,), tail=tail if turn.islower() else None)
            last = one.sent
    while cross_sum.todo or key_sum.todo or value_sum.todo:
        for turn in (cross_sum, key_sum, value_sum):
            if turn.todo:
                turn.step()
    if m_total is None:
        m_total = cross_sum.end()
    while tail.todo[0]:
        tail.step()
    if s_own is None:
        s_own = tail.add()
    s_got = swap_cores(s_own)
    (partial,) = call(
        functools.partial(query_own_kernel, total),
        "grad_points_own",
        (shape((rows, width), F32),),
        (partial, cotangent, w_query, s_own),
        [VMEM] * 4,
        scratch=[pltpu.VMEM((rows, half), BF16)],
        us=1.0,
    )
    block = shape((rb, cb), F32)
    grad_points, grad_query, grad_key = call(
        functools.partial(last_kernel, total),
        "outputs",
        (low, block, block),
        [partial, cotangent, w_query, s_own, s_got, m_total, key_sum.kept.reshape(rb, cb), key_sum.got],
        [VMEM] * 8,
        scratch=[
            pltpu.VMEM((rows, half), BF16),
            pltpu.VMEM((rows, width), BF16),
            pltpu.VMEM((2, rb, cb), F32),
            pltpu.SemaphoreType.DMA((2 + BLOCKS,)),
        ],
        us=0.01,
        outs=(HBM,) * 3,
    )
    (grad_value,) = call(
        functools.partial(value_out_kernel, total),
        "value_out",
        (block,),
        (value_sum.kept.reshape(rb, cb), value_sum.got, pltpu.with_memory_space_constraint(grad_query, pltpu.HBM)),
        [VMEM, VMEM, HBM],
        us=0.01,
    )
    return grad_points, grad_query, grad_key, grad_value


def solution(mesh):
    whole = P(("groups", "points", "mp", "sub"), None)
    block = P(("groups", "points", "sub"), "mp")
    return jax.shard_map(
        local,
        mesh=mesh,
        in_specs=(whole, whole, P(), P(), P()),
        out_specs=(whole, block, block, block),
        check_vma=False,
    )
```

```python
import functools

import jax
import jax.numpy as jnp
from jax import lax
from jax.experimental import pallas as pl
from jax.experimental.pallas import tpu as pltpu
from jax.sharding import PartitionSpec as P

HS = 32
F32 = jnp.float32
BF16 = jnp.bfloat16
NT = (((1,), (1,)), ((), ()))
TN = (((0,), (0,)), ((), ()))
NN = (((1,), (0,)), ((), ()))
VMEM = pl.BlockSpec(memory_space=pltpu.VMEM)
HBM = pl.BlockSpec(memory_space=pltpu.HBM)
ANY = pl.BlockSpec(memory_space=pl.ANY)
CHUNKS = 2
BLOCKS = 4
EARLY_Z = ("state", "value")
ORDER = "kVMPkVTKSVS"
US = {"end_query": 2.0, "grad_points": 0.01, "back_own": 0.01, "add_key_0": 5.0, "sum_0": 5.0, "back_key": 5.0, "back_value": 5.0}

PARAMS = pltpu.CompilerParams(vmem_limit_bytes=16 * 1024 * 1024)


def dot(a, b, dims):
    return lax.dot_general(a, b, dims, preferred_element_type=F32)


def split(x):
    high = x.astype(BF16)
    return high, (x - high.astype(F32)).astype(BF16)


def head_mask(size):
    rows = lax.broadcasted_iota(jnp.int32, (size, size), 0) // HS
    cols = lax.broadcasted_iota(jnp.int32, (size, size), 1) // HS
    return rows == cols


def averager(size):
    return jnp.where(head_mask(size), F32(1.0 / HS), F32(0.0)).astype(BF16)


def pack(full):
    size = full.shape[0]
    kept = jnp.where(head_mask(size), full, F32(0.0))
    total = kept[:HS]
    for i in range(1, size // HS):
        total = total + kept[i * HS : (i + 1) * HS]
    return total


def unpack(packed):
    size = packed.shape[1]
    tiled = jnp.concatenate([packed] * (size // HS), axis=0)
    return jnp.where(head_mask(size), tiled, F32(0.0))


def bits(axis):
    bit = 1
    while bit < lax.axis_size(axis):
        yield axis, bit
        bit *= 2


def routes(name):
    x, z = list(bits("mp")), list(bits("points"))
    if name in EARLY_Z:
        return x + z, z + x
    return x + z, z[:1] + x + z[1:]


def place(send_ref, keep_ref, ref, first, g, name):
    z, x, s = lax.axis_index("points"), lax.axis_index("mp"), lax.axis_index("sub")
    nz, ns = lax.axis_size("points"), lax.axis_size("sub")
    _, rb, cb = keep_ref.shape
    count = ref.shape[0] // ns // cb
    for zb in range(nz):
        for j in range(count):
            away = {"points": z ^ zb, "mp": x ^ (g * count + j)}
            spots = []
            for route in routes(name):
                spot = 0
                for t, (axis, bit) in enumerate(route):
                    spot = spot + jnp.where((away[axis] & bit) != 0, 1 << t, 0)
                spots.append(spot)
            cols = slice(first + j * cb, first + (j + 1) * cb)
            for out_ref, core in ((send_ref, 1 - s), (keep_ref, s)):
                rows = pl.ds(pl.multiple_of((zb * ns + core) * rb, rb), rb)
                out_ref[jnp.where(core == 0, spots[0], spots[1])] = ref[rows, cols]


def half_columns(g, width):
    half = width // lax.axis_size("sub")
    return pl.ds(pl.multiple_of(g * half, half), half)


def cross_kernel(p_hbm, c_hbm, wq_hbm, sums, g_ref, p_ref, pt_ref, c_ref, wq_ref, sems):
    rows, width = p_hbm.shape
    ns = lax.axis_size("sub")
    s = lax.axis_index("sub")
    half = width // ns
    chunk = rows // CHUNKS
    spans = [slice(r * chunk, (r + 1) * chunk) for r in range(CHUNKS)]
    loads = []
    for r, span in enumerate(spans):
        for k, (src, dst) in enumerate(((p_hbm, p_ref), (c_hbm, c_ref))):
            loads.append(pltpu.make_async_copy(src.at[span, :], dst.at[span, :], sems.at[2 * r + k]))
    loads.append(pltpu.make_async_copy(wq_hbm, wq_ref, sems.at[2 * CHUNKS]))
    for load in loads:
        load.start()
    for r, span in enumerate(spans):
        loads[2 * r].wait()
        flipped = p_ref[span, :].T
        pt_ref[:, span] = flipped
        loads[2 * r + 1].wait()
        for g in range(ns):
            cols = slice(g * half, (g + 1) * half)
            part = dot(flipped, c_ref[span, cols], NN)
            sums[:, cols] = part if r == 0 else sums[:, cols] + part
    loads[-1].wait()
    for g in range(ns):
        cols = slice(g * half, (g + 1) * half)
        high, low = split(sums[:, cols])
        wq = wq_ref[:, cols]
        g_ref[s ^ g] = pack(dot(wq, high, TN) + dot(wq, low, TN))


def deal_kernel(sums_ref, *rest):
    half = sums_ref.shape[1] // lax.axis_size("sub")
    for g in range(lax.axis_size("sub")):
        place(rest[-2], rest[-1], sums_ref, g * half, g, "query")


def centre_weights(raw):
    return split(raw.astype(F32) - dot(raw, averager(raw.shape[1]), NN))


def norm_kernel(other, p_ref, *rest):
    rows, width = p_ref.shape
    half = width // lax.axis_size("sub")
    mean = averager(half)
    c_ref, sq_ref = rest[-2:]
    if other:
        w_ref = rest[0]
        kn_ref, kr_ref, vn_ref, vr_ref, s_ref = rest[-7:-2]
        weights = [(w_ref[2 * w], w_ref[2 * w + 1]) for w in range(2)]
    else:
        kn_ref, kr_ref, vn_ref, vr_ref, s_ref, w_ref = rest[-8:-2]
        s = lax.axis_index("sub")
        weights = [centre_weights(ref[:, half_columns(s, width)]) for ref in rest[:2]]
    for w, (high, low) in enumerate(weights):
        p = p_ref[...]
        centred = dot(p, high, NN) + dot(p, low, NN)
        c_ref[w] = centred
        sq_ref[w] = (centred * centred).astype(BF16)
    for w, (n_ref, r_ref) in enumerate(((kn_ref, kr_ref), (vn_ref, vr_ref))):
        inverse = lax.rsqrt(dot(sq_ref[w], mean, NN) + 1e-05)
        n_ref[...] = c_ref[w] * inverse
        r_ref[...] = inverse
    s_ref[...] = pack(dot(kn_ref[...].astype(BF16), vn_ref[...].astype(BF16), TN))
    if not other:
        for w, ref in enumerate(rest[:2]):
            w_ref[2 * w], w_ref[2 * w + 1] = centre_weights(ref[:, half_columns(1 - s, width)])


def back_centre(total, key, g_ref):
    full = unpack((g_ref[...] / total).astype(BF16).astype(F32))
    mean = averager(full.shape[0])
    grouped = dot(mean, full.astype(BF16), NN) if key else dot(full.astype(BF16), mean, NN)
    return split(full - grouped)


def back_halves(total, keys, g_ref, sets, gl_refs, grad_refs, prod_refs):
    rows, half = gl_refs[0].shape
    mean = averager(half)
    chunk = rows // BLOCKS
    spans = [slice(r * chunk, (r + 1) * chunk) for r in range(BLOCKS)]
    centred = [back_centre(total, key, g_ref) for key in keys]
    for key, (high, small), (n_ref, r_ref, o_ref), grad_ref, prod_ref in zip(keys, centred, sets, grad_refs, prod_refs):
        dims = NT if key else NN
        for span in spans:
            low = o_ref[span, :].astype(BF16)
            grad = dot(low, high, dims) + dot(low, small, dims)
            grad_ref[span, :] = grad
            prod_ref[span, :] = (grad * n_ref[span, :]).astype(BF16)
    for (n_ref, r_ref, o_ref), gl_ref, grad_ref, prod_ref in zip(sets, gl_refs, grad_refs, prod_refs):
        for span in spans:
            second = dot(prod_ref[span, :], mean, NN)
            gl_ref[span, :] = ((grad_ref[span, :] - n_ref[span, :] * second) * r_ref[span, :]).astype(BF16)


def own_kernel(total, pt_ref, g_ref, kn_ref, kr_ref, vn_ref, vr_ref, *rest):
    gk_ref, gv_ref, wk_ref, wv_ref, kgrad_ref, vgrad_ref, kprod_ref, vprod_ref = rest[-8:]
    sets = ((kn_ref, kr_ref, vn_ref), (vn_ref, vr_ref, kn_ref))
    back_halves(total, (True, False), g_ref, sets, (gk_ref, gv_ref), (kgrad_ref, vgrad_ref), (kprod_ref, vprod_ref))
    wk_ref[...] = dot(pt_ref[...], gk_ref[...], NN)
    wv_ref[...] = dot(pt_ref[...], gv_ref[...], NN)


def other_kernel(total, key, pt_ref, own_ref, g_ref, n_ref, r_ref, o_ref, *rest):
    gl_ref, send_ref, keep_ref, w_ref, grad_ref, prod_ref = rest[-6:]
    s = lax.axis_index("sub")
    back_halves(total, (key,), g_ref, ((n_ref, r_ref, o_ref),), (gl_ref,), (grad_ref,), (prod_ref,))
    name = "key" if key else "value"
    w_ref[...] = dot(pt_ref[...], gl_ref[...], NN)
    place(send_ref, keep_ref, own_ref, 0, s, name)
    place(send_ref, keep_ref, w_ref, 0, 1 - s, name)


def points_kernel(*refs):
    acc_ref = refs[-1]
    rows, width = acc_ref.shape
    s = lax.axis_index("sub")
    chunk = rows // BLOCKS
    for r in range(BLOCKS):
        span = slice(r * chunk, (r + 1) * chunk)
        total = None
        for w_ref, halves in ((refs[4], refs[:2]), (refs[5], refs[2:4])):
            for other, gl_ref in enumerate(halves):
                part = dot(gl_ref[span, :], w_ref[:, half_columns(s ^ other, width)], NT)
                total = part if total is None else total + part
        acc_ref[span, :] = total


def state_low(total, ref):
    return (ref[...] / total).astype(BF16).astype(F32)


def query_own_kernel(total, acc_ref, c_ref, wq_ref, own_ref, *rest):
    out_ref, q_ref = rest[-2:]
    rows, width = c_ref.shape
    cols = half_columns(lax.axis_index("sub"), width)
    q_ref[...] = dot(c_ref[:, cols], unpack(state_low(total, own_ref)).astype(BF16), NT).astype(BF16)
    chunk = rows // BLOCKS
    for r in range(BLOCKS):
        span = slice(r * chunk, (r + 1) * chunk)
        out_ref[span, :] = acc_ref[span, :] + dot(q_ref[span, :], wq_ref[:, cols], NT)


def last_kernel(total, acc_ref, c_ref, wq_ref, own_ref, got_ref, m_ref, *rest):
    kept_ref, got_part, outs, (q_ref, gp_ref, g_ref, sems) = rest[0], rest[1], rest[-7:-4], rest[-4:]
    rows, width = c_ref.shape
    rb, cb = m_ref.shape
    ns, nx = lax.axis_size("sub"), lax.axis_size("mp")
    s, x = lax.axis_index("sub"), lax.axis_index("mp")
    other = 1 - s
    cols = half_columns(other, width)
    low_own, low_got = state_low(total, own_ref), state_low(total, got_ref)
    q_ref[...] = dot(c_ref[:, cols], unpack(low_got).astype(BF16), NT).astype(BF16)
    g_ref[1] = (kept_ref[...] + got_part[:rb, :]) / total
    copies = [pltpu.make_async_copy(g_ref.at[1], outs[2], sems.at[1])]
    copies[0].start()
    chunk = rows // BLOCKS
    for r in range(BLOCKS):
        span = slice(r * chunk, (r + 1) * chunk)
        gp_ref[span, :] = (acc_ref[span, :] + dot(q_ref[span, :], wq_ref[:, cols], NT)).astype(BF16)
        copies.append(pltpu.make_async_copy(gp_ref.at[span, :], outs[0].at[span, :], sems.at[2 + r]))
        copies[-1].start()
    whole = jnp.concatenate([jnp.where(s == g, low_own, low_got) for g in range(ns)], axis=1)
    high, rest_ = split(m_ref[...])
    third = (m_ref[...] - high.astype(F32) - rest_.astype(F32)).astype(BF16)
    mine = whole[:, :cb]
    for xb in range(1, nx):
        mine = jnp.where(x == xb, whole[:, xb * cb : (xb + 1) * cb], mine)
    state = unpack(mine).astype(BF16)
    g_ref[0] = (dot(high, state, NT) + dot(rest_, state, NT) + dot(third, state, NT)) / total
    copies.append(pltpu.make_async_copy(g_ref.at[0], outs[1], sems.at[0]))
    copies[-1].start()
    for copy in copies:
        copy.wait()


def step_kernel(arrived, tailed, *refs):
    kept_ref, send_ref, keep_ref = refs[0], refs[-2], refs[-1]
    count, size = keep_ref.shape[0], keep_ref.shape[1]

    def block(i):
        return kept_ref[i] + refs[1][i * size : (i + 1) * size, :] if arrived else kept_ref[i]

    for i in range(count):
        keep_ref[i] = block(2 * i)
        send_ref[i * size : (i + 1) * size, :] = block(2 * i + 1)
    if tailed:
        send_ref[count * size :, :] = refs[1 + arrived][...]


def call(kernel, name, out_shape, inputs, specs, after=(), scratch=(), us=1.0, outs=None):
    us = US.get(name, us)
    inputs, specs = list(inputs) + list(after), list(specs) + [ANY] * len(after)
    return pl.pallas_call(
        kernel,
        out_shape=out_shape,
        in_specs=specs,
        out_specs=outs or (VMEM,) * len(out_shape),
        scratch_shapes=scratch,
        compiler_params=PARAMS,
        cost_estimate=pl.CostEstimate(flops=int(us * 1.1e9), bytes_accessed=int(us * 1e5), transcendentals=0),
        name=name,
    )(*inputs)


def swap_cores(value):
    return lax.ppermute(value, "sub", [(i, i ^ 1) for i in range(lax.axis_size("sub"))])


def swap(value, exchanges):
    nz, nx, ns = lax.axis_size("points"), lax.axis_size("mp"), lax.axis_size("sub")
    pairs = []
    for z in range(nz):
        for x in range(nx):
            for s, (axis, bit) in enumerate(exchanges):
                to = (z ^ bit, x) if axis == "points" else (z, x ^ bit)
                pairs.append(((z * nx + x) * ns + s, (to[0] * nx + to[1]) * ns + s))
    return lax.ppermute(value, ("points", "mp", "sub"), pairs)


def sum_kernel(a_ref, b_ref, *rest):
    rest[-1][...] = a_ref[...] + b_ref[: a_ref.shape[0], :]


def value_out_kernel(total, kept_ref, got_ref, *rest):
    rest[-1][...] = (kept_ref[...] + got_ref[...]) / total


class Total:
    def __init__(self, parts):
        self.value, self.got, self.done, self.over = parts[0], swap_cores(parts[1]), 0, False
        self.todo = list(zip(*routes("state")))

    def add(self, after=()):
        (self.value,) = call(
            sum_kernel,
            "sum_%d" % self.done,
            (jax.ShapeDtypeStruct(self.value.shape, F32),),
            (self.value, self.got),
            [VMEM] * 2,
            after=after,
            us=0.1,
        )
        self.sent = self.value
        self.done += 1
        if self.todo:
            self.got = swap(self.value, self.todo.pop(0))
        else:
            self.got, self.over = swap_cores(self.value), True


class Tail:
    def __init__(self, value):
        self.value, self.got = value, None
        self.todo = [list(route) for route in routes("state")]

    def takes(self, exchanges):
        return all(one in todo for one, todo in zip(exchanges, self.todo))

    def add(self, after=()):
        if self.got is not None:
            (self.value,) = call(
                sum_kernel,
                "sum_state",
                (jax.ShapeDtypeStruct(self.value.shape, F32),),
                (self.value, self.got.reshape(self.value.shape)),
                [VMEM] * 2,
                after=after,
                us=0.1,
            )
            self.got = None
        return self.value

    def sent(self, exchanges, got):
        self.got = got
        for one, todo in zip(exchanges, self.todo):
            todo.remove(one)

    def step(self, after=()):
        self.add(after)
        exchanges = [todo[0] for todo in self.todo]
        self.sent(exchanges, swap(self.value, exchanges))


class Scatter:
    def __init__(self, blocks, name):
        self.name, self.done = name, 0
        self.kept, self.got = blocks[1], swap_cores(blocks[0])
        self.todo = list(zip(*routes(name)))

    def step(self, after=(), tail=None):
        exchanges = self.todo.pop(0)
        blocks, rb, cb = self.kept.shape
        got = () if self.got is None else (self.got.reshape(-1, cb),)
        count = blocks // 2
        tailed = tail is not None and tail.takes(exchanges)
        extra = (tail.add().reshape(-1, cb),) if tailed else ()
        rows = count * rb
        shape = jax.ShapeDtypeStruct
        self.sent, self.kept = call(
            functools.partial(step_kernel, len(got), tailed),
            "add_%s_%d" % (self.name, self.done),
            (shape((rows + (extra[0].shape[0] if tailed else 0), cb), F32), shape((count, rb, cb), F32)),
            (self.kept,) + got + extra,
            [VMEM] * (1 + len(got) + tailed),
            after=after,
            us=0.2,
        )
        self.got = swap(self.sent, exchanges)
        if tailed:
            tail.sent(exchanges, self.got[rows:])
        self.done += 1

    def settle(self):
        blocks, rb, cb = self.kept.shape
        (summed,) = call(
            sum_kernel,
            "settle_" + self.name,
            (jax.ShapeDtypeStruct((blocks * rb, cb), F32),),
            (self.kept.reshape(blocks * rb, cb), self.got.reshape(-1, cb)),
            [VMEM] * 2,
            us=0.1,
        )
        self.kept, self.got = summed.reshape(blocks, rb, cb), None
        self.sent = summed

    def end(self, after=()):
        _, rb, cb = self.kept.shape
        (total,) = call(
            sum_kernel,
            "end_" + self.name,
            (jax.ShapeDtypeStruct((rb, cb), F32),),
            (self.kept.reshape(rb, cb), self.got),
            [VMEM] * 2,
            after=after,
            us=0.1,
        )
        return total


def local(points_in, cotangent, w_query, w_key, w_value):
    rows, width = points_in.shape
    nz, nx, ns = lax.axis_size("points"), lax.axis_size("mp"), lax.axis_size("sub")
    total = rows * nz * nx * ns
    half = width // ns
    rb, cb = width // (nz * ns), width // nx
    shape = jax.ShapeDtypeStruct
    dealt = shape((nz * nx, rb, cb), F32)
    state = shape((ns, HS, half), F32)
    low = shape((rows, width), BF16)
    tall = shape((rows, half), F32)

    sums, grad_part, p_in, p_flip = call(
        cross_kernel,
        "cross",
        (shape((width, width), F32), state, low, shape((width, rows), BF16)),
        [pltpu.with_memory_space_constraint(a, pltpu.HBM) for a in (points_in, cotangent, w_query)],
        [HBM] * 3,
        scratch=[
            pltpu.VMEM((rows, width), BF16),
            pltpu.VMEM((width, width), BF16),
            pltpu.SemaphoreType.DMA((2 * CHUNKS + 1,)),
        ],
        us=3.0,
    )
    g_sum = Total(grad_part)
    cross = call(deal_kernel, "deal", (dealt, dealt), (sums,), [VMEM], us=0.3)
    cross_sum = Scatter(cross, "query")
    g_sum.add()
    cross_sum.step(after=(g_sum.sent,))
    g_sum.add(after=(cross_sum.sent,))
    norms, states = [], []
    weights = (w_key, w_value)
    for other in range(ns):
        first = other == 0
        res = call(
            functools.partial(norm_kernel, other),
            "norm",
            (tall, tall, tall, tall, shape((HS, half), F32)) + ((shape((4, width, half), BF16),) if first else ()),
            (p_in,) + weights,
            [VMEM] * (1 + len(weights)),
            after=(g_sum.sent, cross_sum.sent),
            scratch=[pltpu.VMEM((2, rows, half), F32), pltpu.VMEM((2, rows, half), BF16)],
            us=2.3,
        )
        norms.append(res[:5])
        states.append(res[4])
        g_sum.add(after=(states[-1],))
        if first:
            weights = (res[5],)
            cross_sum.step(after=(g_sum.sent,))
    while not g_sum.over:
        g_sum.add()
    g_own, g_got = g_sum.value, g_sum.got
    key_norm, key_inv, value_norm, value_inv, _ = zip(*norms)
    tail = Tail(states[0] + swap_cores(states[1]))
    cross_sum.settle()

    scratch = [pltpu.VMEM((rows, half), F32), pltpu.VMEM((rows, half), BF16)]
    short, column = shape((rows, half), BF16), shape((width, half), F32)
    k_own, v_own, wk_own, wv_own = call(
        functools.partial(own_kernel, total),
        "back_own",
        (short, short, column, column),
        (p_flip, g_own, key_norm[0], key_inv[0], value_norm[0], value_inv[0]),
        [VMEM] * 6,
        scratch=[scratch[0]] * 2 + [scratch[1]] * 2,
        us=1.8,
    )

    def back(key, part, after):
        return call(
            functools.partial(other_kernel, total, key),
            "back_key" if key else "back_value",
            (short, dealt, dealt),
            (p_flip, part, g_got) + ((key_norm[1], key_inv[1], value_norm[1]) if key else (value_norm[1], value_inv[1], key_norm[1])),
            [VMEM] * 6,
            after=after,
            scratch=[pltpu.VMEM((width, half), F32)] + scratch,
            us=1.0,
        )

    k_other, *key_blocks = back(True, wk_own, (cross_sum.sent,))
    key_sum = Scatter(key_blocks, "key")
    v_other, *value_blocks = back(False, wv_own, (k_other,))
    value_sum = Scatter(value_blocks, "value")
    key_low, value_low = (k_own, k_other), (v_own, v_other)
    last = v_other
    m_total, s_own = None, None
    for turn in ORDER:
        if turn == "P":
            (partial,) = call(
                points_kernel,
                "grad_points_part",
                (shape((rows, width), F32),),
                key_low + value_low + (w_key, w_value),
                [VMEM] * 6,
                after=(last,),
                us=1.3,
            )
            last = partial
        elif turn == "T":
            if not cross_sum.todo:
                m_total = last = cross_sum.end(after=(last,))
        elif turn == "S":
            if tail.todo[0]:
                tail.step(after=(last,))
            else:
                s_own = tail.add(after=(last,))
            last = tail.value
        else:
            one = {"M": cross_sum, "K": key_sum, "V": value_sum}[turn.upper()]
            one.step(after=(last,), tail=tail if turn.islower() else None)
            last = one.sent
    while cross_sum.todo or key_sum.todo or value_sum.todo:
        for turn in (cross_sum, key_sum, value_sum):
            if turn.todo:
                turn.step()
    if m_total is None:
        m_total = cross_sum.end()
    while tail.todo[0]:
        tail.step()
    if s_own is None:
        s_own = tail.add()
    s_got = swap_cores(s_own)
    (partial,) = call(
        functools.partial(query_own_kernel, total),
        "grad_points_own",
        (shape((rows, width), F32),),
        (partial, cotangent, w_query, s_own),
        [VMEM] * 4,
        scratch=[pltpu.VMEM((rows, half), BF16)],
        us=1.0,
    )
    block = shape((rb, cb), F32)
    grad_points, grad_query, grad_key = call(
        functools.partial(last_kernel, total),
        "outputs",
        (low, block, block),
        [partial, cotangent, w_query, s_own, s_got, m_total, key_sum.kept.reshape(rb, cb), key_sum.got],
        [VMEM] * 8,
        scratch=[
            pltpu.VMEM((rows, half), BF16),
            pltpu.VMEM((rows, width), BF16),
            pltpu.VMEM((2, rb, cb), F32),
            pltpu.SemaphoreType.DMA((2 + BLOCKS,)),
        ],
        us=0.01,
        outs=(HBM,) * 3,
    )
    (grad_value,) = call(
        functools.partial(value_out_kernel, total),
        "value_out",
        (block,),
        (value_sum.kept.reshape(rb, cb), value_sum.got, pltpu.with_memory_space_constraint(grad_query, pltpu.HBM)),
        [VMEM, VMEM, HBM],
        us=0.01,
    )
    return grad_points, grad_query, grad_key, grad_value


def solution(mesh):
    whole = P(("groups", "points", "mp", "sub"), None)
    block = P(("groups", "points", "sub"), "mp")
    return jax.shard_map(
        local,
        mesh=mesh,
        in_specs=(whole, whole, P(), P(), P()),
        out_specs=(whole, block, block, block),
        check_vma=False,
    )
```

```python
import functools

import jax
import jax.numpy as jnp
from jax import lax
from jax.experimental import pallas as pl
from jax.experimental.pallas import tpu as pltpu
from jax.sharding import PartitionSpec as P

HS = 32
F32 = jnp.float32
BF16 = jnp.bfloat16
NT = (((1,), (1,)), ((), ()))
TN = (((0,), (0,)), ((), ()))
NN = (((1,), (0,)), ((), ()))
VMEM = pl.BlockSpec(memory_space=pltpu.VMEM)
HBM = pl.BlockSpec(memory_space=pltpu.HBM)
ANY = pl.BlockSpec(memory_space=pl.ANY)
CHUNKS = 2
BLOCKS = 4
EARLY_Z = ("state", "value")
ORDER = "kVMPkVTKSVS"
US = {"end_query": 2.0, "grad_points": 0.01, "back_own": 0.01, "add_key_0": 5.0, "sum_0": 5.0, "back_key": 5.0, "back_value": 5.0}

PARAMS = pltpu.CompilerParams(vmem_limit_bytes=16 * 1024 * 1024)


def dot(a, b, dims):
    return lax.dot_general(a, b, dims, preferred_element_type=F32)


def split(x):
    high = x.astype(BF16)
    return high, (x - high.astype(F32)).astype(BF16)


def head_mask(size):
    rows = lax.broadcasted_iota(jnp.int32, (size, size), 0) // HS
    cols = lax.broadcasted_iota(jnp.int32, (size, size), 1) // HS
    return rows == cols


def averager(size):
    return jnp.where(head_mask(size), F32(1.0 / HS), F32(0.0)).astype(BF16)


def pack(full):
    size = full.shape[0]
    kept = jnp.where(head_mask(size), full, F32(0.0))
    total = kept[:HS]
    for i in range(1, size // HS):
        total = total + kept[i * HS : (i + 1) * HS]
    return total


def unpack(packed):
    size = packed.shape[1]
    tiled = jnp.concatenate([packed] * (size // HS), axis=0)
    return jnp.where(head_mask(size), tiled, F32(0.0))


def bits(axis):
    bit = 1
    while bit < lax.axis_size(axis):
        yield axis, bit
        bit *= 2


def routes(name):
    x, z = list(bits("mp")), list(bits("points"))
    if name in EARLY_Z:
        return x + z, z + x
    return x + z, z[:1] + x + z[1:]


def place(send_ref, keep_ref, ref, first, g, name):
    z, x, s = lax.axis_index("points"), lax.axis_index("mp"), lax.axis_index("sub")
    nz, ns = lax.axis_size("points"), lax.axis_size("sub")
    _, rb, cb = keep_ref.shape
    count = ref.shape[0] // ns // cb
    for zb in range(nz):
        for j in range(count):
            away = {"points": z ^ zb, "mp": x ^ (g * count + j)}
            spots = []
            for route in routes(name):
                spot = 0
                for t, (axis, bit) in enumerate(route):
                    spot = spot + jnp.where((away[axis] & bit) != 0, 1 << t, 0)
                spots.append(spot)
            cols = slice(first + j * cb, first + (j + 1) * cb)
            for out_ref, core in ((send_ref, 1 - s), (keep_ref, s)):
                rows = pl.ds(pl.multiple_of((zb * ns + core) * rb, rb), rb)
                out_ref[jnp.where(core == 0, spots[0], spots[1])] = ref[rows, cols]


def half_columns(g, width):
    half = width // lax.axis_size("sub")
    return pl.ds(pl.multiple_of(g * half, half), half)


def cross_kernel(p_hbm, c_hbm, wq_hbm, sums, g_ref, p_ref, pt_ref, c_ref, wq_ref, sems):
    rows, width = p_hbm.shape
    ns = lax.axis_size("sub")
    s = lax.axis_index("sub")
    half = width // ns
    chunk = rows // CHUNKS
    spans = [slice(r * chunk, (r + 1) * chunk) for r in range(CHUNKS)]
    loads = []
    for r, span in enumerate(spans):
        for k, (src, dst) in enumerate(((p_hbm, p_ref), (c_hbm, c_ref))):
            loads.append(pltpu.make_async_copy(src.at[span, :], dst.at[span, :], sems.at[2 * r + k]))
    loads.append(pltpu.make_async_copy(wq_hbm, wq_ref, sems.at[2 * CHUNKS]))
    for load in loads:
        load.start()
    for r, span in enumerate(spans):
        loads[2 * r].wait()
        flipped = p_ref[span, :].T
        pt_ref[:, span] = flipped
        loads[2 * r + 1].wait()
        for g in range(ns):
            cols = slice(g * half, (g + 1) * half)
            part = dot(flipped, c_ref[span, cols], NN)
            sums[:, cols] = part if r == 0 else sums[:, cols] + part
    loads[-1].wait()
    for g in range(ns):
        cols = slice(g * half, (g + 1) * half)
        high, low = split(sums[:, cols])
        wq = wq_ref[:, cols]
        g_ref[s ^ g] = pack(dot(wq, high, TN) + dot(wq, low, TN))


def deal_kernel(sums_ref, *rest):
    half = sums_ref.shape[1] // lax.axis_size("sub")
    for g in range(lax.axis_size("sub")):
        place(rest[-2], rest[-1], sums_ref, g * half, g, "query")


def centre_weights(raw):
    return split(raw.astype(F32) - dot(raw, averager(raw.shape[1]), NN))


def norm_kernel(other, p_ref, *rest):
    rows, width = p_ref.shape
    half = width // lax.axis_size("sub")
    mean = averager(half)
    c_ref, sq_ref = rest[-2:]
    if other:
        w_ref = rest[0]
        kn_ref, kr_ref, vn_ref, vr_ref, s_ref = rest[-7:-2]
        weights = [(w_ref[2 * w], w_ref[2 * w + 1]) for w in range(2)]
    else:
        kn_ref, kr_ref, vn_ref, vr_ref, s_ref, w_ref = rest[-8:-2]
        s = lax.axis_index("sub")
        weights = [centre_weights(ref[:, half_columns(s, width)]) for ref in rest[:2]]
    for w, (high, low) in enumerate(weights):
        p = p_ref[...]
        centred = dot(p, high, NN) + dot(p, low, NN)
        c_ref[w] = centred
        sq_ref[w] = (centred * centred).astype(BF16)
    for w, (n_ref, r_ref) in enumerate(((kn_ref, kr_ref), (vn_ref, vr_ref))):
        inverse = lax.rsqrt(dot(sq_ref[w], mean, NN) + 1e-05)
        n_ref[...] = c_ref[w] * inverse
        r_ref[...] = inverse
    s_ref[...] = pack(dot(kn_ref[...].astype(BF16), vn_ref[...].astype(BF16), TN))
    if not other:
        for w, ref in enumerate(rest[:2]):
            w_ref[2 * w], w_ref[2 * w + 1] = centre_weights(ref[:, half_columns(1 - s, width)])


def back_centre(total, key, g_ref):
    full = unpack((g_ref[...] / total).astype(BF16).astype(F32))
    mean = averager(full.shape[0])
    grouped = dot(mean, full.astype(BF16), NN) if key else dot(full.astype(BF16), mean, NN)
    return split(full - grouped)


def back_halves(total, keys, g_ref, sets, gl_refs, grad_refs, prod_refs):
    rows, half = gl_refs[0].shape
    mean = averager(half)
    chunk = rows // BLOCKS
    spans = [slice(r * chunk, (r + 1) * chunk) for r in range(BLOCKS)]
    centred = [back_centre(total, key, g_ref) for key in keys]
    for key, (high, small), (n_ref, r_ref, o_ref), grad_ref, prod_ref in zip(keys, centred, sets, grad_refs, prod_refs):
        dims = NT if key else NN
        for span in spans:
            low = o_ref[span, :].astype(BF16)
            grad = dot(low, high, dims) + dot(low, small, dims)
            grad_ref[span, :] = grad
            prod_ref[span, :] = (grad * n_ref[span, :]).astype(BF16)
    for (n_ref, r_ref, o_ref), gl_ref, grad_ref, prod_ref in zip(sets, gl_refs, grad_refs, prod_refs):
        for span in spans:
            second = dot(prod_ref[span, :], mean, NN)
            gl_ref[span, :] = ((grad_ref[span, :] - n_ref[span, :] * second) * r_ref[span, :]).astype(BF16)


def own_kernel(total, pt_ref, g_ref, kn_ref, kr_ref, vn_ref, vr_ref, *rest):
    gk_ref, gv_ref, wk_ref, wv_ref, kgrad_ref, vgrad_ref, kprod_ref, vprod_ref = rest[-8:]
    sets = ((kn_ref, kr_ref, vn_ref), (vn_ref, vr_ref, kn_ref))
    back_halves(total, (True, False), g_ref, sets, (gk_ref, gv_ref), (kgrad_ref, vgrad_ref), (kprod_ref, vprod_ref))
    wk_ref[...] = dot(pt_ref[...], gk_ref[...], NN)
    wv_ref[...] = dot(pt_ref[...], gv_ref[...], NN)


def other_kernel(total, key, pt_ref, own_ref, g_ref, n_ref, r_ref, o_ref, *rest):
    gl_ref, send_ref, keep_ref, w_ref, grad_ref, prod_ref = rest[-6:]
    s = lax.axis_index("sub")
    back_halves(total, (key,), g_ref, ((n_ref, r_ref, o_ref),), (gl_ref,), (grad_ref,), (prod_ref,))
    name = "key" if key else "value"
    w_ref[...] = dot(pt_ref[...], gl_ref[...], NN)
    place(send_ref, keep_ref, own_ref, 0, s, name)
    place(send_ref, keep_ref, w_ref, 0, 1 - s, name)


def points_kernel(*refs):
    acc_ref = refs[-1]
    rows, width = acc_ref.shape
    s = lax.axis_index("sub")
    chunk = rows // BLOCKS
    for r in range(BLOCKS):
        span = slice(r * chunk, (r + 1) * chunk)
        total = None
        for w_ref, halves in ((refs[4], refs[:2]), (refs[5], refs[2:4])):
            for other, gl_ref in enumerate(halves):
                part = dot(gl_ref[span, :], w_ref[:, half_columns(s ^ other, width)], NT)
                total = part if total is None else total + part
        acc_ref[span, :] = total


def state_low(total, ref):
    return (ref[...] / total).astype(BF16).astype(F32)


def query_own_kernel(total, acc_ref, c_ref, wq_ref, own_ref, *rest):
    out_ref, q_ref = rest[-2:]
    rows, width = c_ref.shape
    cols = half_columns(lax.axis_index("sub"), width)
    q_ref[...] = dot(c_ref[:, cols], unpack(state_low(total, own_ref)).astype(BF16), NT).astype(BF16)
    chunk = rows // BLOCKS
    for r in range(BLOCKS):
        span = slice(r * chunk, (r + 1) * chunk)
        out_ref[span, :] = acc_ref[span, :] + dot(q_ref[span, :], wq_ref[:, cols], NT)


def last_kernel(total, acc_ref, c_ref, wq_ref, own_ref, got_ref, m_ref, *rest):
    outs, (q_ref, gp_ref, g_ref, sems) = rest[-6:-4], rest[-4:]
    rows, width = c_ref.shape
    rb, cb = m_ref.shape
    ns, nx = lax.axis_size("sub"), lax.axis_size("mp")
    s, x = lax.axis_index("sub"), lax.axis_index("mp")
    other = 1 - s
    cols = half_columns(other, width)
    low_own, low_got = state_low(total, own_ref), state_low(total, got_ref)
    q_ref[...] = dot(c_ref[:, cols], unpack(low_got).astype(BF16), NT).astype(BF16)
    copies = []
    chunk = rows // BLOCKS
    for r in range(BLOCKS):
        span = slice(r * chunk, (r + 1) * chunk)
        gp_ref[span, :] = (acc_ref[span, :] + dot(q_ref[span, :], wq_ref[:, cols], NT)).astype(BF16)
        copies.append(pltpu.make_async_copy(gp_ref.at[span, :], outs[0].at[span, :], sems.at[1 + r]))
        copies[-1].start()
    whole = jnp.concatenate([jnp.where(s == g, low_own, low_got) for g in range(ns)], axis=1)
    high, rest_ = split(m_ref[...])
    third = (m_ref[...] - high.astype(F32) - rest_.astype(F32)).astype(BF16)
    mine = whole[:, :cb]
    for xb in range(1, nx):
        mine = jnp.where(x == xb, whole[:, xb * cb : (xb + 1) * cb], mine)
    state = unpack(mine).astype(BF16)
    g_ref[...] = (dot(high, state, NT) + dot(rest_, state, NT) + dot(third, state, NT)) / total
    copies.append(pltpu.make_async_copy(g_ref, outs[1], sems.at[0]))
    copies[-1].start()
    for copy in copies:
        copy.wait()


def step_kernel(arrived, tailed, *refs):
    kept_ref, send_ref, keep_ref = refs[0], refs[-2], refs[-1]
    count, size = keep_ref.shape[0], keep_ref.shape[1]

    def block(i):
        return kept_ref[i] + refs[1][i * size : (i + 1) * size, :] if arrived else kept_ref[i]

    for i in range(count):
        keep_ref[i] = block(2 * i)
        send_ref[i * size : (i + 1) * size, :] = block(2 * i + 1)
    if tailed:
        send_ref[count * size :, :] = refs[1 + arrived][...]


def call(kernel, name, out_shape, inputs, specs, after=(), scratch=(), us=1.0, outs=None):
    us = US.get(name, us)
    inputs, specs = list(inputs) + list(after), list(specs) + [ANY] * len(after)
    return pl.pallas_call(
        kernel,
        out_shape=out_shape,
        in_specs=specs,
        out_specs=outs or (VMEM,) * len(out_shape),
        scratch_shapes=scratch,
        compiler_params=PARAMS,
        cost_estimate=pl.CostEstimate(flops=int(us * 1.1e9), bytes_accessed=int(us * 1e5), transcendentals=0),
        name=name,
    )(*inputs)


def swap_cores(value):
    return lax.ppermute(value, "sub", [(i, i ^ 1) for i in range(lax.axis_size("sub"))])


def swap(value, exchanges):
    nz, nx, ns = lax.axis_size("points"), lax.axis_size("mp"), lax.axis_size("sub")
    pairs = []
    for z in range(nz):
        for x in range(nx):
            for s, (axis, bit) in enumerate(exchanges):
                to = (z ^ bit, x) if axis == "points" else (z, x ^ bit)
                pairs.append(((z * nx + x) * ns + s, (to[0] * nx + to[1]) * ns + s))
    return lax.ppermute(value, ("points", "mp", "sub"), pairs)


def sum_kernel(a_ref, b_ref, *rest):
    rest[-1][...] = a_ref[...] + b_ref[: a_ref.shape[0], :]


def sums_out_kernel(total, *refs):
    for i in range(2):
        kept_ref, got_ref = refs[2 * i : 2 * i + 2]
        refs[-2 + i][...] = (kept_ref[...] + got_ref[: kept_ref.shape[0], :]) / total


class Total:
    def __init__(self, parts):
        self.value, self.got, self.done, self.over = parts[0], swap_cores(parts[1]), 0, False
        self.todo = list(zip(*routes("state")))

    def add(self, after=()):
        (self.value,) = call(
            sum_kernel,
            "sum_%d" % self.done,
            (jax.ShapeDtypeStruct(self.value.shape, F32),),
            (self.value, self.got),
            [VMEM] * 2,
            after=after,
            us=0.1,
        )
        self.sent = self.value
        self.done += 1
        if self.todo:
            self.got = swap(self.value, self.todo.pop(0))
        else:
            self.got, self.over = swap_cores(self.value), True


class Tail:
    def __init__(self, value):
        self.value, self.got = value, None
        self.todo = [list(route) for route in routes("state")]

    def takes(self, exchanges):
        return all(one in todo for one, todo in zip(exchanges, self.todo))

    def add(self, after=()):
        if self.got is not None:
            (self.value,) = call(
                sum_kernel,
                "sum_state",
                (jax.ShapeDtypeStruct(self.value.shape, F32),),
                (self.value, self.got.reshape(self.value.shape)),
                [VMEM] * 2,
                after=after,
                us=0.1,
            )
            self.got = None
        return self.value

    def sent(self, exchanges, got):
        self.got = got
        for one, todo in zip(exchanges, self.todo):
            todo.remove(one)

    def step(self, after=()):
        self.add(after)
        exchanges = [todo[0] for todo in self.todo]
        self.sent(exchanges, swap(self.value, exchanges))


class Scatter:
    def __init__(self, blocks, name):
        self.name, self.done = name, 0
        self.kept, self.got = blocks[1], swap_cores(blocks[0])
        self.todo = list(zip(*routes(name)))

    def step(self, after=(), tail=None):
        exchanges = self.todo.pop(0)
        blocks, rb, cb = self.kept.shape
        got = () if self.got is None else (self.got.reshape(-1, cb),)
        count = blocks // 2
        tailed = tail is not None and tail.takes(exchanges)
        extra = (tail.add().reshape(-1, cb),) if tailed else ()
        rows = count * rb
        shape = jax.ShapeDtypeStruct
        self.sent, self.kept = call(
            functools.partial(step_kernel, len(got), tailed),
            "add_%s_%d" % (self.name, self.done),
            (shape((rows + (extra[0].shape[0] if tailed else 0), cb), F32), shape((count, rb, cb), F32)),
            (self.kept,) + got + extra,
            [VMEM] * (1 + len(got) + tailed),
            after=after,
            us=0.2,
        )
        self.got = swap(self.sent, exchanges)
        if tailed:
            tail.sent(exchanges, self.got[rows:])
        self.done += 1

    def settle(self):
        blocks, rb, cb = self.kept.shape
        (summed,) = call(
            sum_kernel,
            "settle_" + self.name,
            (jax.ShapeDtypeStruct((blocks * rb, cb), F32),),
            (self.kept.reshape(blocks * rb, cb), self.got.reshape(-1, cb)),
            [VMEM] * 2,
            us=0.1,
        )
        self.kept, self.got = summed.reshape(blocks, rb, cb), None
        self.sent = summed

    def end(self, after=()):
        _, rb, cb = self.kept.shape
        (total,) = call(
            sum_kernel,
            "end_" + self.name,
            (jax.ShapeDtypeStruct((rb, cb), F32),),
            (self.kept.reshape(rb, cb), self.got),
            [VMEM] * 2,
            after=after,
            us=0.1,
        )
        return total


def local(points_in, cotangent, w_query, w_key, w_value):
    rows, width = points_in.shape
    nz, nx, ns = lax.axis_size("points"), lax.axis_size("mp"), lax.axis_size("sub")
    total = rows * nz * nx * ns
    half = width // ns
    rb, cb = width // (nz * ns), width // nx
    shape = jax.ShapeDtypeStruct
    dealt = shape((nz * nx, rb, cb), F32)
    state = shape((ns, HS, half), F32)
    low = shape((rows, width), BF16)
    tall = shape((rows, half), F32)

    sums, grad_part, p_in, p_flip = call(
        cross_kernel,
        "cross",
        (shape((width, width), F32), state, low, shape((width, rows), BF16)),
        [pltpu.with_memory_space_constraint(a, pltpu.HBM) for a in (points_in, cotangent, w_query)],
        [HBM] * 3,
        scratch=[
            pltpu.VMEM((rows, width), BF16),
            pltpu.VMEM((width, width), BF16),
            pltpu.SemaphoreType.DMA((2 * CHUNKS + 1,)),
        ],
        us=3.0,
    )
    g_sum = Total(grad_part)
    cross = call(deal_kernel, "deal", (dealt, dealt), (sums,), [VMEM], us=0.3)
    cross_sum = Scatter(cross, "query")
    g_sum.add()
    cross_sum.step(after=(g_sum.sent,))
    g_sum.add(after=(cross_sum.sent,))
    norms, states = [], []
    weights = (w_key, w_value)
    for other in range(ns):
        first = other == 0
        res = call(
            functools.partial(norm_kernel, other),
            "norm",
            (tall, tall, tall, tall, shape((HS, half), F32)) + ((shape((4, width, half), BF16),) if first else ()),
            (p_in,) + weights,
            [VMEM] * (1 + len(weights)),
            after=(g_sum.sent, cross_sum.sent),
            scratch=[pltpu.VMEM((2, rows, half), F32), pltpu.VMEM((2, rows, half), BF16)],
            us=2.3,
        )
        norms.append(res[:5])
        states.append(res[4])
        g_sum.add(after=(states[-1],))
        if first:
            weights = (res[5],)
            cross_sum.step(after=(g_sum.sent,))
    while not g_sum.over:
        g_sum.add()
    g_own, g_got = g_sum.value, g_sum.got
    key_norm, key_inv, value_norm, value_inv, _ = zip(*norms)
    tail = Tail(states[0] + swap_cores(states[1]))
    cross_sum.settle()

    scratch = [pltpu.VMEM((rows, half), F32), pltpu.VMEM((rows, half), BF16)]
    short, column = shape((rows, half), BF16), shape((width, half), F32)
    k_own, v_own, wk_own, wv_own = call(
        functools.partial(own_kernel, total),
        "back_own",
        (short, short, column, column),
        (p_flip, g_own, key_norm[0], key_inv[0], value_norm[0], value_inv[0]),
        [VMEM] * 6,
        scratch=[scratch[0]] * 2 + [scratch[1]] * 2,
        us=1.8,
    )

    def back(key, part, after):
        return call(
            functools.partial(other_kernel, total, key),
            "back_key" if key else "back_value",
            (short, dealt, dealt),
            (p_flip, part, g_got) + ((key_norm[1], key_inv[1], value_norm[1]) if key else (value_norm[1], value_inv[1], key_norm[1])),
            [VMEM] * 6,
            after=after,
            scratch=[pltpu.VMEM((width, half), F32)] + scratch,
            us=1.0,
        )

    k_other, *key_blocks = back(True, wk_own, (cross_sum.sent,))
    key_sum = Scatter(key_blocks, "key")
    v_other, *value_blocks = back(False, wv_own, (k_other,))
    value_sum = Scatter(value_blocks, "value")
    key_low, value_low = (k_own, k_other), (v_own, v_other)
    last = v_other
    m_total, s_own = None, None
    for turn in ORDER:
        if turn == "P":
            (partial,) = call(
                points_kernel,
                "grad_points_part",
                (shape((rows, width), F32),),
                key_low + value_low + (w_key, w_value),
                [VMEM] * 6,
                after=(last,),
                us=1.3,
            )
            last = partial
        elif turn == "T":
            if not cross_sum.todo:
                m_total = last = cross_sum.end(after=(last,))
        elif turn == "S":
            if tail.todo[0]:
                tail.step(after=(last,))
            else:
                s_own = tail.add(after=(last,))
            last = tail.value
        else:
            one = {"M": cross_sum, "K": key_sum, "V": value_sum}[turn.upper()]
            one.step(after=(last,), tail=tail if turn.islower() else None)
            last = one.sent
    while cross_sum.todo or key_sum.todo or value_sum.todo:
        for turn in (cross_sum, key_sum, value_sum):
            if turn.todo:
                turn.step()
    if m_total is None:
        m_total = cross_sum.end()
    while tail.todo[0]:
        tail.step()
    if s_own is None:
        s_own = tail.add()
    s_got = swap_cores(s_own)
    (partial,) = call(
        functools.partial(query_own_kernel, total),
        "grad_points_own",
        (shape((rows, width), F32),),
        (partial, cotangent, w_query, s_own),
        [VMEM] * 4,
        scratch=[pltpu.VMEM((rows, half), BF16)],
        us=1.0,
    )
    block = shape((rb, cb), F32)
    grad_points, grad_query = call(
        functools.partial(last_kernel, total),
        "outputs",
        (low, block),
        (partial, cotangent, w_query, s_own, s_got, m_total),
        [VMEM] * 6,
        scratch=[
            pltpu.VMEM((rows, half), BF16),
            pltpu.VMEM((rows, width), BF16),
            pltpu.VMEM((rb, cb), F32),
            pltpu.SemaphoreType.DMA((1 + BLOCKS,)),
        ],
        us=0.01,
        outs=(HBM,) * 2,
    )
    parts = []
    for one in (key_sum, value_sum):
        parts += [one.kept.reshape(rb, cb), one.got]
    grad_key, grad_value = call(
        functools.partial(sums_out_kernel, total),
        "sums_out",
        (block, block),
        parts + [pltpu.with_memory_space_constraint(grad_query, pltpu.HBM)],
        [VMEM] * 4 + [HBM],
        us=0.01,
    )
    return grad_points, grad_query, grad_key, grad_value


def solution(mesh):
    whole = P(("groups", "points", "mp", "sub"), None)
    block = P(("groups", "points", "sub"), "mp")
    return jax.shard_map(
        local,
        mesh=mesh,
        in_specs=(whole, whole, P(), P(), P()),
        out_specs=(whole, block, block, block),
        check_vma=False,
    )
```

```python
import functools

import jax
import jax.numpy as jnp
from jax import lax
from jax.experimental import pallas as pl
from jax.experimental.pallas import tpu as pltpu
from jax.sharding import PartitionSpec as P

HS = 32
F32 = jnp.float32
BF16 = jnp.bfloat16
NT = (((1,), (1,)), ((), ()))
TN = (((0,), (0,)), ((), ()))
NN = (((1,), (0,)), ((), ()))
VMEM = pl.BlockSpec(memory_space=pltpu.VMEM)
HBM = pl.BlockSpec(memory_space=pltpu.HBM)
ANY = pl.BlockSpec(memory_space=pl.ANY)
CHUNKS = 2
BLOCKS = 4
EARLY_Z = ("state", "value")
ORDER = "kVMPkVTSKVS"
US = {"end_query": 2.0, "grad_points": 0.01, "back_own": 0.01, "add_key_0": 5.0, "sum_0": 5.0, "back_key": 5.0, "back_value": 5.0}

PARAMS = pltpu.CompilerParams(vmem_limit_bytes=16 * 1024 * 1024)


def dot(a, b, dims):
    return lax.dot_general(a, b, dims, preferred_element_type=F32)


def split(x):
    high = x.astype(BF16)
    return high, (x - high.astype(F32)).astype(BF16)


def head_mask(size):
    rows = lax.broadcasted_iota(jnp.int32, (size, size), 0) // HS
    cols = lax.broadcasted_iota(jnp.int32, (size, size), 1) // HS
    return rows == cols


def averager(size):
    return jnp.where(head_mask(size), F32(1.0 / HS), F32(0.0)).astype(BF16)


def pack(full):
    size = full.shape[0]
    kept = jnp.where(head_mask(size), full, F32(0.0))
    total = kept[:HS]
    for i in range(1, size // HS):
        total = total + kept[i * HS : (i + 1) * HS]
    return total


def unpack(packed):
    size = packed.shape[1]
    tiled = jnp.concatenate([packed] * (size // HS), axis=0)
    return jnp.where(head_mask(size), tiled, F32(0.0))


def bits(axis):
    bit = 1
    while bit < lax.axis_size(axis):
        yield axis, bit
        bit *= 2


def routes(name):
    x, z = list(bits("mp")), list(bits("points"))
    if name in EARLY_Z:
        return x + z, z + x
    return x + z, z[:1] + x + z[1:]


def place(send_ref, keep_ref, ref, first, g, name):
    z, x, s = lax.axis_index("points"), lax.axis_index("mp"), lax.axis_index("sub")
    nz, ns = lax.axis_size("points"), lax.axis_size("sub")
    _, rb, cb = keep_ref.shape
    count = ref.shape[0] // ns // cb
    for zb in range(nz):
        for j in range(count):
            away = {"points": z ^ zb, "mp": x ^ (g * count + j)}
            spots = []
            for route in routes(name):
                spot = 0
                for t, (axis, bit) in enumerate(route):
                    spot = spot + jnp.where((away[axis] & bit) != 0, 1 << t, 0)
                spots.append(spot)
            cols = slice(first + j * cb, first + (j + 1) * cb)
            for out_ref, core in ((send_ref, 1 - s), (keep_ref, s)):
                rows = pl.ds(pl.multiple_of((zb * ns + core) * rb, rb), rb)
                out_ref[jnp.where(core == 0, spots[0], spots[1])] = ref[rows, cols]


def half_columns(g, width):
    half = width // lax.axis_size("sub")
    return pl.ds(pl.multiple_of(g * half, half), half)


def cross_kernel(p_hbm, c_hbm, wq_hbm, sums, g_ref, p_ref, pt_ref, c_ref, wq_ref, sems):
    rows, width = p_hbm.shape
    ns = lax.axis_size("sub")
    s = lax.axis_index("sub")
    half = width // ns
    chunk = rows // CHUNKS
    spans = [slice(r * chunk, (r + 1) * chunk) for r in range(CHUNKS)]
    loads = []
    for r, span in enumerate(spans):
        for k, (src, dst) in enumerate(((p_hbm, p_ref), (c_hbm, c_ref))):
            loads.append(pltpu.make_async_copy(src.at[span, :], dst.at[span, :], sems.at[2 * r + k]))
    loads.append(pltpu.make_async_copy(wq_hbm, wq_ref, sems.at[2 * CHUNKS]))
    for load in loads:
        load.start()
    for r, span in enumerate(spans):
        loads[2 * r].wait()
        flipped = p_ref[span, :].T
        pt_ref[:, span] = flipped
        loads[2 * r + 1].wait()
        for g in range(ns):
            cols = slice(g * half, (g + 1) * half)
            part = dot(flipped, c_ref[span, cols], NN)
            sums[:, cols] = part if r == 0 else sums[:, cols] + part
    loads[-1].wait()
    for g in range(ns):
        cols = slice(g * half, (g + 1) * half)
        high, low = split(sums[:, cols])
        wq = wq_ref[:, cols]
        g_ref[s ^ g] = pack(dot(wq, high, TN) + dot(wq, low, TN))


def deal_kernel(sums_ref, *rest):
    half = sums_ref.shape[1] // lax.axis_size("sub")
    for g in range(lax.axis_size("sub")):
        place(rest[-2], rest[-1], sums_ref, g * half, g, "query")


def centre_weights(raw):
    return split(raw.astype(F32) - dot(raw, averager(raw.shape[1]), NN))


def norm_kernel(other, p_ref, *rest):
    rows, width = p_ref.shape
    half = width // lax.axis_size("sub")
    mean = averager(half)
    c_ref, sq_ref = rest[-2:]
    if other:
        w_ref = rest[0]
        kn_ref, kr_ref, vn_ref, vr_ref, s_ref = rest[-7:-2]
        weights = [(w_ref[2 * w], w_ref[2 * w + 1]) for w in range(2)]
    else:
        kn_ref, kr_ref, vn_ref, vr_ref, s_ref, w_ref = rest[-8:-2]
        s = lax.axis_index("sub")
        weights = [centre_weights(ref[:, half_columns(s, width)]) for ref in rest[:2]]
    for w, (high, low) in enumerate(weights):
        p = p_ref[...]
        centred = dot(p, high, NN) + dot(p, low, NN)
        c_ref[w] = centred
        sq_ref[w] = (centred * centred).astype(BF16)
    for w, (n_ref, r_ref) in enumerate(((kn_ref, kr_ref), (vn_ref, vr_ref))):
        inverse = lax.rsqrt(dot(sq_ref[w], mean, NN) + 1e-05)
        n_ref[...] = c_ref[w] * inverse
        r_ref[...] = inverse
    s_ref[...] = pack(dot(kn_ref[...].astype(BF16), vn_ref[...].astype(BF16), TN))
    if not other:
        for w, ref in enumerate(rest[:2]):
            w_ref[2 * w], w_ref[2 * w + 1] = centre_weights(ref[:, half_columns(1 - s, width)])


def back_centre(total, key, g_ref):
    full = unpack((g_ref[...] / total).astype(BF16).astype(F32))
    mean = averager(full.shape[0])
    grouped = dot(mean, full.astype(BF16), NN) if key else dot(full.astype(BF16), mean, NN)
    return split(full - grouped)


def back_halves(total, keys, g_ref, sets, gl_refs, grad_refs, prod_refs):
    rows, half = gl_refs[0].shape
    mean = averager(half)
    chunk = rows // BLOCKS
    spans = [slice(r * chunk, (r + 1) * chunk) for r in range(BLOCKS)]
    centred = [back_centre(total, key, g_ref) for key in keys]
    for key, (high, small), (n_ref, r_ref, o_ref), grad_ref, prod_ref in zip(keys, centred, sets, grad_refs, prod_refs):
        dims = NT if key else NN
        for span in spans:
            low = o_ref[span, :].astype(BF16)
            grad = dot(low, high, dims) + dot(low, small, dims)
            grad_ref[span, :] = grad
            prod_ref[span, :] = (grad * n_ref[span, :]).astype(BF16)
    for (n_ref, r_ref, o_ref), gl_ref, grad_ref, prod_ref in zip(sets, gl_refs, grad_refs, prod_refs):
        for span in spans:
            second = dot(prod_ref[span, :], mean, NN)
            gl_ref[span, :] = ((grad_ref[span, :] - n_ref[span, :] * second) * r_ref[span, :]).astype(BF16)


def own_kernel(total, pt_ref, g_ref, kn_ref, kr_ref, vn_ref, vr_ref, *rest):
    gk_ref, gv_ref, wk_ref, wv_ref, kgrad_ref, vgrad_ref, kprod_ref, vprod_ref = rest[-8:]
    sets = ((kn_ref, kr_ref, vn_ref), (vn_ref, vr_ref, kn_ref))
    back_halves(total, (True, False), g_ref, sets, (gk_ref, gv_ref), (kgrad_ref, vgrad_ref), (kprod_ref, vprod_ref))
    wk_ref[...] = dot(pt_ref[...], gk_ref[...], NN)
    wv_ref[...] = dot(pt_ref[...], gv_ref[...], NN)


def other_kernel(total, key, pt_ref, own_ref, g_ref, n_ref, r_ref, o_ref, *rest):
    gl_ref, send_ref, keep_ref, w_ref, grad_ref, prod_ref = rest[-6:]
    s = lax.axis_index("sub")
    back_halves(total, (key,), g_ref, ((n_ref, r_ref, o_ref),), (gl_ref,), (grad_ref,), (prod_ref,))
    name = "key" if key else "value"
    w_ref[...] = dot(pt_ref[...], gl_ref[...], NN)
    place(send_ref, keep_ref, own_ref, 0, s, name)
    place(send_ref, keep_ref, w_ref, 0, 1 - s, name)


def points_kernel(*refs):
    acc_ref = refs[-1]
    rows, width = acc_ref.shape
    s = lax.axis_index("sub")
    chunk = rows // BLOCKS
    for r in range(BLOCKS):
        span = slice(r * chunk, (r + 1) * chunk)
        total = None
        for w_ref, halves in ((refs[4], refs[:2]), (refs[5], refs[2:4])):
            for other, gl_ref in enumerate(halves):
                part = dot(gl_ref[span, :], w_ref[:, half_columns(s ^ other, width)], NT)
                total = part if total is None else total + part
        acc_ref[span, :] = total


def state_low(total, ref):
    return (ref[...] / total).astype(BF16).astype(F32)


def query_own_kernel(total, acc_ref, c_ref, wq_ref, own_ref, *rest):
    out_ref, q_ref = rest[-2:]
    rows, width = c_ref.shape
    cols = half_columns(lax.axis_index("sub"), width)
    q_ref[...] = dot(c_ref[:, cols], unpack(state_low(total, own_ref)).astype(BF16), NT).astype(BF16)
    chunk = rows // BLOCKS
    for r in range(BLOCKS):
        span = slice(r * chunk, (r + 1) * chunk)
        out_ref[span, :] = acc_ref[span, :] + dot(q_ref[span, :], wq_ref[:, cols], NT)


def last_kernel(total, acc_ref, c_ref, wq_ref, own_ref, got_ref, m_ref, *rest):
    outs, (q_ref, gp_ref, g_ref, sems) = rest[-6:-4], rest[-4:]
    rows, width = c_ref.shape
    rb, cb = m_ref.shape
    ns, nx = lax.axis_size("sub"), lax.axis_size("mp")
    s, x = lax.axis_index("sub"), lax.axis_index("mp")
    other = 1 - s
    cols = half_columns(other, width)
    low_own, low_got = state_low(total, own_ref), state_low(total, got_ref)
    q_ref[...] = dot(c_ref[:, cols], unpack(low_got).astype(BF16), NT).astype(BF16)
    copies = []
    chunk = rows // BLOCKS
    for r in range(BLOCKS):
        span = slice(r * chunk, (r + 1) * chunk)
        gp_ref[span, :] = (acc_ref[span, :] + dot(q_ref[span, :], wq_ref[:, cols], NT)).astype(BF16)
        copies.append(pltpu.make_async_copy(gp_ref.at[span, :], outs[0].at[span, :], sems.at[1 + r]))
        copies[-1].start()
    whole = jnp.concatenate([jnp.where(s == g, low_own, low_got) for g in range(ns)], axis=1)
    high, rest_ = split(m_ref[...])
    third = (m_ref[...] - high.astype(F32) - rest_.astype(F32)).astype(BF16)
    mine = whole[:, :cb]
    for xb in range(1, nx):
        mine = jnp.where(x == xb, whole[:, xb * cb : (xb + 1) * cb], mine)
    state = unpack(mine).astype(BF16)
    g_ref[...] = (dot(high, state, NT) + dot(rest_, state, NT) + dot(third, state, NT)) / total
    copies.append(pltpu.make_async_copy(g_ref, outs[1], sems.at[0]))
    copies[-1].start()
    for copy in copies:
        copy.wait()


def step_kernel(arrived, tailed, *refs):
    kept_ref, send_ref, keep_ref = refs[0], refs[-2], refs[-1]
    count, size = keep_ref.shape[0], keep_ref.shape[1]

    def block(i):
        return kept_ref[i] + refs[1][i * size : (i + 1) * size, :] if arrived else kept_ref[i]

    for i in range(count):
        keep_ref[i] = block(2 * i)
        send_ref[i * size : (i + 1) * size, :] = block(2 * i + 1)
    if tailed:
        send_ref[count * size :, :] = refs[1 + arrived][...]


def call(kernel, name, out_shape, inputs, specs, after=(), scratch=(), us=1.0, outs=None):
    us = US.get(name, us)
    inputs, specs = list(inputs) + list(after), list(specs) + [ANY] * len(after)
    return pl.pallas_call(
        kernel,
        out_shape=out_shape,
        in_specs=specs,
        out_specs=outs or (VMEM,) * len(out_shape),
        scratch_shapes=scratch,
        compiler_params=PARAMS,
        cost_estimate=pl.CostEstimate(flops=int(us * 1.1e9), bytes_accessed=int(us * 1e5), transcendentals=0),
        name=name,
    )(*inputs)


def swap_cores(value):
    return lax.ppermute(value, "sub", [(i, i ^ 1) for i in range(lax.axis_size("sub"))])


def swap(value, exchanges):
    nz, nx, ns = lax.axis_size("points"), lax.axis_size("mp"), lax.axis_size("sub")
    pairs = []
    for z in range(nz):
        for x in range(nx):
            for s, (axis, bit) in enumerate(exchanges):
                to = (z ^ bit, x) if axis == "points" else (z, x ^ bit)
                pairs.append(((z * nx + x) * ns + s, (to[0] * nx + to[1]) * ns + s))
    return lax.ppermute(value, ("points", "mp", "sub"), pairs)


def sum_kernel(a_ref, b_ref, *rest):
    rest[-1][...] = a_ref[...] + b_ref[: a_ref.shape[0], :]


def sums_out_kernel(total, *refs):
    for i in range(2):
        kept_ref, got_ref = refs[2 * i : 2 * i + 2]
        refs[-2 + i][...] = (kept_ref[...] + got_ref[: kept_ref.shape[0], :]) / total


class Total:
    def __init__(self, parts):
        self.value, self.got, self.done, self.over = parts[0], swap_cores(parts[1]), 0, False
        self.todo = list(zip(*routes("state")))

    def add(self, after=()):
        (self.value,) = call(
            sum_kernel,
            "sum_%d" % self.done,
            (jax.ShapeDtypeStruct(self.value.shape, F32),),
            (self.value, self.got),
            [VMEM] * 2,
            after=after,
            us=0.1,
        )
        self.sent = self.value
        self.done += 1
        if self.todo:
            self.got = swap(self.value, self.todo.pop(0))
        else:
            self.got, self.over = swap_cores(self.value), True


class Tail:
    def __init__(self, value):
        self.value, self.got = value, None
        self.todo = [list(route) for route in routes("state")]

    def takes(self, exchanges):
        return all(one in todo for one, todo in zip(exchanges, self.todo))

    def add(self, after=()):
        if self.got is not None:
            (self.value,) = call(
                sum_kernel,
                "sum_state",
                (jax.ShapeDtypeStruct(self.value.shape, F32),),
                (self.value, self.got.reshape(self.value.shape)),
                [VMEM] * 2,
                after=after,
                us=0.1,
            )
            self.got = None
        return self.value

    def sent(self, exchanges, got):
        self.got = got
        for one, todo in zip(exchanges, self.todo):
            todo.remove(one)

    def step(self, after=()):
        self.add(after)
        exchanges = [todo[0] for todo in self.todo]
        self.sent(exchanges, swap(self.value, exchanges))


class Scatter:
    def __init__(self, blocks, name):
        self.name, self.done = name, 0
        self.kept, self.got = blocks[1], swap_cores(blocks[0])
        self.todo = list(zip(*routes(name)))

    def step(self, after=(), tail=None):
        exchanges = self.todo.pop(0)
        blocks, rb, cb = self.kept.shape
        got = () if self.got is None else (self.got.reshape(-1, cb),)
        count = blocks // 2
        tailed = tail is not None and tail.takes(exchanges)
        extra = (tail.add().reshape(-1, cb),) if tailed else ()
        rows = count * rb
        shape = jax.ShapeDtypeStruct
        self.sent, self.kept = call(
            functools.partial(step_kernel, len(got), tailed),
            "add_%s_%d" % (self.name, self.done),
            (shape((rows + (extra[0].shape[0] if tailed else 0), cb), F32), shape((count, rb, cb), F32)),
            (self.kept,) + got + extra,
            [VMEM] * (1 + len(got) + tailed),
            after=after,
            us=0.2,
        )
        self.got = swap(self.sent, exchanges)
        if tailed:
            tail.sent(exchanges, self.got[rows:])
        self.done += 1

    def settle(self):
        blocks, rb, cb = self.kept.shape
        (summed,) = call(
            sum_kernel,
            "settle_" + self.name,
            (jax.ShapeDtypeStruct((blocks * rb, cb), F32),),
            (self.kept.reshape(blocks * rb, cb), self.got.reshape(-1, cb)),
            [VMEM] * 2,
            us=0.1,
        )
        self.kept, self.got = summed.reshape(blocks, rb, cb), None
        self.sent = summed

    def end(self, after=()):
        _, rb, cb = self.kept.shape
        (total,) = call(
            sum_kernel,
            "end_" + self.name,
            (jax.ShapeDtypeStruct((rb, cb), F32),),
            (self.kept.reshape(rb, cb), self.got),
            [VMEM] * 2,
            after=after,
            us=0.1,
        )
        return total


def local(points_in, cotangent, w_query, w_key, w_value):
    rows, width = points_in.shape
    nz, nx, ns = lax.axis_size("points"), lax.axis_size("mp"), lax.axis_size("sub")
    total = rows * nz * nx * ns
    half = width // ns
    rb, cb = width // (nz * ns), width // nx
    shape = jax.ShapeDtypeStruct
    dealt = shape((nz * nx, rb, cb), F32)
    state = shape((ns, HS, half), F32)
    low = shape((rows, width), BF16)
    tall = shape((rows, half), F32)

    sums, grad_part, p_in, p_flip = call(
        cross_kernel,
        "cross",
        (shape((width, width), F32), state, low, shape((width, rows), BF16)),
        [pltpu.with_memory_space_constraint(a, pltpu.HBM) for a in (points_in, cotangent, w_query)],
        [HBM] * 3,
        scratch=[
            pltpu.VMEM((rows, width), BF16),
            pltpu.VMEM((width, width), BF16),
            pltpu.SemaphoreType.DMA((2 * CHUNKS + 1,)),
        ],
        us=3.0,
    )
    g_sum = Total(grad_part)
    cross = call(deal_kernel, "deal", (dealt, dealt), (sums,), [VMEM], us=0.3)
    cross_sum = Scatter(cross, "query")
    g_sum.add()
    cross_sum.step(after=(g_sum.sent,))
    g_sum.add(after=(cross_sum.sent,))
    norms, states = [], []
    weights = (w_key, w_value)
    for other in range(ns):
        first = other == 0
        res = call(
            functools.partial(norm_kernel, other),
            "norm",
            (tall, tall, tall, tall, shape((HS, half), F32)) + ((shape((4, width, half), BF16),) if first else ()),
            (p_in,) + weights,
            [VMEM] * (1 + len(weights)),
            after=(g_sum.sent, cross_sum.sent),
            scratch=[pltpu.VMEM((2, rows, half), F32), pltpu.VMEM((2, rows, half), BF16)],
            us=2.3,
        )
        norms.append(res[:5])
        states.append(res[4])
        g_sum.add(after=(states[-1],))
        if first:
            weights = (res[5],)
            cross_sum.step(after=(g_sum.sent,))
    while not g_sum.over:
        g_sum.add()
    g_own, g_got = g_sum.value, g_sum.got
    key_norm, key_inv, value_norm, value_inv, _ = zip(*norms)
    tail = Tail(states[0] + swap_cores(states[1]))
    cross_sum.settle()

    scratch = [pltpu.VMEM((rows, half), F32), pltpu.VMEM((rows, half), BF16)]
    short, column = shape((rows, half), BF16), shape((width, half), F32)
    k_own, v_own, wk_own, wv_own = call(
        functools.partial(own_kernel, total),
        "back_own",
        (short, short, column, column),
        (p_flip, g_own, key_norm[0], key_inv[0], value_norm[0], value_inv[0]),
        [VMEM] * 6,
        scratch=[scratch[0]] * 2 + [scratch[1]] * 2,
        us=1.8,
    )

    def back(key, part, after):
        return call(
            functools.partial(other_kernel, total, key),
            "back_key" if key else "back_value",
            (short, dealt, dealt),
            (p_flip, part, g_got) + ((key_norm[1], key_inv[1], value_norm[1]) if key else (value_norm[1], value_inv[1], key_norm[1])),
            [VMEM] * 6,
            after=after,
            scratch=[pltpu.VMEM((width, half), F32)] + scratch,
            us=1.0,
        )

    k_other, *key_blocks = back(True, wk_own, (cross_sum.sent,))
    key_sum = Scatter(key_blocks, "key")
    v_other, *value_blocks = back(False, wv_own, (k_other,))
    value_sum = Scatter(value_blocks, "value")
    key_low, value_low = (k_own, k_other), (v_own, v_other)
    last = v_other
    m_total, s_own = None, None
    for turn in ORDER:
        if turn == "P":
            (partial,) = call(
                points_kernel,
                "grad_points_part",
                (shape((rows, width), F32),),
                key_low + value_low + (w_key, w_value),
                [VMEM] * 6,
                after=(last,),
                us=1.3,
            )
            last = partial
        elif turn == "T":
            if not cross_sum.todo:
                m_total = last = cross_sum.end(after=(last,))
        elif turn == "S":
            if tail.todo[0]:
                tail.step(after=(last,))
            else:
                s_own = tail.add(after=(last,))
            last = tail.value
        else:
            one = {"M": cross_sum, "K": key_sum, "V": value_sum}[turn.upper()]
            one.step(after=(last,), tail=tail if turn.islower() else None)
            last = one.sent
    while cross_sum.todo or key_sum.todo or value_sum.todo:
        for turn in (cross_sum, key_sum, value_sum):
            if turn.todo:
                turn.step()
    if m_total is None:
        m_total = cross_sum.end()
    while tail.todo[0]:
        tail.step()
    if s_own is None:
        s_own = tail.add()
    s_got = swap_cores(s_own)
    (partial,) = call(
        functools.partial(query_own_kernel, total),
        "grad_points_own",
        (shape((rows, width), F32),),
        (partial, cotangent, w_query, s_own),
        [VMEM] * 4,
        scratch=[pltpu.VMEM((rows, half), BF16)],
        us=1.0,
    )
    block = shape((rb, cb), F32)
    grad_points, grad_query = call(
        functools.partial(last_kernel, total),
        "outputs",
        (low, block),
        (partial, cotangent, w_query, s_own, s_got, m_total),
        [VMEM] * 6,
        scratch=[
            pltpu.VMEM((rows, half), BF16),
            pltpu.VMEM((rows, width), BF16),
            pltpu.VMEM((rb, cb), F32),
            pltpu.SemaphoreType.DMA((1 + BLOCKS,)),
        ],
        us=0.01,
        outs=(HBM,) * 2,
    )
    parts = []
    for one in (key_sum, value_sum):
        parts += [one.kept.reshape(rb, cb), one.got]
    grad_key, grad_value = call(
        functools.partial(sums_out_kernel, total),
        "sums_out",
        (block, block),
        parts + [pltpu.with_memory_space_constraint(grad_query, pltpu.HBM)],
        [VMEM] * 4 + [HBM],
        us=0.01,
    )
    return grad_points, grad_query, grad_key, grad_value


def solution(mesh):
    whole = P(("groups", "points", "mp", "sub"), None)
    block = P(("groups", "points", "sub"), "mp")
    return jax.shard_map(
        local,
        mesh=mesh,
        in_specs=(whole, whole, P(), P(), P()),
        out_specs=(whole, block, block, block),
        check_vma=False,
    )
```
